32 devices in a mesh: dp: 4 (over y, x), fsdp: 8 (over z, core).
Axes of the slice: x: 2, y: 2, z: 4, core: 2. Of those that a mesh axis runs over, the one named last changes fastest.
Arguments:
- block_input: bfloat16 [4, 2, 2048, 1536], P('dp', None, 'fsdp'), may hold values from -6 to 6
- seq_lengths: int32 [4, 2, 3], P('dp'), may hold values from 0 to 2048, as said below
- adapter_ids: int32 [4, 2, 3], P('dp'), may hold values from 0 to 7
- norm_gain: float32 [1536], replicated, may hold values from 0.5 to 1.5
- w_in: bfloat16 [1536, 6400], P('fsdp'), may hold values from -0.15625 to 0.15625
- w_dt: bfloat16 [1536, 48], P('fsdp'), may hold values from -0.15625 to 0.15625
- conv_weight: float32 [4, 3328], replicated, may hold values from -3 to 3
- conv_bias: float32 [3328], replicated, may hold values from -0.5 to 0.5
- dt_bias: float32 [48], replicated, may hold values from -3 to -1
- head_rates: float32 [48], replicated, may hold values from 0.00048828125 to 0.3
- skip_gain: float32 [48], replicated, may hold values from 0.5 to 1.5
- gate_gain: float32 [3072], replicated, may hold values from 0.5 to 1.5
- w_out: bfloat16 [3072, 1536], P('fsdp'), may hold values from -0.109375 to 0.109375
- in_down: bfloat16 [8, 16, 1536], replicated, may hold values from -0.15625 to 0.15625
- in_up: bfloat16 [8, 16, 6400], replicated, may hold values from -1.5 to 1.5
- out_down: bfloat16 [8, 16, 3072], replicated, may hold values from -0.109375 to 0.109375
- out_up: bfloat16 [8, 16, 1536], replicated, may hold values from -1.5 to 1.5
- out_grad: bfloat16 [4, 2, 2048, 1536], P('dp', None, 'fsdp'), may hold values from -6 to 6
Outputs:
- block_output: bfloat16 [4, 2, 2048, 1536], P('dp', None, 'fsdp')
- input_grad: float32 [4, 2, 2048, 1536], P('dp', None, 'fsdp')
- grad_in_down: float32 [8, 16, 1536], P(None, None, 'fsdp')
- grad_in_up: float32 [8, 16, 6400], P(None, None, 'fsdp')
- grad_out_down: float32 [8, 16, 3072], P(None, None, 'fsdp')
- grad_out_up: float32 [8, 16, 1536], P(None, None, 'fsdp')
The draws below stay inside these ranges and needn't reach their ends.
Inputs may be any that keep to these rules, and one draw needn't show every extreme that they name: `seq_lengths`: in every stream the lengths sum to at most 2048, the rest of the stream being padding; each length is 0 or at least 1024; in every group one stream holds a single sequence of 2048 positions.
All inputs are finite; a program needn't handle non-finite values.
Results may differ from the reference program's by a relative error of at most 0.0074.
Values may be sent and summed in bfloat16 or wider, within the bound.
No kernel may reach another device: no remote copies, remote signals or barrier semaphores. Data moves between devices by JAX's collectives and lax.ppermute only.
A program may use at most 384 MiB of HBM per device.

```python
import math
import jax
import jax.numpy as jnp
from jax import lax

D = 1536
HEADS = 48
HEADDIM = 64
DSTATE = 128
CONV = 4
SPAN = 256
RANK = 16
ADAPTERS = 8
NSEQ = 3
MINLEN = 1024
STREAMS = 2
DI = 3072
CONVW = 3328
INW = 6400
STREAM_LEN = 2048
N_DP = 4


def draw_seq_lengths(key, part):
    key = jax.random.fold_in(key, 11)
    key_list = jax.random.split(key, 4)
    grid_shape = (N_DP, STREAMS)
    first_len = jax.random.randint(key_list[0], grid_shape, MINLEN, STREAM_LEN + 1)
    remaining = STREAM_LEN - first_len
    second_len = jax.random.randint(key_list[1], grid_shape, MINLEN, jnp.maximum(remaining, MINLEN) + 1)
    second_len = jnp.where(remaining >= MINLEN, second_len, 0)
    remaining = remaining - second_len
    third_len = jax.random.randint(key_list[2], grid_shape, MINLEN, jnp.maximum(remaining, MINLEN) + 1)
    third_len = jnp.where(remaining >= MINLEN, third_len, 0)
    reach_stream = jax.random.randint(key_list[3], (N_DP, 1), 0, STREAMS)
    is_whole = jnp.arange(STREAMS)[None, :] == reach_stream
    first_len = jnp.where(is_whole, STREAM_LEN, first_len)
    second_len = jnp.where(is_whole, 0, second_len)
    third_len = jnp.where(is_whole, 0, third_len)
    return jnp.stack([first_len, second_len, third_len], axis=-1).astype(jnp.int32)


def place_ends(entries, own_key, low, largest):
    shape = entries.shape
    index_at = [jax.random.randint(jax.random.fold_in(own_key, axis), (), 0, shape[axis]) for axis in range(len(shape))]
    entries = entries.at[tuple(index_at)].set(low)
    longest = shape.index(max(shape))
    index_at[longest] = (index_at[longest] + 1) % shape[longest]
    return entries.at[tuple(index_at)].set(largest)


def block_levels(key, dims, cuts, least, high):
    gain, own = 1.0, jax.random.fold_in(key, 6)
    for dim, shards_of in cuts:
        draws = jnp.exp(jax.random.uniform(jax.random.fold_in(own, dim), (shards_of,), jnp.float32, least / len(cuts), high / len(cuts)))
        gain = gain * jnp.repeat(draws, dims[dim] // shards_of).reshape([-1 if axis == dim else 1 for axis in range(len(dims))])
    return gain


def gaussian(own_key, dims, width, limit, cuts=(), held_as=jnp.bfloat16):
    entries = jax.random.normal(own_key, dims, jnp.float32) * width
    if len(cuts) > 0:
        entries = block_levels(own_key, dims, cuts, -0.22, 0.18) * entries
    return jnp.clip(entries, min=-limit, max=limit).astype(held_as)


def setup_inputs(seed: int = 0) -> dict:
    seeds = jax.random.split(jax.random.key(seed), 19)
    block_input = gaussian(seeds[0], (N_DP, STREAMS, STREAM_LEN, D), 1.0, 6.0, ((0, 4), (2, 8)))
    seq_lengths = draw_seq_lengths(jax.random.fold_in(seeds[18], 71), 0)
    adapter_ids = place_ends(jax.random.randint(seeds[2], (N_DP, STREAMS, NSEQ), 0, ADAPTERS), jax.random.fold_in(seeds[2], 1), 0, ADAPTERS - 1).astype(jnp.int32)
    norm_gain = jnp.clip(1.0 + 0.1 * jax.random.normal(seeds[3], (D,), jnp.float32), 0.5, 1.5)
    w_in = gaussian(seeds[4], (D, INW), D ** -0.5, 0.15625, ((0, 8),))
    w_dt = gaussian(seeds[5], (D, HEADS), D ** -0.5, 0.15625, ((0, 8),))
    conv_weight = gaussian(seeds[6], (CONV, CONVW), CONV ** -0.5, 3.0, (), jnp.float32)
    conv_bias = jnp.clip(jax.random.uniform(seeds[7], (CONVW,), jnp.float32, -0.5, 0.5), -0.5, 0.5)
    dt_bias = jnp.clip(jax.random.uniform(seeds[8], (HEADS,), jnp.float32, -3.0, -1.0), -3.0, -1.0)
    head_rates = jnp.clip(jnp.exp(jax.random.uniform(seeds[9], (HEADS,), jnp.float32, math.log(0.00048828125), math.log(0.3))), 0.00048828125, 0.3)
    skip_gain = jnp.clip(jax.random.uniform(seeds[10], (HEADS,), jnp.float32, 0.5, 1.5), 0.5, 1.5)
    gate_gain = jnp.clip(1.0 + 0.1 * jax.random.normal(seeds[11], (DI,), jnp.float32), 0.5, 1.5)
    w_out = gaussian(seeds[12], (DI, D), DI ** -0.5, 0.109375, ((0, 8),))
    in_down = gaussian(seeds[13], (ADAPTERS, RANK, D), D ** -0.5, 0.15625)
    in_up = gaussian(seeds[14], (ADAPTERS, RANK, INW), RANK ** -0.5, 1.5)
    out_down = gaussian(seeds[15], (ADAPTERS, RANK, DI), DI ** -0.5, 0.109375)
    out_up = gaussian(seeds[16], (ADAPTERS, RANK, D), RANK ** -0.5, 1.5)
    out_grad = gaussian(seeds[17], (N_DP, STREAMS, STREAM_LEN, D), 1.0, 6.0, ((0, 4), (2, 8)))
    return dict(block_input=block_input, seq_lengths=seq_lengths, adapter_ids=adapter_ids, norm_gain=norm_gain, w_in=w_in, w_dt=w_dt, conv_weight=conv_weight, conv_bias=conv_bias, dt_bias=dt_bias, head_rates=head_rates, skip_gain=skip_gain, gate_gain=gate_gain, w_out=w_out, in_down=in_down, in_up=in_up, out_down=out_down, out_up=out_up, out_grad=out_grad)


EPSILON = 1e-05
HIGHEST = lax.Precision.HIGHEST

@jax.custom_vjp
def low(v):
    return lax.optimization_barrier(v.astype(jnp.bfloat16)).astype(jnp.float32)

@jax.custom_vjp
def low_back(v):
    return v

def low_keep(v):
    return (low(v), None)

def low_pass(kept, grad):
    return (grad,)

def back_keep(v):
    return (v, None)

def back_low(kept, grad):
    return (low(grad),)
low.defvjp(low_keep, low_pass)
low_back.defvjp(back_keep, back_low)

def rms_scale(values, gain_vec):
    mean_sq = lax.optimization_barrier(jnp.mean(values * values, axis=-1, keepdims=True))
    return values * lax.rsqrt(mean_sq + EPSILON) * gain_vec

def segment_ids(seq_lens, positions):
    seg_ends = jnp.cumsum(seq_lens, axis=-1, dtype=jnp.int32)
    counted = lax.optimization_barrier(jnp.sum((positions[None, :, None] >= seg_ends[:, None, :]).astype(jnp.int32), axis=-1, dtype=jnp.int32))
    return jnp.where(positions[None, :] < 0, -1, counted).astype(jnp.int32)

def tap_masks(seg_ext, conv_taps, length):
    own_seg = seg_ext[:, conv_taps - 1:]
    return jnp.stack([(seg_ext[:, offset:offset + length] == own_seg).astype(jnp.float32) for offset in range(conv_taps)], axis=-1)

def adapter_table(segment, seq_ids, adapters):
    kinds = jnp.arange(adapters, dtype=jnp.int32)
    chosen = (seq_ids[:, :, None] == kinds[None, None, :]).astype(jnp.float32)
    slot_range = jnp.arange(seq_ids.shape[1], dtype=jnp.int32)
    member = (segment[:, :, None] == slot_range[None, None, :]).astype(jnp.float32)
    return jnp.einsum('slj,sjk->slk', member, chosen, precision=HIGHEST)

def convolve(extended, tap_valid, conv_weight, conv_bias):
    length = tap_valid.shape[1]
    running = conv_bias
    for offset in range(conv_weight.shape[0]):
        running = running + conv_weight[offset] * extended[:, offset:offset + length, :] * tap_valid[:, :, offset, None]
    return jax.nn.silu(running)

def span_masks(segment, prior_seg):
    length = segment.shape[1]
    in_span = jnp.arange(length, dtype=jnp.int32)
    pair_mask = (in_span[None, :, None] >= in_span[None, None, :]) & (segment[:, :, None] == segment[:, None, :])
    enter_mask = (segment == prior_seg[:, None]).astype(jnp.float32)
    last_seg = segment[:, -1]
    last_mask = (segment == last_seg[:, None]).astype(jnp.float32)
    carry_mask = (last_seg == prior_seg).astype(jnp.float32)
    return (pair_mask, enter_mask, last_mask, carry_mask)

def span_summary(conv_x, step_size, input_b, head_rates, last_mask, carry_mask):
    streams, length, inner = conv_x.shape
    heads = head_rates.shape[0]
    log_decay = jnp.cumsum(-step_size * head_rates, axis=1)
    weight = jnp.exp(log_decay[:, -1:, :] - log_decay) * step_size * last_mask[:, :, None]
    heads_x = conv_x.reshape(streams, length, heads, inner // heads)
    span_state = jnp.einsum('slhp,sln,slh->shpn', heads_x, input_b, weight, precision=HIGHEST)
    through = carry_mask[:, None] * jnp.exp(log_decay[:, -1, :])
    return (through, span_state)

def span_mix(conv_x, step_size, input_b, output_c, state_in, head_rates, skip_gain, pair_mask, enter_mask):
    streams, length, inner = conv_x.shape
    heads = head_rates.shape[0]
    log_decay = jnp.cumsum(-step_size * head_rates, axis=1)
    by_head = jnp.transpose(log_decay, (0, 2, 1))
    decay_gap = by_head[:, :, :, None] - by_head[:, :, None, :]
    decay_mat = jnp.exp(jnp.where(pair_mask[:, None, :, :], decay_gap, -1e+30))
    c_dot_b = jnp.einsum('sln,smn->slm', output_c, input_b, precision=HIGHEST)
    heads_x = conv_x.reshape(streams, length, heads, inner // heads)
    scaled_x = heads_x * step_size[:, :, :, None]
    inside = jnp.einsum('slm,shlm,smhp->slhp', c_dot_b, decay_mat, scaled_x, precision=HIGHEST)
    entering = enter_mask[:, :, None] * jnp.exp(log_decay)
    outside = jnp.einsum('sln,shpn->slhp', output_c, state_in, precision=HIGHEST) * entering[:, :, :, None]
    mixed_out = inside + outside + skip_gain[:, None] * heads_x
    return mixed_out.reshape(streams, length, inner)

def stream_branch(inputs, seq_lens, seq_ids, adapters_in, frozen):
    in_down, in_up, out_down, out_up = adapters_in
    norm_gain, w_in, w_dt, conv_weight, conv_bias, dt_bias, head_rates, skip_gain, gate_gain, w_out = frozen
    positions = jnp.arange(-(CONV - 1), STREAM_LEN, dtype=jnp.int32)
    seg_ext = segment_ids(seq_lens[None, :], positions)
    segment = seg_ext[:, CONV - 1:]
    tap_valid = tap_masks(seg_ext, CONV, STREAM_LEN)
    valid_rows = (segment[0] < NSEQ).astype(jnp.float32)[:, None]
    onehot = adapter_table(segment, seq_ids[None, :], ADAPTERS)[0]
    normed = low(rms_scale(inputs, norm_gain))
    hidden_in = low(low_back(jnp.einsum('rd,kqd->rkq', normed, in_down, precision=HIGHEST) * onehot[:, :, None]))
    projected = jnp.dot(normed, w_in, precision=HIGHEST) + jnp.dot(hidden_in.reshape(STREAM_LEN, ADAPTERS * RANK), in_up.reshape(ADAPTERS * RANK, INW), precision=HIGHEST)
    proj_low = low(low_back(projected))
    dt_raw = low_back(jnp.dot(normed, w_dt, precision=HIGHEST))
    gate_in = proj_low[:, :DI]
    extended = jnp.concatenate([jnp.zeros((CONV - 1, CONVW), jnp.float32), proj_low[:, DI:]], axis=0)[None]
    conv_out = convolve(extended, tap_valid, conv_weight, conv_bias)[0]
    step_size = jax.nn.softplus(dt_raw + dt_bias)
    span_count = STREAM_LEN // SPAN
    prior_all = seg_ext[0, CONV - 2::SPAN][:span_count]
    span_items = (conv_out[:, :DI].reshape(span_count, SPAN, DI), step_size.reshape(span_count, SPAN, HEADS), conv_out[:, DI:DI + DSTATE].reshape(span_count, SPAN, DSTATE), conv_out[:, DI + DSTATE:].reshape(span_count, SPAN, DSTATE), segment[0].reshape(span_count, SPAN), prior_all)

    def span_step(span_state, span_item):
        conv_x, step_part, input_b, output_c, seg_part, prior_part = span_item
        pair_mask, enter_mask, last_mask, carry_mask = span_masks(seg_part[None], prior_part[None])
        mixed_out = span_mix(conv_x[None], step_part[None], input_b[None], output_c[None], span_state[None], head_rates, skip_gain, pair_mask, enter_mask)[0]
        through, local_state = span_summary(conv_x[None], step_part[None], input_b[None], head_rates, last_mask, carry_mask)
        return (through[0][:, None, None] * span_state + local_state[0], mixed_out)
    zero_state = jnp.zeros((HEADS, HEADDIM, DSTATE), jnp.float32)
    mixed_all = lax.scan(jax.checkpoint(span_step), zero_state, span_items)[1].reshape(STREAM_LEN, DI)
    normed_out = low(rms_scale(mixed_all * jax.nn.silu(gate_in), gate_gain))
    hidden_out = low(low_back(jnp.einsum('ri,kqi->rkq', normed_out, out_down, precision=HIGHEST) * onehot[:, :, None]))
    branch = jnp.dot(normed_out, w_out, precision=HIGHEST) + jnp.dot(hidden_out.reshape(STREAM_LEN, ADAPTERS * RANK), out_up.reshape(ADAPTERS * RANK, D), precision=HIGHEST)
    return branch * valid_rows

def reference(block_input, seq_lengths, adapter_ids, norm_gain, w_in, w_dt, conv_weight, conv_bias, dt_bias, head_rates, skip_gain, gate_gain, w_out, in_down, in_up, out_down, out_up, out_grad):
    stream_count = N_DP * STREAMS
    inputs = block_input.astype(jnp.float32).reshape(stream_count, STREAM_LEN, D)
    seq_lens = seq_lengths.reshape(stream_count, NSEQ)
    seq_ids = adapter_ids.reshape(stream_count, NSEQ)
    frozen = (norm_gain, w_in.astype(jnp.float32), w_dt.astype(jnp.float32), conv_weight, conv_bias, dt_bias, head_rates, skip_gain, gate_gain, w_out.astype(jnp.float32))

    def forward(values, down_in, up_in, down_out, up_out):
        adapters_in = (down_in, up_in, down_out, up_out)

        def one_stream(carried, stream_item):
            return (carried, jax.checkpoint(stream_branch)(stream_item[0], stream_item[1], stream_item[2], adapters_in, frozen))
        branches = lax.scan(one_stream, None, (values, seq_lens, seq_ids))[1]
        return values + branches
    outputs, pull = jax.vjp(forward, inputs, in_down.astype(jnp.float32), in_up.astype(jnp.float32), out_down.astype(jnp.float32), out_up.astype(jnp.float32))
    grads = pull(out_grad.astype(jnp.float32).reshape(stream_count, STREAM_LEN, D))
    block_output = outputs.astype(jnp.bfloat16).reshape(N_DP, STREAMS, STREAM_LEN, D)
    input_grad = grads[0].reshape(N_DP, STREAMS, STREAM_LEN, D)
    return (block_output, input_grad, grads[1], grads[2], grads[3], grads[4])
```

```python
import functools

import jax
import jax.numpy as jnp
from jax import lax
from jax.experimental import pallas as pl
from jax.experimental.pallas import tpu as pltpu
from jax.sharding import PartitionSpec as P

EPSILON = 1e-05
HIGHEST = lax.Precision.HIGHEST
F32, LOW = jnp.float32, jnp.bfloat16
HALO = 16
LANES = 128
BLOCK = 256
VMEM = 48 * 1024 * 1024


def dot(a, b, precision=None):
    return lax.dot_general(
        a, b, (((1,), (0,)), ((), ())), precision=precision, preferred_element_type=F32
    )


def dot_nt(a, b, precision=None):
    return lax.dot_general(
        a, b, (((1,), (1,)), ((), ())), precision=precision, preferred_element_type=F32
    )


def iota(shape, dim):
    return lax.broadcasted_iota(jnp.int32, shape, dim)


def expand(values, spread, terms):
    total, rest = None, values
    for _ in range(terms):
        part = rest.astype(LOW)
        rest = rest - part.astype(F32)
        got = dot(part, spread)
        total = got if total is None else total + got
    return total


def sigmoid(v):
    return 1.0 / (1.0 + jnp.exp(-v))


def core_at(groups, streams, slots):
    return groups + 1 + streams * slots


class Meta:
    def __init__(self, ref, groups, slots):
        self.ref, self.groups, self.slots = ref, groups, slots

    def first(self):
        return self.ref[self.groups]

    def core(self, streams):
        return self.ref[core_at(self.groups, streams, self.slots)]

    def end(self, stream, slot):
        return self.ref[self.groups + 1 + stream * self.slots + slot]

    def segment(self, stream, pos):
        seg = jnp.zeros_like(pos)
        for slot in range(self.slots):
            seg = seg + (pos >= self.end(stream, slot)).astype(jnp.int32)
        return jnp.where(pos < 0, -1, seg)

    def scalar_segment(self, stream, pos):
        seg = jnp.int32(0)
        for slot in range(self.slots):
            seg = seg + jnp.where(pos >= self.end(stream, slot), 1, 0)
        return jnp.where(pos < 0, -1, seg)


def tap_masks(meta, stream, taps, length):
    pos = meta.first() + iota((length, LANES), 0)
    own = meta.segment(stream, pos)
    masks = []
    for k in range(taps - 1):
        masks.append((meta.segment(stream, pos - (taps - 1 - k)) == own).astype(F32))
    return masks


def wide(mask, cols):
    return jnp.concatenate([mask] * (cols // LANES), axis=1)


def conv_pre(block, masks, cw, cb):
    taps, cols = cw.shape
    total = cb + cw[taps - 1 : taps] * block[HALO:]
    for k in range(taps - 1):
        moved = pltpu.roll(block, taps - 1 - k, 0)[HALO:]
        total = total + cw[k : k + 1] * moved * wide(masks[k], cols)
    return total


def conv_back(d_out, block, masks, cw, cb):
    taps, cols = cw.shape
    pre = conv_pre(block, masks, cw, cb)
    sig = sigmoid(pre)
    d_pre = d_out * (sig * (1.0 + pre * (1.0 - sig)))
    total = jnp.concatenate([jnp.zeros((HALO, cols), F32), cw[taps - 1 : taps] * d_pre], axis=0)
    rows = total.shape[0]
    for k in range(taps - 1):
        part = cw[k : k + 1] * d_pre * wide(masks[k], cols)
        part = jnp.concatenate([jnp.zeros((HALO, cols), F32), part], axis=0)
        total = total + pltpu.roll(part, rows - (taps - 1 - k), 0)
    return total


def spread_of(first_head, cols, per_head):
    head = lax.shift_right_logical(iota((LANES, cols), 1), per_head.bit_length() - 1) + first_head
    return (iota((LANES, cols), 0) == head).astype(LOW)


def gather_of(first_head, cols, per_head):
    head = lax.shift_right_logical(iota((cols, LANES), 0), per_head.bit_length() - 1) + first_head
    return (iota((cols, LANES), 1) == head).astype(LOW)


def sum_heads(values, gather):
    part = values.astype(LOW)
    rest = (values - part.astype(F32)).astype(LOW)
    return dot(part, gather) + dot(rest, gather)


def halves_product(nx, hx, w_mine, w_other, up, core):
    return (
        dot(nx[core], w_mine[...]) + dot(nx[1 - core], w_other[...]) + dot(hx[...], up[...])
    ).astype(LOW)


def gate_project_kernel(cfg, meta_ref, nx, hx, w_mine, w_other, up, out):
    streams, length, slots, groups, per_group, headdim = cfg
    core = meta_ref[core_at(groups, streams, slots)]
    out[...] = halves_product(nx, hx, w_mine, w_other, up, core)


def half_specs(cfg, weights, cols):
    streams, length, slots, groups, per_group, headdim = cfg
    core = core_at(groups, streams, slots)
    mine, other = weights
    if mine is other:
        half = mine.shape[0] // 2
        return [
            pl.BlockSpec((half, cols), lambda i, m: (m[core], i)),
            pl.BlockSpec((half, cols), lambda i, m: (1 - m[core], i)),
        ]
    return [pl.BlockSpec((mine.shape[0], cols), lambda i, m: (0, i))] * 2


def gate_project(cfg, meta, slot, nx, hx, weights, in_up):
    cols = weights[0].shape[1]
    rows = nx.shape[1]
    blocks = cols // BLOCK
    return pl.pallas_call(
        functools.partial(gate_project_kernel, cfg),
        grid_spec=pltpu.PrefetchScalarGridSpec(
            num_scalar_prefetch=1, grid=(blocks,),
            in_specs=[
                pl.BlockSpec(nx.shape, lambda i, m: (0, 0, 0)),
                pl.BlockSpec(hx.shape, lambda i, m: (0, 0)),
                *half_specs(cfg, weights, BLOCK),
                pl.BlockSpec((in_up.shape[0], BLOCK), lambda i, m: (0, m[slot] * blocks + i)),
            ],
            out_specs=pl.BlockSpec((rows, BLOCK), lambda i, m: (0, i)),
        ),
        out_shape=jax.ShapeDtypeStruct((rows, cols), LOW),
        compiler_params=pltpu.CompilerParams(vmem_limit_bytes=VMEM),
        cost_estimate=pl.CostEstimate(
            flops=2 * rows * (2 * nx.shape[2] + 256) * cols, bytes_accessed=6 * nx.shape[2] * cols, transcendentals=0
        ),
        name="project_gate",
    )(meta, nx, hx, *weights, in_up)


def project_kernel(cfg, slot, with_state, meta_ref, nx, hx, w_mine, w_other, up, cw, cb, *rest):
    streams, length, slots, groups, per_group, headdim = cfg
    meta = Meta(meta_ref, groups, slots)
    if with_state:
        weight, bt, ci, x_out, state = rest
        per_block = BLOCK // headdim
        first_head = meta_ref[slot] * per_group + pl.program_id(0) * per_block
        spread = spread_of(first_head, BLOCK, headdim)
    else:
        ci, x_out = rest
    low = halves_product(nx, hx, w_mine, w_other, up, meta.core(streams))
    ci[...] = low
    full = low.astype(F32)
    for s in range(streams):
        block = full[s * (HALO + length) : (s + 1) * (HALO + length)]
        masks = tap_masks(meta, s, cw.shape[0], length)
        pre = conv_pre(block, masks, cw[...], cb[...])
        x = pre * sigmoid(pre)
        x_out[s * length : (s + 1) * length] = x
        if with_state:
            scale = expand(weight[s * length : (s + 1) * length], spread, 2)
            state[s] = dot(bt[s], (x * scale).astype(LOW)).astype(LOW)


def project(cfg, meta, slot, nx, hx, weights, in_up, conv_weight, conv_bias, first_block, blocks, weight=None, bt=None):
    streams, length, slots, groups, per_group, headdim = cfg
    rows = streams * length
    ext = nx.shape[1]
    with_state = weight is not None
    gate_blocks = (in_up.shape[1] - conv_weight.shape[1]) // BLOCK

    def place(i, m):
        return first_block + (m[slot] * blocks if with_state else 0) + i

    whole = lambda i, m: (0, 0)
    own = lambda i, m: (0, i)
    conv_at = lambda i, m: (0, place(i, m))
    in_specs = [
        pl.BlockSpec(nx.shape, lambda i, m: (0, 0, 0)),
        pl.BlockSpec(hx.shape, whole),
        *half_specs(cfg, weights, BLOCK),
        pl.BlockSpec((in_up.shape[0], BLOCK), lambda i, m: (0, gate_blocks + place(i, m))),
        pl.BlockSpec((conv_weight.shape[0], BLOCK), conv_at),
        pl.BlockSpec((1, BLOCK), conv_at),
    ]
    args = [nx, hx, *weights, in_up, conv_weight, conv_bias]
    out_specs = [pl.BlockSpec((ext, BLOCK), own), pl.BlockSpec((rows, BLOCK), own)]
    cols = blocks * BLOCK
    out_shape = [jax.ShapeDtypeStruct((ext, cols), LOW), jax.ShapeDtypeStruct((rows, cols), F32)]
    if with_state:
        args += [weight, bt]
        in_specs += [
            pl.BlockSpec(weight.shape, whole),
            pl.BlockSpec(bt.shape, lambda i, m: (0, 0, 0)),
        ]
        out_specs.append(pl.BlockSpec((streams, bt.shape[1], BLOCK), lambda i, m: (0, 0, i)))
        out_shape.append(jax.ShapeDtypeStruct((streams, bt.shape[1], cols), LOW))
    return pl.pallas_call(
        functools.partial(project_kernel, cfg, slot, with_state),
        grid_spec=pltpu.PrefetchScalarGridSpec(
            num_scalar_prefetch=1, grid=(blocks,), in_specs=in_specs, out_specs=out_specs
        ),
        out_shape=out_shape,
        compiler_params=pltpu.CompilerParams(vmem_limit_bytes=VMEM),
        cost_estimate=pl.CostEstimate(
            flops=2 * ext * (2 * nx.shape[2] + 256) * cols,
            bytes_accessed=4 * nx.shape[2] * cols + ext * cols * 8,
            transcendentals=rows * cols,
        ),
        name="project_conv",
    )(meta, *args)


def decay_kernel(cfg, state_size, meta_ref, step, rates, bc, log_d, enter_d, rest_d, weight, log_t, through, g, gt, b_low, c_low, bt, ct):
    streams, length, slots, groups, per_group, headdim = cfg
    meta = Meta(meta_ref, groups, slots)
    first = meta.first()
    lower = (iota((length, length), 0) >= iota((length, length), 1)).astype(F32)
    per_block = BLOCK // headdim
    for s in range(streams):
        at = slice(s * length, (s + 1) * length)
        prior = meta.scalar_segment(s, first - 1)
        last = meta.scalar_segment(s, first + length - 1)
        seg = meta.segment(s, first + iota((length, LANES), 0))
        seg_u = meta.segment(s, first + iota((length, length), 1))
        seg_t = meta.segment(s, first + iota((length, length), 0))
        st = step[at]
        logs = dot(lower, -st * rates[...], HIGHEST)
        log_d[at] = logs
        enter_d[at] = jnp.where(seg == prior, jnp.exp(logs), 0.0)
        remain = jnp.where(seg == last, jnp.exp(logs[length - 1 : length] - logs), 0.0)
        rest_d[at] = remain
        weight[at] = remain * st
        through[s] = jnp.broadcast_to(
            jnp.where(prior == last, jnp.exp(logs[length - 1 : length]), 0.0), (8, LANES)
        )
        turned = jnp.transpose(logs)
        for b in range(log_t.shape[1]):
            log_t[s, b, 0:per_block] = turned[b * per_block : (b + 1) * per_block]
        b_in, c_in = bc[at, :state_size], bc[at, state_size:]
        pairs = jnp.where(seg_u == seg_t, lower, 0.0) * dot_nt(c_in, b_in, HIGHEST)
        g[s] = pairs
        gt[s] = jnp.transpose(pairs)
        b_low[at] = b_in.astype(LOW)
        c_low[at] = c_in.astype(LOW)
        bt[s] = jnp.transpose(b_in).astype(LOW)
        ct[s] = jnp.transpose(c_in).astype(LOW)


def decays(cfg, meta, step, rates, bc, heads):
    streams, length, slots, groups, per_group, headdim = cfg
    rows = streams * length
    state_size = bc.shape[1] // 2
    blocks = heads * headdim // BLOCK
    row = lambda dtype, cols: jax.ShapeDtypeStruct((rows, cols), dtype)
    cube = lambda dtype, a, b: jax.ShapeDtypeStruct((streams, a, b), dtype)
    outs = [
        row(F32, LANES), row(F32, LANES), row(F32, LANES), row(F32, LANES),
        jax.ShapeDtypeStruct((streams, blocks, 8, length), F32),
        cube(F32, 8, LANES),
        cube(F32, length, length), cube(F32, length, length),
        row(LOW, state_size), row(LOW, state_size),
        cube(LOW, state_size, length), cube(LOW, state_size, length),
    ]
    zeros = lambda n: (lambda i, m: (0,) * n)
    return pl.pallas_call(
        functools.partial(decay_kernel, cfg, state_size),
        grid_spec=pltpu.PrefetchScalarGridSpec(
            num_scalar_prefetch=1, grid=(1,),
            in_specs=[pl.BlockSpec(a.shape, zeros(a.ndim)) for a in (step, rates, bc)],
            out_specs=[pl.BlockSpec(a.shape, zeros(len(a.shape))) for a in outs],
        ),
        out_shape=outs,
        compiler_params=pltpu.CompilerParams(vmem_limit_bytes=VMEM),
        name="decays",
    )(meta, step, rates, bc)


def inside_kernel(cfg, slot, meta_ref, x, step, logs, log_t, g, y):
    streams, length, slots, groups, per_group, headdim = cfg
    per_block = BLOCK // headdim
    first_head = meta_ref[slot] * per_group + pl.program_id(0) * per_block
    spread = spread_of(first_head, BLOCK, headdim)
    columns = spread_of(first_head, per_block * LANES, LANES)
    half = length // 2
    left = iota((length, LANES), 1) < headdim
    for s in range(streams):
        at = slice(s * length, (s + 1) * length)
        log_col = expand(logs[at], columns, 3)
        xs = (x[at] * expand(step[at], spread, 2)).astype(LOW)
        for pair in range(per_block // 2):
            cols = slice(pair * LANES, (pair + 1) * LANES)
            got = []
            for h in (2 * pair, 2 * pair + 1):
                col = log_col[:, h * LANES : (h + 1) * LANES]
                row = log_t[s, 0, h : h + 1]
                top = jnp.exp(jnp.minimum(col[:half] - row[:, :half], 0.0)) * g[s, :half, :half]
                low = jnp.exp(jnp.minimum(wide(col[half:], length) - row, 0.0)) * g[s, half:]
                got.append(
                    jnp.concatenate(
                        [dot(top.astype(LOW), xs[:half, cols]), dot(low.astype(LOW), xs[:, cols])], axis=0
                    )
                )
            y[at, cols] = jnp.where(left, got[0], got[1])


def inside(cfg, meta, slot, x, step, logs, log_t, g):
    streams, length, slots, groups, per_group, headdim = cfg
    blocks = x.shape[1] // BLOCK
    whole = lambda i, m: (0, 0)
    own = pl.BlockSpec((x.shape[0], BLOCK), lambda i, m: (0, i))
    return pl.pallas_call(
        functools.partial(inside_kernel, cfg, slot),
        grid_spec=pltpu.PrefetchScalarGridSpec(
            num_scalar_prefetch=1, grid=(blocks,),
            in_specs=[
                own,
                pl.BlockSpec(step.shape, whole),
                pl.BlockSpec(logs.shape, whole),
                pl.BlockSpec((streams, 1, 8, length), lambda i, m: (0, m[slot] * blocks + i, 0, 0)),
                pl.BlockSpec(g.shape, lambda i, m: (0, 0, 0)),
            ],
            out_specs=own,
        ),
        out_shape=jax.ShapeDtypeStruct(x.shape, F32),
        compiler_params=pltpu.CompilerParams(vmem_limit_bytes=VMEM),
        cost_estimate=pl.CostEstimate(
            flops=8 * x.shape[0] * length * x.shape[1], bytes_accessed=x.size * 8, transcendentals=4 * x.size
        ),
        name="inside",
    )(meta, x, step, logs, log_t, g)


def gate_kernel(cfg, meta_ref, *refs):
    streams, length, slots, groups, per_group, headdim = cfg
    xs, ys, states, gates = (refs[i * groups : (i + 1) * groups] for i in range(4))
    refs = refs[4 * groups :]
    d_out, enter_d, c_low, ct, skip, gain = refs[:6]
    out_low, d_mixed, d_gate, row_sum, d_state, y_all, v_all = refs[6:]
    width = per_group * headdim
    inner = groups * width
    rows = d_out.shape[0]
    per_stream = length // rows
    entering = enter_d[...]
    squares = jnp.zeros((rows, LANES), F32)
    crossed = jnp.zeros((rows, LANES), F32)

    def fold(values):
        total = values[:, :LANES]
        for j in range(1, values.shape[1] // LANES):
            total = total + values[:, j * LANES : (j + 1) * LANES]
        return total

    for j in range(groups):
        place = meta_ref[j]
        cols = pl.ds(pl.multiple_of(place * width, width), width)
        spread = spread_of(place * per_group, width, headdim)
        scale = expand(entering, spread, 2)
        y = ys[j][...] + dot(c_low[...], states[j][0]) * scale
        y_all[:, cols] = y
        gated = gates[j][...].astype(F32)
        v = (y + skip[:, cols] * xs[j][...]) * (gated * sigmoid(gated))
        v_all[:, cols] = v
        squares = squares + fold(v * v)
        crossed = crossed + fold(v * d_out[:, cols] * gain[:, cols])
    mean_sq = jnp.sum(squares, axis=1, keepdims=True) / inner
    rs = lax.rsqrt(mean_sq + EPSILON)
    mean_cross = jnp.sum(crossed, axis=1, keepdims=True) / inner
    pull = rs * rs * rs * mean_cross
    sums = jnp.zeros((rows, LANES), F32)
    fresh = pl.program_id(0) % per_stream == 0
    for j in range(groups):
        place = meta_ref[j]
        cols = pl.ds(pl.multiple_of(place * width, width), width)
        spread = spread_of(place * per_group, width, headdim)
        gated = gates[j][...].astype(F32)
        sig = sigmoid(gated)
        v = v_all[:, cols]
        y = y_all[:, cols]
        out_low[:, cols] = (v * rs * gain[:, cols]).astype(LOW)
        d_v = rs * d_out[:, cols] * gain[:, cols] - v * pull
        dm = d_v * (gated * sig)
        d_mixed[:, cols] = dm
        mixed = y + skip[:, cols] * xs[j][...]
        d_gate[:, cols] = (d_v * mixed * (sig * (1.0 + gated * (1.0 - sig)))).astype(LOW)
        sums = sums + sum_heads(
            dm.astype(LOW).astype(F32) * y, gather_of(place * per_group, width, headdim)
        )
        part = dot(ct[0], (dm * expand(entering, spread, 2)).astype(LOW))

        @pl.when(fresh)
        def _():
            d_state[0, :, cols] = part

        @pl.when(jnp.logical_not(fresh))
        def _():
            d_state[0, :, cols] += part

    row_sum[...] = sums


def gated(cfg, meta, xs, ys, states, gates, d_out, enter_d, c_low, ct, skip, gain):
    streams, length, slots, groups, per_group, headdim = cfg
    rows = 128
    per_stream = length // rows
    width = xs[0].shape[1]
    inner = d_out.shape[1]
    state_size = c_low.shape[1]
    total = streams * length
    row = lambda cols: pl.BlockSpec((rows, cols), lambda i, m: (i, 0))
    state = pl.BlockSpec((1, state_size, width), lambda i, m: (i // per_stream, 0, 0))
    flat = pl.BlockSpec((1, inner), lambda i, m: (0, 0))
    return pl.pallas_call(
        functools.partial(gate_kernel, cfg),
        grid_spec=pltpu.PrefetchScalarGridSpec(
            num_scalar_prefetch=1, grid=(total // rows,),
            in_specs=[row(width)] * (2 * groups) + [state] * groups + [row(width)] * groups
            + [
                row(inner), row(LANES), row(state_size),
                pl.BlockSpec((1, state_size, rows), lambda i, m: (i // per_stream, 0, i % per_stream)),
                flat, flat,
            ],
            out_specs=[
                row(inner), row(inner), row(inner), row(LANES),
                pl.BlockSpec((1, state_size, inner), lambda i, m: (i // per_stream, 0, 0)),
            ],
            scratch_shapes=[pltpu.VMEM((rows, inner), F32), pltpu.VMEM((rows, inner), F32)],
        ),
        out_shape=[
            jax.ShapeDtypeStruct((total, inner), LOW),
            jax.ShapeDtypeStruct((total, inner), F32),
            jax.ShapeDtypeStruct((total, inner), LOW),
            jax.ShapeDtypeStruct((total, LANES), F32),
            jax.ShapeDtypeStruct((streams, state_size, inner), F32),
        ],
        compiler_params=pltpu.CompilerParams(vmem_limit_bytes=VMEM),
        name="gated",
    )(meta, *xs, *ys, *states, *gates, d_out, enter_d, c_low, ct, skip, gain)


def inside_back_kernel(cfg, slot, meta_ref, x, d_mixed, step, logs, enter_d, log_t, gt, state, dxs, dgt, dc):
    streams, length, slots, groups, per_group, headdim = cfg
    per_block = BLOCK // headdim
    first_head = meta_ref[slot] * per_group + pl.program_id(0) * per_block
    spread = spread_of(first_head, BLOCK, headdim)
    columns = spread_of(first_head, per_block * LANES, LANES)
    half = length // 2
    left = iota((length, LANES), 1) < headdim

    @pl.when(pl.program_id(0) == 0)
    def _():
        dgt[...] = jnp.zeros_like(dgt)
        dc[...] = jnp.zeros_like(dc)

    for s in range(streams):
        at = slice(s * length, (s + 1) * length)
        log_col = expand(logs[at], columns, 3)
        xs = (x[at] * expand(step[at], spread, 2)).astype(LOW)
        dm = d_mixed[at]
        dm_low = dm.astype(LOW)
        dc[at] += dot_nt((dm * expand(enter_d[at], spread, 2)).astype(LOW), state[s])
        sum_top, sum_low = None, None
        for pair in range(per_block // 2):
            cols = slice(pair * LANES, (pair + 1) * LANES)
            got = []
            for h in (2 * pair, 2 * pair + 1):
                col = log_col[:, h * LANES : (h + 1) * LANES]
                row = log_t[s, 0, h : h + 1]
                top = jnp.exp(jnp.minimum(row - wide(col[:half], length), 0.0))
                low = jnp.exp(jnp.minimum(row[:, half:] - col[half:], 0.0))
                k_top = (top * gt[s, :half]).astype(LOW)
                k_low = (low * gt[s, half:, half:]).astype(LOW)
                got.append(
                    jnp.concatenate([dot(k_top, dm_low[:, cols]), dot(k_low, dm_low[half:, cols])], axis=0)
                )
                mine = left if h % 2 == 0 else jnp.logical_not(left)
                x_mine = jnp.where(mine, xs[:, cols], jnp.zeros_like(xs[:, cols]))
                add_top = dot_nt(x_mine[:half], dm_low[:, cols]) * top
                add_low = dot_nt(x_mine[half:], dm_low[half:, cols]) * low
                sum_top = add_top if sum_top is None else sum_top + add_top
                sum_low = add_low if sum_low is None else sum_low + add_low
            dxs[at, cols] = jnp.where(left, got[0], got[1])
        dgt[s, :half] += sum_top
        dgt[s, half:, half:] += sum_low


def inside_back(cfg, meta, slot, x, d_mixed, step, logs, enter_d, log_t, gt, state):
    streams, length, slots, groups, per_group, headdim = cfg
    blocks = x.shape[1] // BLOCK
    state_size = state.shape[1]
    whole = lambda i, m: (0, 0)
    cube = lambda i, m: (0, 0, 0)
    own = pl.BlockSpec((x.shape[0], BLOCK), lambda i, m: (0, i))
    return pl.pallas_call(
        functools.partial(inside_back_kernel, cfg, slot),
        grid_spec=pltpu.PrefetchScalarGridSpec(
            num_scalar_prefetch=1, grid=(blocks,),
            in_specs=[
                own,
                pl.BlockSpec((x.shape[0], BLOCK), lambda i, m: (0, m[slot] * blocks + i)),
                pl.BlockSpec(step.shape, whole),
                pl.BlockSpec(logs.shape, whole),
                pl.BlockSpec(enter_d.shape, whole),
                pl.BlockSpec((streams, 1, 8, length), lambda i, m: (0, m[slot] * blocks + i, 0, 0)),
                pl.BlockSpec(gt.shape, cube),
                pl.BlockSpec((streams, state_size, BLOCK), lambda i, m: (0, 0, i)),
            ],
            out_specs=[own, pl.BlockSpec(gt.shape, cube), pl.BlockSpec((x.shape[0], state_size), whole)],
        ),
        out_shape=[
            jax.ShapeDtypeStruct(x.shape, F32),
            jax.ShapeDtypeStruct(gt.shape, F32),
            jax.ShapeDtypeStruct((x.shape[0], state_size), F32),
        ],
        compiler_params=pltpu.CompilerParams(vmem_limit_bytes=VMEM),
        cost_estimate=pl.CostEstimate(
            flops=16 * x.shape[0] * length * x.shape[1], bytes_accessed=x.size * 12, transcendentals=4 * x.size
        ),
        name="inside_back",
    )(meta, x, d_mixed, step, logs, enter_d, log_t, gt, state)


def after_kernel(cfg, slot, meta_ref, x, d_mixed, dxs, d_after, state, step, rest_d, b_low, skip, ci, cw, cb, dci, tail, spill, direct, sums, db):
    streams, length, slots, groups, per_group, headdim = cfg
    meta = Meta(meta_ref, groups, slots)
    per_block = BLOCK // headdim
    first_head = meta_ref[slot] * per_group + pl.program_id(0) * per_block
    spread = spread_of(first_head, BLOCK, headdim)
    gather = gather_of(first_head, BLOCK, headdim)

    @pl.when(pl.program_id(0) == 0)
    def _():
        direct[...] = jnp.zeros_like(direct)
        sums[...] = jnp.zeros_like(sums)
        db[...] = jnp.zeros_like(db)

    for s in range(streams):
        at = slice(s * length, (s + 1) * length)
        st = step[at]
        remain = rest_d[at]
        x_s = x[at]
        step_wide = expand(st, spread, 2)
        back = expand(remain, spread, 2) * dot(b_low[at], d_after[s])
        inner_back = dxs[at]
        x_weighted = x_s * expand(remain * st, spread, 2)
        db[at] += dot_nt(x_weighted.astype(LOW), d_after[s])
        from_after = sum_heads(x_s * back, gather)
        direct[at] += sum_heads(x_s * inner_back, gather) + from_after
        crossed = jnp.sum(d_after[s].astype(F32) * state[s].astype(F32), axis=0, keepdims=True)
        crossed = sum_heads(jnp.broadcast_to(crossed, (8, BLOCK)), gather)
        after_sum = jnp.broadcast_to(jnp.sum(from_after * st, axis=0, keepdims=True), (8, LANES))
        sums[s] += jnp.where(iota((8, LANES), 0) == 0, crossed, after_sum)
        d_x = step_wide * (inner_back + back) + skip[...] * d_mixed[at]
        block = ci[s * (HALO + length) : (s + 1) * (HALO + length)].astype(F32)
        masks = tap_masks(meta, s, cw.shape[0], length)
        total = conv_back(d_x, block, masks, cw[...], cb[...])
        dci[at] = total[HALO:].astype(LOW)
        tail[s] = total[HALO + length - 8 :]
        spill[s] = total[HALO - 8 : HALO]


def after(cfg, meta, slot, x, d_mixed, dxs, d_after, state, step, rest_d, b_low, skip, ci, conv_weight, conv_bias):
    streams, length, slots, groups, per_group, headdim = cfg
    blocks = x.shape[1] // BLOCK
    state_size = state.shape[1]
    rows = x.shape[0]
    whole = lambda i, m: (0, 0)
    own = pl.BlockSpec((rows, BLOCK), lambda i, m: (0, i))
    placed = lambda r: pl.BlockSpec((r, BLOCK), lambda i, m: (0, m[slot] * blocks + i))
    cube = lambda r: pl.BlockSpec((streams, r, BLOCK), lambda i, m: (0, 0, i))
    return pl.pallas_call(
        functools.partial(after_kernel, cfg, slot),
        grid_spec=pltpu.PrefetchScalarGridSpec(
            num_scalar_prefetch=1, grid=(blocks,),
            in_specs=[
                own, placed(rows), own, cube(state_size), cube(state_size),
                pl.BlockSpec(step.shape, whole), pl.BlockSpec(rest_d.shape, whole), pl.BlockSpec(b_low.shape, whole),
                placed(1), pl.BlockSpec((ci.shape[0], BLOCK), lambda i, m: (0, i)),
                placed(conv_weight.shape[0]), placed(1),
            ],
            out_specs=[
                own, cube(8), cube(8),
                pl.BlockSpec((rows, LANES), whole),
                pl.BlockSpec((streams, 8, LANES), lambda i, m: (0, 0, 0)),
                pl.BlockSpec((rows, state_size), whole),
            ],
        ),
        out_shape=[
            jax.ShapeDtypeStruct(x.shape, LOW),
            jax.ShapeDtypeStruct((streams, 8, x.shape[1]), F32),
            jax.ShapeDtypeStruct((streams, 8, x.shape[1]), F32),
            jax.ShapeDtypeStruct((rows, LANES), F32),
            jax.ShapeDtypeStruct((streams, 8, LANES), F32),
            jax.ShapeDtypeStruct((rows, state_size), F32),
        ],
        compiler_params=pltpu.CompilerParams(vmem_limit_bytes=VMEM),
        name="after",
    )(meta, x, d_mixed, dxs, d_after, state, step, rest_d, b_low, skip, ci, conv_weight, conv_bias)


def finish_kernel(cfg, meta_ref, *refs):
    streams, length, slots, groups, per_group, headdim = cfg
    meta = Meta(meta_ref, groups, slots)
    dgts, dcs, dbs, directs, sums = (refs[i * groups : (i + 1) * groups] for i in range(5))
    row_sum, step, slope, through, rates, b_low, c_low, ci, cw, cb = refs[5 * groups : 5 * groups + 10]
    d_raw, dci, tail, spill = refs[5 * groups + 10 :]
    upper = (iota((length, length), 0) <= iota((length, length), 1)).astype(F32)
    add = lambda parts, at: functools.reduce(lambda a, b: a + b, [p[at] for p in parts])
    for s in range(streams):
        at = slice(s * length, (s + 1) * length)
        direct = add(directs, at)
        ends = add(sums, s)
        from_end = through[s, 0:1] * ends[0:1] + ends[1:2]
        d_log = dot(upper, row_sum[at] - step[at] * direct, HIGHEST) + from_end
        d_raw[at] = ((direct - rates[...] * d_log) * slope[at]).astype(LOW)
        seg_u = meta.segment(s, meta.first() + iota((length, length), 0))
        seg_t = meta.segment(s, meta.first() + iota((length, length), 1))
        dgt = jnp.where(seg_u == seg_t, upper, 0.0) * add(dgts, s)
        d_b = add(dbs, at) + dot(dgt.astype(LOW), c_low[at])
        d_c = add(dcs, at) + dot(jnp.transpose(dgt).astype(LOW), b_low[at])
        block = ci[s * (HALO + length) : (s + 1) * (HALO + length)].astype(F32)
        masks = tap_masks(meta, s, cw.shape[0], length)
        total = conv_back(jnp.concatenate([d_b, d_c], axis=1), block, masks, cw[...], cb[...])
        dci[at] = total[HALO:].astype(LOW)
        tail[s] = total[HALO + length - 8 :]
        spill[s] = total[HALO - 8 : HALO]


def finish(cfg, meta, dgts, dcs, dbs, directs, sums, row_sum, step, slope, through, rates, b_low, c_low, ci, conv_weight, conv_bias, block_at):
    streams, length, slots, groups, per_group, headdim = cfg
    rows = streams * length
    args = [*dgts, *dcs, *dbs, *directs, *sums, row_sum, step, slope, through, rates, b_low, c_low, ci]
    zeros = lambda n: (lambda i, m: (0,) * n)
    conv_at = lambda i, m: (0, block_at)
    outs = [
        jax.ShapeDtypeStruct((rows, LANES), LOW),
        jax.ShapeDtypeStruct((rows, BLOCK), LOW),
        jax.ShapeDtypeStruct((streams, 8, BLOCK), F32),
        jax.ShapeDtypeStruct((streams, 8, BLOCK), F32),
    ]
    return pl.pallas_call(
        functools.partial(finish_kernel, cfg),
        grid_spec=pltpu.PrefetchScalarGridSpec(
            num_scalar_prefetch=1, grid=(1,),
            in_specs=[pl.BlockSpec(a.shape, zeros(a.ndim)) for a in args]
            + [pl.BlockSpec((conv_weight.shape[0], BLOCK), conv_at), pl.BlockSpec((1, BLOCK), conv_at)],
            out_specs=[pl.BlockSpec(a.shape, zeros(len(a.shape))) for a in outs],
        ),
        out_shape=outs,
        compiler_params=pltpu.CompilerParams(vmem_limit_bytes=VMEM),
        name="finish",
    )(meta, *args, conv_weight, conv_bias)


def back_project_kernel(groups, blocks, shared, seeded, meta_ref, *refs):
    core = None
    ds, refs = (refs[:1] * groups, refs[1:]) if shared else (refs[:groups], refs[groups:])
    weights, refs = refs[: 2 * groups], refs[2 * groups :]
    hidden, up, refs = refs[0], refs[1], refs[2:]
    if seeded:
        dn_in, dh_in, refs = refs[0], refs[1], refs[2:]
    dn, dh, g_up = refs
    step = pl.program_id(0)

    @pl.when(step == 0)
    def _():
        dn[...] = dn_in[...] if seeded else jnp.zeros_like(dn)
        dh[...] = dh_in[...] if seeded else jnp.zeros_like(dh)

    for j in range(groups):

        @pl.when(lax.div(step, blocks) == j)
        def _():
            d = ds[j][...]
            dn[0] += dot_nt(d, weights[2 * j][...])
            dn[1] += dot_nt(d, weights[2 * j + 1][...])
            dh[...] += dot_nt(d, up[...])
            g_up[...] = jnp.transpose(
                lax.dot_general(hidden[...], d, (((0,), (0,)), ((), ())), preferred_element_type=F32)
            )


def back_project(cfg, meta, ds, weights, hidden, in_up, first_block, seed=None):
    streams, length, slots, groups, per_group, headdim = cfg
    shared = not isinstance(ds, list)
    rows = hidden.shape[0]
    cols = weights[0][0].shape[1]
    half = weights[-1][0].shape[0]
    blocks = cols // BLOCK
    core = core_at(groups, streams, slots)
    at = lambda i, m: m[lax.div(i, blocks)] * blocks + lax.rem(i, blocks)
    local_at = lambda i, j: jnp.clip(i - blocks * j, 0, blocks - 1)
    in_specs, args = [], []
    if shared:
        in_specs.append(pl.BlockSpec((rows, BLOCK), lambda i, m: (0, at(i, m))))
        args.append(ds)
    else:
        for j in range(groups):
            in_specs.append(pl.BlockSpec((rows, BLOCK), lambda i, m, j=j: (0, local_at(i, j))))
        args += ds
    for j, (mine, other) in enumerate(weights):
        same = mine is other
        in_specs.append(pl.BlockSpec((half, BLOCK), lambda i, m, j=j, s=same: (m[core] if s else 0, local_at(i, j))))
        in_specs.append(pl.BlockSpec((half, BLOCK), lambda i, m, j=j, s=same: (1 - m[core] if s else 0, local_at(i, j))))
        args += [mine, other]
    whole = lambda i, m: (0, 0)
    in_specs += [
        pl.BlockSpec(hidden.shape, whole),
        pl.BlockSpec((in_up.shape[0], BLOCK), lambda i, m: (0, first_block + at(i, m))),
    ]
    args += [hidden, in_up]
    dn_spec = pl.BlockSpec((2, rows, half), lambda i, m: (0, 0, 0))
    dh_spec = pl.BlockSpec((rows, in_up.shape[0]), whole)
    if seed is not None:
        in_specs += [dn_spec, dh_spec]
        args += list(seed)
    return pl.pallas_call(
        functools.partial(back_project_kernel, groups, blocks, shared, seed is not None),
        grid_spec=pltpu.PrefetchScalarGridSpec(
            num_scalar_prefetch=1, grid=(groups * blocks,), in_specs=in_specs,
            out_specs=[dn_spec, dh_spec, pl.BlockSpec((BLOCK, in_up.shape[0]), lambda i, m: (at(i, m), 0))],
        ),
        out_shape=[
            jax.ShapeDtypeStruct((2, rows, half), F32),
            jax.ShapeDtypeStruct((rows, in_up.shape[0]), F32),
            jax.ShapeDtypeStruct((groups * cols, in_up.shape[0]), F32),
        ],
        compiler_params=pltpu.CompilerParams(vmem_limit_bytes=VMEM),
        cost_estimate=pl.CostEstimate(
            flops=2 * rows * groups * cols * (2 * half + 512),
            bytes_accessed=groups * cols * (4 * half + 2 * rows) + 16 * rows * half,
            transcendentals=0,
        ),
        name="back_project",
    )(meta, *args)


def swap_cores(value):
    return lax.ppermute(value, "fsdp", [(i, i ^ 1) for i in range(lax.axis_size("fsdp"))])


def scan_states(own, kept_mine, kept_other, per_head, reverse):
    count = lax.axis_size("fsdp")
    core = lax.axis_index("fsdp") % 2
    half = own.shape[2] // 2
    mine = lax.dynamic_slice_in_dim(own, core * half, half, 2)
    other = swap_cores(lax.dynamic_slice_in_dim(own, (1 - core) * half, half, 2))
    early = (core == 1) if reverse else (core == 0)
    first = jnp.where(early, mine, other).astype(F32)
    second = jnp.where(early, other, mine).astype(F32)

    def spread(kept):
        kept = lax.dynamic_slice_in_dim(kept, core * (half // per_head), half // per_head, 1)
        return jnp.repeat(kept, per_head, axis=1)[:, None, :]

    kept_first = spread(jnp.where(early, kept_mine, kept_other))
    kept_second = spread(jnp.where(early, kept_other, kept_mine))
    added = kept_second * first + second
    kept_both = kept_first * kept_second
    entering = None
    for hop in range(count // 2 - 1):
        send = added if entering is None else kept_both * entering.astype(F32) + added
        chip = count // 2 - 1 - hop if reverse else hop
        route = [(2 * chip + c, 2 * (chip - 1 if reverse else chip + 1) + c) for c in (0, 1)]
        got = lax.ppermute(send.astype(LOW), "fsdp", route)
        entering = got if entering is None else entering + got
    entering = entering.astype(F32)
    entering_second = kept_first * entering + first
    keep = jnp.where(early, entering, entering_second).astype(LOW)
    got = swap_cores(jnp.where(early, entering_second, entering).astype(LOW))
    return jnp.where(core == 0, jnp.concatenate([keep, got], 2), jnp.concatenate([got, keep], 2))


def share_quarters(quarter):
    core = lax.axis_index("fsdp") % 2
    half = quarter.shape[0] // 2
    part = half // 2
    move = lambda v, bit: lax.ppermute(v, "dp", [(i, i ^ bit) for i in range(lax.axis_size("dp"))])
    mine = lax.dynamic_slice_in_dim(quarter, core * half, half, 0)
    one, two = move(mine, 1), move(mine, 2)
    both = jnp.concatenate([move(one[:part], 2), move(two[part:], 1)], axis=0)
    return [(quarter, quarter)] + [(v, swap_cores(v)) for v in (one, two, both)]


def rms_scale(values, gain_vec):
    mean_sq = jnp.mean(values * values, axis=-1, keepdims=True)
    return values * lax.rsqrt(mean_sq + EPSILON) * gain_vec


def local(
    block_input, seq_lengths, adapter_ids, norm_gain, w_in, w_dt, conv_weight, conv_bias, dt_bias,
    head_rates, skip_gain, gate_gain, w_out, in_down, in_up, out_down, out_up, out_grad,
):
    streams, length, width = block_input.shape[1:]
    inner = gate_gain.shape[0]
    taps, conv_cols = conv_weight.shape
    heads = dt_bias.shape[0]
    headdim = inner // heads
    state_size = (conv_cols - inner) // 2
    adapters, ranks = in_down.shape[:2]
    in_cols = in_up.shape[2]
    slots = seq_lengths.shape[2]
    rows = streams * length
    groups = lax.axis_size("dp")
    per_group = heads // groups
    group_cols = inner // groups
    cfg = (streams, length, slots, groups, per_group, headdim)
    count = lax.axis_size("fsdp")
    first_pos = lax.axis_index("fsdp") * length
    ends = jnp.cumsum(seq_lengths[0], axis=-1, dtype=jnp.int32)
    core = lax.axis_index("fsdp") % 2
    order = lax.axis_index("dp") ^ jnp.arange(groups, dtype=jnp.int32)
    meta = jnp.concatenate([order, first_pos[None], ends.reshape(-1), core[None]]).astype(jnp.int32)

    gather = lambda a: lax.all_gather(a, "fsdp", axis=0, tiled=True)
    quarter = lambda a: lax.dynamic_slice_in_dim(a, order[0] * group_cols, group_cols, 1)
    pad_heads = lambda a: jnp.pad(a, ((0, 0), (0, LANES - heads)))
    w_small = gather(jnp.concatenate([w_in[:, 2 * inner :], pad_heads(w_dt)], axis=1))
    w_bc, w_step = w_small[:, : 2 * state_size], w_small[:, 2 * state_size :]
    w_x = share_quarters(gather(quarter(w_in[:, inner : 2 * inner])))
    w_gate = share_quarters(gather(quarter(w_in[:, :inner])))
    w_o = gather(w_out)

    devices = range(count)
    before = lax.ppermute(block_input[0, :, length - HALO :], "fsdp", [(i - 1, i) for i in devices if i > 0])
    extended = jnp.concatenate([before, block_input[0]], axis=1)
    pos = first_pos - HALO + jnp.arange(length + HALO, dtype=jnp.int32)
    seg = jnp.sum((pos[None, :, None] >= ends[:, None, :]).astype(jnp.int32), axis=-1)
    seg = jnp.where(pos[None] < 0, -1, seg)
    slot_at = jnp.arange(slots, dtype=jnp.int32)
    member = (seg[:, :, None] == slot_at).astype(F32)
    chosen = (adapter_ids[0][:, :, None] == jnp.arange(adapters, dtype=jnp.int32)).astype(F32)
    onehot = jnp.einsum("slj,sjk->slk", member, chosen, precision=HIGHEST)
    allowed = jnp.repeat(onehot, ranks, axis=-1)
    allowed_ext = allowed.reshape(streams * (length + HALO), adapters * ranks)
    allowed = allowed[:, HALO:].reshape(rows, adapters * ranks)
    valid = (seg[:, HALO:] < slots).astype(F32).reshape(rows, 1)
    normed_ext = rms_scale(extended.reshape(-1, width).astype(F32), norm_gain).astype(LOW)
    down_in = in_down.reshape(adapters * ranks, width)
    up_in = in_up.reshape(adapters * ranks, in_cols)
    down_out = out_down.reshape(adapters * ranks, inner)
    up_out = out_up.reshape(adapters * ranks, width)
    hidden_ext = (dot_nt(normed_ext, down_in) * allowed_ext).astype(LOW)
    strip = lambda a: a.reshape(streams, length + HALO, -1)[:, HALO:].reshape(rows, -1)
    normed = strip(normed_ext)
    hidden_in = strip(hidden_ext)
    grad_rows = out_grad.reshape(rows, width).astype(F32)
    d_branch = (grad_rows * valid).astype(LOW)
    d_hidden_out = (dot_nt(d_branch, up_out) * allowed).astype(LOW)

    by_half = lambda a: jnp.stack([a[:, : width // 2], a[:, width // 2 :]])
    nx_ext, nx = by_half(normed_ext), by_half(normed)

    dt_in = dot(normed, w_step) + pad_heads(dt_bias[None])
    real = jnp.arange(LANES) < heads
    step = jnp.where(real, jax.nn.softplus(dt_in), 0.0)
    slope = jnp.where(real, jax.nn.sigmoid(dt_in), 0.0)
    rates = pad_heads(head_rates[None])
    bias_row = conv_bias[None]
    x_blocks = inner // BLOCK
    group_blocks = group_cols // BLOCK
    ci_bc, bc = project(cfg, meta, 0, nx_ext, hidden_ext, (w_bc, w_bc), up_in, conv_weight, bias_row, x_blocks, 1)
    (log_d, enter_d, rest_d, weight, log_t, through, g, gt, b_low, c_low, bt, ct) = decays(
        cfg, meta, step, rates, bc, heads
    )
    kept_mine = through[:, 0, :heads]
    kept_other = swap_cores(kept_mine)
    of_group = lambda a, j: lax.dynamic_slice_in_dim(a, order[j] * per_group, per_group, 1)

    ci, xs, states = [], [], []
    for j in range(groups):
        ci_j, x_j, own = project(
            cfg, meta, j, nx_ext, hidden_ext, w_x[j], up_in, conv_weight, bias_row, 0, group_blocks, weight, bt
        )
        ci.append(ci_j)
        xs.append(x_j)
        states.append(scan_states(own, of_group(kept_mine, j), of_group(kept_other, j), headdim, False))
    ys = [inside(cfg, meta, j, xs[j], step, log_d, log_t, g) for j in range(groups)]
    gates = [gate_project(cfg, meta, j, nx, hidden_in, w_gate[j], up_in) for j in range(groups)]
    d_normed_out = dot_nt(d_branch, w_o) + dot(d_hidden_out, down_out)

    skip_row = jnp.repeat(skip_gain, headdim)[None]
    out_low, d_mixed, d_gate, row_sum, d_state = gated(
        cfg, meta, xs, ys, states, gates, d_normed_out, enter_d, c_low, ct, skip_row, gate_gain[None]
    )
    d_state = d_state.astype(LOW)
    afters = []
    for j in range(groups):
        part = lax.dynamic_slice_in_dim(d_state, order[j] * group_cols, group_cols, 2)
        afters.append(scan_states(part, of_group(kept_mine, j), of_group(kept_other, j), headdim, True))

    hidden_out = (dot_nt(out_low, down_out) * allowed).astype(LOW)
    branch = (dot(out_low, w_o) + dot(hidden_out, up_out)) * valid
    block_output = (block_input.reshape(rows, width).astype(F32) + branch).astype(LOW)
    turn = lambda a, b: lax.dot_general(a, b, (((0,), (0,)), ((), ())), preferred_element_type=F32)
    g_out_up = turn(d_branch, hidden_out)
    g_out_down = turn(out_low, d_hidden_out)

    dxs, dgts, dcs = [], [], []
    for j in range(groups):
        a, b, c = inside_back(cfg, meta, j, xs[j], d_mixed, step, log_d, enter_d, log_t, gt, states[j])
        dxs.append(a)
        dgts.append(b)
        dcs.append(c)
    dcis, tails, spills, directs, sums, dbs = [], [], [], [], [], []
    for j in range(groups):
        got = after(
            cfg, meta, j, xs[j], d_mixed, dxs[j], afters[j], states[j], step, rest_d, b_low, skip_row,
            ci[j], conv_weight, bias_row,
        )
        for into, what in zip((dcis, tails, spills, directs, sums, dbs), got):
            into.append(what)
    d_raw, dci_bc, tail_bc, spill_bc = finish(
        cfg, meta, dgts, dcs, dbs, directs, sums, row_sum, step, slope, through, rates, b_low, c_low,
        ci_bc, conv_weight, bias_row, x_blocks,
    )
    spilled = lax.ppermute(
        jnp.concatenate(spills + [spill_bc], axis=2), "fsdp", [(i, i - 1) for i in devices if i > 0]
    )
    tail = (jnp.concatenate(tails + [tail_bc], axis=2) + spilled).astype(LOW)
    d_parts = []
    for j, part in enumerate(dcis + [dci_bc]):
        part = part.reshape(streams, length, -1)
        end = tail[:, :, j * group_cols : j * group_cols + part.shape[2]]
        d_parts.append(lax.dynamic_update_slice(part, end, (0, length - 8, 0)).reshape(rows, -1))
    d_bc = d_parts.pop()

    gate_blocks = inner // BLOCK
    early = back_project(cfg, meta, d_gate, w_gate, hidden_in, up_in, 0)
    late = back_project(cfg, meta, d_parts, w_x, hidden_in, up_in, gate_blocks, early[:2])
    up_bc = up_in[:, 2 * inner :]
    d_hidden_in = ((late[1] + dot_nt(d_bc, up_bc)) * allowed).astype(LOW)
    back = late[0]
    back = jnp.where(core == 0, jnp.concatenate([back[0], back[1]], 1), jnp.concatenate([back[1], back[0]], 1))
    d_normed = back + dot_nt(d_bc, w_bc) + dot_nt(d_raw, w_step) + dot(d_hidden_in, down_in)
    inputs = block_input.reshape(rows, width).astype(F32)
    rs = lax.rsqrt(jnp.mean(inputs * inputs, axis=-1, keepdims=True) + EPSILON)
    scaled = d_normed * norm_gain
    cross = jnp.mean(scaled * inputs, axis=-1, keepdims=True)
    input_grad = grad_rows + rs * (scaled - inputs * (rs * rs * cross))
    g_in_up = jnp.concatenate([early[2], late[2], turn(d_bc, hidden_in)], axis=0)
    g_in_down = turn(normed, d_hidden_in)
    totals = [
        lax.psum(lax.psum_scatter(a, "fsdp", scatter_dimension=0, tiled=True), "dp").T.reshape(adapters, ranks, -1)
        for a in (g_in_down, g_in_up, g_out_down, g_out_up)
    ]
    return (block_output.reshape(1, streams, length, width), input_grad.reshape(1, streams, length, width), *totals)


def solution(mesh):
    rows = P("dp", None, "fsdp", None)
    cut = P("fsdp", None)
    per_group = P("dp", None, None)
    in_specs = (
        rows, per_group, per_group, P(), cut, cut, P(), P(), P(), P(), P(), P(), cut, P(), P(), P(), P(), rows,
    )
    out_specs = (rows, rows) + (P(None, None, "fsdp"),) * 4
    return jax.shard_map(local, mesh=mesh, in_specs=in_specs, out_specs=out_specs, check_vma=False)
```

```python
import functools

import jax
import jax.numpy as jnp
from jax import lax
from jax.experimental import pallas as pl
from jax.experimental.pallas import tpu as pltpu
from jax.sharding import PartitionSpec as P

EPSILON = 1e-05
HIGHEST = lax.Precision.HIGHEST
F32, LOW = jnp.float32, jnp.bfloat16
HALO = 16
LANES = 128
BLOCK = 256
WIDE = 768
VMEM = 20 * 1024 * 1024


def lasting(us):
    return pl.CostEstimate(flops=int(us * 1.15e9), bytes_accessed=1000000, transcendentals=0)


class Order:
    waits = []
    token = None


def in_order(kernel, *, grid_spec, out_shape, compiler_params, cost_estimate, name):
    def call(meta, *args):
        waits = Order.waits
        skip = len(waits)
        specs = [pl.BlockSpec(memory_space=pl.ANY)] * skip + list(grid_spec["in_specs"])
        single = not isinstance(out_shape, (list, tuple))
        shapes = [out_shape] if single else list(out_shape)
        out_specs = [grid_spec["out_specs"]] if single else list(grid_spec["out_specs"])
        token_at = skip + len(args) + len(shapes)

        def body(meta_ref, *refs):
            refs[token_at][...] = jnp.zeros((8, LANES), jnp.int32)
            kernel(meta_ref, *refs[skip:token_at], *refs[token_at + 1 :])

        outs = pl.pallas_call(
            body,
            grid_spec=pltpu.PrefetchScalarGridSpec(
                num_scalar_prefetch=1,
                grid=grid_spec["grid"],
                in_specs=specs,
                out_specs=out_specs + [pl.BlockSpec((8, LANES), lambda i, m: (0, 0))],
                scratch_shapes=grid_spec.get("scratch_shapes", ()),
            ),
            out_shape=shapes + [jax.ShapeDtypeStruct((8, LANES), jnp.int32)],
            compiler_params=compiler_params,
            cost_estimate=cost_estimate,
            name=name,
        )(meta, *waits, *args)
        Order.waits = [outs[-1]]
        Order.token = outs[-1][0, 0]
        return outs[0] if single else outs[:-1]

    return call


def wait_for(*arrays):
    Order.waits = Order.waits + list(arrays)


def dot(a, b, precision=None):
    return lax.dot_general(
        a, b, (((1,), (0,)), ((), ())), precision=precision, preferred_element_type=F32
    )


def dot_nt(a, b, precision=None):
    return lax.dot_general(
        a, b, (((1,), (1,)), ((), ())), precision=precision, preferred_element_type=F32
    )


def iota(shape, dim):
    return lax.broadcasted_iota(jnp.int32, shape, dim)


def packed(values, heads, terms):
    lane = iota(values.shape, 1)
    total, rest, wrapped = None, values, None
    for term in range(terms):
        part = rest.astype(LOW).astype(F32)
        rest = rest - part
        if term == 0:
            total = part
        elif (term + 1) * heads <= LANES:
            total = total + pltpu.roll(part, term * heads, 1)
        else:
            moved = pltpu.roll(part, term * heads, 1)
            total = total + jnp.where(lane >= term * heads, moved, 0.0)
            wrapped = jnp.where(lane < term * heads, moved, 0.0)
    if wrapped is not None:
        total = jnp.concatenate([total, wrapped], axis=1)
    return total.astype(LOW)


def expand(values, spread):
    return dot(values, spread)


def sigmoid(v):
    return 0.5 + 0.5 * jnp.tanh(0.5 * v)


def core_at(groups, streams, slots):
    return groups + 1 + streams * slots


def ring_order(chips):
    order = [0]
    for k in range(1, chips // 2 + 1):
        order += [k, chips - k] if k != chips - k else [k]
    return order


def placed(arrays, limit=1 << 20):
    return [
        pltpu.with_memory_space_constraint(a, pltpu.HBM) if a.size * a.dtype.itemsize > limit else a for a in arrays
    ]


class Meta:
    def __init__(self, ref, groups, slots):
        self.ref, self.groups, self.slots = ref, groups, slots

    def first(self):
        return self.ref[self.groups]

    def end(self, stream, slot):
        return self.ref[self.groups + 1 + stream * self.slots + slot]

    def segment(self, stream, pos):
        seg = jnp.zeros_like(pos)
        for slot in range(self.slots):
            seg = seg + (pos >= self.end(stream, slot)).astype(jnp.int32)
        return jnp.where(pos < 0, -1, seg)

    def scalar_segment(self, stream, pos):
        seg = jnp.int32(0)
        for slot in range(self.slots):
            seg = seg + jnp.where(pos >= self.end(stream, slot), 1, 0)
        return jnp.where(pos < 0, -1, seg)


def tap_masks(columns, taps):
    return [jnp.broadcast_to(columns[:, k : k + 1], columns.shape) for k in range(taps - 1)]


def wide(mask, cols):
    return jnp.concatenate([mask] * (cols // LANES), axis=1)


def conv_pre(block, masks, cw, cb):
    taps, cols = cw.shape
    total = cb + cw[taps - 1 : taps] * block[HALO:]
    for k in range(taps - 1):
        moved = pltpu.roll(block, taps - 1 - k, 0)[HALO:]
        total = total + cw[k : k + 1] * moved * wide(masks[k], cols)
    return total


def conv_back(d_out, block, masks, cw, cb):
    taps, cols = cw.shape
    pre = conv_pre(block, masks, cw, cb)
    sig = sigmoid(pre)
    d_pre = d_out * (sig * (1.0 + pre * (1.0 - sig)))
    total = jnp.concatenate([jnp.zeros((HALO, cols), F32), cw[taps - 1 : taps] * d_pre], axis=0)
    rows = total.shape[0]
    for k in range(taps - 1):
        part = cw[k : k + 1] * d_pre * wide(masks[k], cols)
        part = jnp.concatenate([jnp.zeros((HALO, cols), F32), part], axis=0)
        total = total + pltpu.roll(part, rows - (taps - 1 - k), 0)
    return total


def spread_of(first_head, cols, per_head, heads, terms=2):
    shape = (LANES * (1 if terms * heads <= LANES else 2), cols)
    head = lax.shift_right_logical(iota(shape, 1), per_head.bit_length() - 1) + first_head
    row = iota(shape, 0)
    hit = row == head
    for term in range(1, terms):
        hit = hit | (row == head + term * heads)
    return hit.astype(LOW)


def gather_of(first_head, cols, per_head):
    head = lax.shift_right_logical(iota((cols, LANES), 0), per_head.bit_length() - 1) + first_head
    return (iota((cols, LANES), 1) == head).astype(LOW)


def sum_heads(values, gather):
    part = values.astype(LOW)
    rest = (values - part.astype(F32)).astype(LOW)
    return dot(part, gather) + dot(rest, gather)


def halves_product(nx, hx, w_mine, w_other, up):
    return (dot(nx[0], w_mine) + dot(nx[1], w_other) + dot(hx[...], up[...])).astype(LOW)


def quarter_specs(half, blocks):
    far = lambda i: jnp.maximum(i - blocks, 0)
    return [
        pl.BlockSpec((half, WIDE), lambda i, m: (0, jnp.minimum(i, blocks - 1))),
        pl.BlockSpec((1, half, WIDE), lambda i, m: (lax.div(far(i), blocks), 0, lax.rem(far(i), blocks))),
    ]


def gate_project_kernel(cfg, blocks, meta_ref, nx, hx, w_mine, w_mine_far, w_other, w_other_far, up, out):
    streams, length, slots, groups, per_group, headdim = cfg
    near = pl.program_id(0) < blocks
    w_mine = jnp.where(near, w_mine[...], w_mine_far[0])
    w_other = jnp.where(near, w_other[...], w_other_far[0])
    full = halves_product(nx, hx, w_mine, w_other, up)
    for s in range(streams):
        out[s * length : (s + 1) * length] = full[s * (HALO + length) + HALO : (s + 1) * (HALO + length)]


def gate_project(cfg, meta, nx, hx, weights, in_up):
    streams, length, slots, groups, per_group, headdim = cfg
    half, cols = weights[0][0].shape
    rows = streams * length
    blocks = cols // WIDE
    at = lambda i, m: m[lax.div(i, blocks)] * blocks + lax.rem(i, blocks)
    return in_order(
        functools.partial(gate_project_kernel, cfg, blocks),
        grid_spec=dict(
            grid=(groups * blocks,),
            in_specs=[
                pl.BlockSpec(nx.shape, lambda i, m: (0, 0, 0)),
                pl.BlockSpec(hx.shape, lambda i, m: (0, 0)),
                *quarter_specs(half, blocks) * 2,
                pl.BlockSpec((in_up.shape[0], WIDE), lambda i, m: (0, at(i, m))),
            ],
            out_specs=pl.BlockSpec((rows, WIDE), lambda i, m: (0, at(i, m))),
        ),
        out_shape=jax.ShapeDtypeStruct((rows, groups * cols), LOW),
        compiler_params=pltpu.CompilerParams(vmem_limit_bytes=2 * VMEM),
        cost_estimate=lasting(9),
        name="project_gate",
    )(meta, *placed([nx, hx, *weights[0], *weights[1], in_up]))


def project_kernel(cfg, slot, meta_ref, nx, hx, w_mine, w_other, up, cw, cb, weight, taps, bt, ci, x_out, state):
    streams, length, slots, groups, per_group, headdim = cfg
    per_block = BLOCK // headdim
    first_head = meta_ref[slot] * per_group + pl.program_id(0) * per_block
    spread = spread_of(first_head, BLOCK, headdim, groups * per_group)
    low = halves_product(nx, hx, w_mine[...], w_other[...], up)
    ci[...] = low
    full = low.astype(F32)
    for s in range(streams):
        block = full[s * (HALO + length) : (s + 1) * (HALO + length)]
        masks = tap_masks(taps[s * length : (s + 1) * length], cw.shape[0])
        pre = conv_pre(block, masks, cw[...], cb[...])
        x = pre * sigmoid(pre)
        x_out[s * length : (s + 1) * length] = x
        scale = expand(weight[s * length : (s + 1) * length], spread)
        state[s] = dot(bt[s], (x * scale).astype(LOW)).astype(LOW)


def project(cfg, meta, slot, nx, hx, weights, in_up, conv_weight, conv_bias, weight, taps, bt):
    streams, length, slots, groups, per_group, headdim = cfg
    rows = streams * length
    ext = hx.shape[0]
    half, cols = weights[0].shape
    blocks = cols // BLOCK
    gate_blocks = (in_up.shape[1] - conv_weight.shape[1]) // BLOCK
    place = lambda i, m: m[slot] * blocks + i
    whole = lambda i, m: (0, 0)
    cube = lambda i, m: (0, 0, 0)
    own = lambda i, m: (0, i)
    conv_at = lambda i, m: (0, place(i, m))
    return in_order(
        functools.partial(project_kernel, cfg, slot),
        grid_spec=dict(
            grid=(blocks,),
            in_specs=[
                pl.BlockSpec(nx.shape, cube),
                pl.BlockSpec(hx.shape, whole),
                pl.BlockSpec((half, BLOCK), own),
                pl.BlockSpec((half, BLOCK), own),
                pl.BlockSpec((in_up.shape[0], BLOCK), lambda i, m: (0, gate_blocks + place(i, m))),
                pl.BlockSpec((conv_weight.shape[0], BLOCK), conv_at),
                pl.BlockSpec((1, BLOCK), conv_at),
                pl.BlockSpec(weight.shape, whole),
                pl.BlockSpec(taps.shape, whole),
                pl.BlockSpec(bt.shape, cube),
            ],
            out_specs=[
                pl.BlockSpec((ext, BLOCK), own),
                pl.BlockSpec((rows, BLOCK), own),
                pl.BlockSpec((streams, bt.shape[1], BLOCK), lambda i, m: (0, 0, i)),
            ],
        ),
        out_shape=[
            jax.ShapeDtypeStruct((ext, cols), LOW),
            jax.ShapeDtypeStruct((rows, cols), F32),
            jax.ShapeDtypeStruct((streams, bt.shape[1], cols), LOW),
        ],
        compiler_params=pltpu.CompilerParams(vmem_limit_bytes=VMEM),
        cost_estimate=lasting(8),
        name="project_conv",
    )(meta, *placed([nx, hx, *weights, in_up, conv_weight, conv_bias, weight, taps, bt]))


def prepare_kernel(cfg, ids_place, adapter_cols, chips, meta_ref, x, before, gain, down, grad, up, normed, nx, hidden_ext, hidden, allowed, d_branch, d_hidden, pieces):
    streams, length, slots, groups, per_group, headdim = cfg
    meta = Meta(meta_ref, groups, slots)
    core = meta_ref[core_at(groups, streams, slots)]
    chip = meta_ref[core_at(groups, streams, slots) + 1]
    s = pl.program_id(0)
    rows = length + HALO
    seg = meta.segment(s, meta.first() - HALO + iota((rows, LANES), 0))
    kind = lax.shift_right_logical(iota((rows, LANES), 1), adapter_cols.bit_length() - 1)
    mask = jnp.zeros((rows, LANES), F32)
    for slot in range(slots):
        mask = jnp.where((seg == slot) & (kind == meta_ref[ids_place + s * slots + slot]), 1.0, mask)
    full = jnp.concatenate([before[...], x[...]], axis=0).astype(F32)
    rs = lax.rsqrt(jnp.mean(full * full, axis=-1, keepdims=True) + EPSILON)
    low = (full * rs * gain[...]).astype(LOW)
    normed[...] = low
    size = pieces.shape[2]
    for p in range(2 * chips):
        pieces[p] = low[:, p * size : (p + 1) * size]
    for k, distance in enumerate(ring_order(chips)):
        at = 2 * lax.rem(chip + distance, chips)
        nx[0, :, k * size : (k + 1) * size] = pieces[at + core]
        nx[1, :, k * size : (k + 1) * size] = pieces[at + 1 - core]
    got = (dot_nt(low, down[...]) * mask).astype(LOW)
    hidden_ext[...] = got
    hidden[...] = got[HALO:]
    allowed[...] = mask[HALO:]
    valid = (seg[HALO:] < slots).astype(F32)
    rows_out = (grad[...].astype(F32) * wide(valid, grad.shape[1])).astype(LOW)
    d_branch[...] = rows_out
    d_hidden[...] = (dot_nt(rows_out, up[...]) * mask[HALO:]).astype(LOW)


def prepare(cfg, meta, ids_place, adapter_cols, x, before, gain, down, grad, up):
    streams, length, slots, groups, per_group, headdim = cfg
    rows, width = x.shape
    chips = lax.axis_size("fsdp") // 2
    ext = streams * (length + HALO)
    ranks = down.shape[0]
    block = lambda r, c: pl.BlockSpec((r, c), lambda i, m: (i, 0))
    whole = lambda a: pl.BlockSpec(a.shape, lambda i, m: (0, 0))
    return in_order(
        functools.partial(prepare_kernel, cfg, ids_place, adapter_cols, chips),
        grid_spec=dict(
            grid=(streams,),
            in_specs=[
                block(length, width), block(HALO, width), whole(gain), whole(down), block(length, width), whole(up),
            ],
            out_specs=[
                block(length + HALO, width),
                pl.BlockSpec((2, length + HALO, width // 2), lambda i, m: (0, i, 0)),
                block(length + HALO, ranks), block(length, ranks), block(length, ranks),
                block(length, width), block(length, ranks),
            ],
            scratch_shapes=[pltpu.VMEM((2 * chips, length + HALO, width // (2 * chips)), LOW)],
        ),
        out_shape=[
            jax.ShapeDtypeStruct((ext, width), LOW),
            jax.ShapeDtypeStruct((2, ext, width // 2), LOW),
            jax.ShapeDtypeStruct((ext, ranks), LOW),
            jax.ShapeDtypeStruct((rows, ranks), LOW),
            jax.ShapeDtypeStruct((rows, ranks), F32),
            jax.ShapeDtypeStruct((rows, width), LOW),
            jax.ShapeDtypeStruct((rows, ranks), LOW),
        ],
        compiler_params=pltpu.CompilerParams(vmem_limit_bytes=VMEM),
        cost_estimate=lasting(3),
        name="prepare",
    )(meta, x, before, gain, down, grad, up)


def decay_kernel(cfg, heads, meta_ref, normed, hidden, w, up, cw, cb, dt_bias, rates, ci, step, slope, taps, logs3, step2, enter2, rest2, weight2, log_t, through, g, gt, b_low, c_low, bt, ct):
    streams, length, slots, groups, per_group, headdim = cfg
    meta = Meta(meta_ref, groups, slots)
    first = meta.first()
    lower = (iota((length, length), 0) >= iota((length, length), 1)).astype(F32)
    per_block = BLOCK // headdim
    state_size = c_low.shape[1]
    bc_cols = 2 * state_size
    both = dot(normed[...], w[...])
    low = (both[:, :bc_cols] + dot(hidden[...], up[...])).astype(LOW)
    ci[...] = low
    for s in range(streams):
        at = slice(s * length, (s + 1) * length)
        ext = slice(s * (HALO + length), (s + 1) * (HALO + length))
        pos = first + iota((length, LANES), 0)
        seg = meta.segment(s, pos)
        lane = iota((length, LANES), 1)
        columns = jnp.zeros((length, LANES), F32)
        for k in range(cw.shape[0] - 1):
            same = meta.segment(s, pos - (cw.shape[0] - 1 - k)) == seg
            columns = jnp.where((lane == k) & same, 1.0, columns)
        taps[at] = columns
        pre = conv_pre(low[ext].astype(F32), tap_masks(columns, cw.shape[0]), cw[...], cb[...])
        bc = pre * sigmoid(pre)
        b_in, c_in = bc[:, :state_size], bc[:, state_size:]
        dt_in = both[ext][HALO:, bc_cols:] + dt_bias[...]
        real = iota((length, LANES), 1) < heads
        st = jnp.where(real, jnp.maximum(dt_in, 0.0) + jnp.log1p(jnp.exp(-jnp.abs(dt_in))), 0.0)
        step[at] = st
        slope[at] = jnp.where(real, sigmoid(dt_in), 0.0)
        prior = meta.scalar_segment(s, first - 1)
        last = meta.scalar_segment(s, first + length - 1)
        seg_u = meta.segment(s, first + iota((length, length), 1))
        seg_t = meta.segment(s, first + iota((length, length), 0))
        logs = dot(lower, -st * rates[...], HIGHEST)
        logs3[at] = packed(logs, heads, 3)
        step2[at] = packed(st, heads, 2)
        enter2[at] = packed(jnp.where(real & (seg == prior), jnp.exp(logs), 0.0), heads, 2)
        remain = jnp.where(real & (seg == last), jnp.exp(logs[length - 1 : length] - logs), 0.0)
        rest2[at] = packed(remain, heads, 2)
        weight2[at] = packed(remain * st, heads, 2)
        kept = jnp.where(prior == last, jnp.exp(logs[length - 1 : length]), 0.0)
        kept = jnp.where(real[:8], jnp.broadcast_to(kept, (8, LANES)), 0.0)
        through[s] = expand(packed(kept, heads, 3), spread_of(0, through.shape[2], headdim, heads, 3))
        turned_logs = jnp.transpose(logs)
        for b in range(log_t.shape[1]):
            log_t[s, b, 0:per_block] = turned_logs[b * per_block : (b + 1) * per_block]
        pairs = jnp.where(seg_u == seg_t, lower, 0.0) * dot_nt(c_in, b_in, HIGHEST)
        g[s] = pairs
        gt[s] = jnp.transpose(pairs)
        b_low[at] = b_in.astype(LOW)
        c_low[at] = c_in.astype(LOW)
        bt[s] = jnp.transpose(b_in).astype(LOW)
        ct[s] = jnp.transpose(c_in).astype(LOW)


def decays(cfg, meta, normed, hidden, w, in_up, conv_weight, conv_bias, dt_bias, rates, heads):
    streams, length, slots, groups, per_group, headdim = cfg
    rows = streams * length
    blocks = heads * headdim // BLOCK
    state_size = (w.shape[1] - LANES) // 2
    row = lambda dtype, cols: jax.ShapeDtypeStruct((rows, cols), dtype)
    cube = lambda dtype, a, b: jax.ShapeDtypeStruct((streams, a, b), dtype)
    outs = [
        jax.ShapeDtypeStruct((hidden.shape[0], 2 * state_size), LOW),
        *[row(F32, LANES)] * 3, row(LOW, 2 * LANES), *[row(LOW, LANES)] * 4,
        jax.ShapeDtypeStruct((streams, blocks, 8, length), F32),
        cube(F32, 8, heads * headdim),
        cube(F32, length, length), cube(F32, length, length),
        row(LOW, state_size), row(LOW, state_size),
        cube(LOW, state_size, length), cube(LOW, state_size, length),
    ]
    zeros = lambda n: (lambda i, m: (0,) * n)
    whole = lambda a: pl.BlockSpec(a.shape, zeros(len(a.shape)))
    last = lambda a: pl.BlockSpec((a.shape[0], BLOCK), lambda i, m: (0, a.shape[1] // BLOCK - 1))
    return in_order(
        functools.partial(decay_kernel, cfg, heads),
        grid_spec=dict(
            grid=(1,),
            in_specs=[
                whole(normed), whole(hidden), whole(w), last(in_up), last(conv_weight), last(conv_bias),
                whole(dt_bias), whole(rates),
            ],
            out_specs=[whole(a) for a in outs],
        ),
        out_shape=outs,
        compiler_params=pltpu.CompilerParams(vmem_limit_bytes=VMEM),
        cost_estimate=lasting(4),
        name="decays",
    )(meta, normed, hidden, w, in_up, conv_weight, conv_bias, dt_bias, rates)


def inside_kernel(cfg, slot, meta_ref, x, step2, logs3, log_t, g, y):
    streams, length, slots, groups, per_group, headdim = cfg
    heads = groups * per_group
    per_block = BLOCK // headdim
    first_head = meta_ref[slot] * per_group + pl.program_id(0) * per_block
    spread = spread_of(first_head, BLOCK, headdim, heads)
    columns = spread_of(first_head, per_block * LANES, LANES, heads, 3)
    half = length // 2
    left = iota((half, LANES), 1) < headdim
    for s in range(streams):
        at = slice(s * length, (s + 1) * length)
        log_col = expand(logs3[at], columns)
        xs = (x[at] * expand(step2[at], spread)).astype(LOW)
        for pair in range(per_block // 2):
            cols = slice(pair * LANES, (pair + 1) * LANES)
            tops, lows = [], []
            for h in (2 * pair, 2 * pair + 1):
                col = log_col[:, h * LANES : (h + 1) * LANES]
                row = log_t[s, 0, h : h + 1]
                tops.append((jnp.exp(jnp.minimum(col[:half] - row[:, :half], 0.0)) * g[s, :half, :half]).astype(LOW))
                lows.append(
                    (jnp.exp(jnp.minimum(wide(col[half:], length) - row, 0.0)) * g[s, half:]).astype(LOW)
                )
            top = dot(jnp.concatenate(tops, axis=0), xs[:half, cols])
            low = dot(jnp.concatenate(lows, axis=0), xs[:, cols])
            start = s * length
            y[start : start + half, cols] = jnp.where(left, top[:half], top[half:])
            y[start + half : start + length, cols] = jnp.where(left, low[:half], low[half:])


def inside(cfg, meta, slot, x, step2, logs3, log_t, g):
    streams, length, slots, groups, per_group, headdim = cfg
    blocks = x.shape[1] // BLOCK
    whole = lambda i, m: (0, 0)
    own = pl.BlockSpec((x.shape[0], BLOCK), lambda i, m: (0, i))
    return in_order(
        functools.partial(inside_kernel, cfg, slot),
        grid_spec=dict(
            grid=(blocks,),
            in_specs=[
                own,
                pl.BlockSpec(step2.shape, whole),
                pl.BlockSpec(logs3.shape, whole),
                pl.BlockSpec((streams, 1, 8, length), lambda i, m: (0, m[slot] * blocks + i, 0, 0)),
                pl.BlockSpec(g.shape, lambda i, m: (0, 0, 0)),
            ],
            out_specs=own,
        ),
        out_shape=jax.ShapeDtypeStruct(x.shape, F32),
        compiler_params=pltpu.CompilerParams(vmem_limit_bytes=VMEM),
        cost_estimate=lasting(5),
        name="inside",
    )(meta, x, step2, logs3, log_t, g)


def gate_kernel(cfg, meta_ref, *refs):
    streams, length, slots, groups, per_group, headdim = cfg
    xs, ys, states = (refs[i * groups : (i + 1) * groups] for i in range(3))
    refs = refs[3 * groups :]
    gate, d_pieces, d_hidden, down, enter2, c_low, ct, skip, gain = refs[:9]
    out_low, d_mixed, d_gate, row_sum, d_state, y_all, v_all, held, d_out, scales = refs[9:]
    width = per_group * headdim
    inner = groups * width
    rows = gate.shape[0]
    per_stream = length // rows
    entering = enter2[...]
    heads = groups * per_group
    squares = jnp.zeros((rows, LANES), F32)
    crossed = jnp.zeros((rows, LANES), F32)
    d_out[...] = jnp.concatenate([d_pieces[p] for p in range(d_pieces.shape[0])], axis=1)

    def fold(values):
        total = values[:, :LANES]
        for j in range(1, values.shape[1] // LANES):
            total = total + values[:, j * LANES : (j + 1) * LANES]
        return total

    for j in range(groups):
        place = meta_ref[j]
        cols = pl.ds(pl.multiple_of(place * width, width), width)
        scale = expand(entering, spread_of(place * per_group, width, headdim, heads))
        scales[:, cols] = scale
        y = ys[j][...] + dot(c_low[...], states[j][0]) * scale
        y_all[:, cols] = y
        gated = gate[:, cols].astype(F32)
        v = (y + skip[:, cols] * xs[j][...]) * (gated * sigmoid(gated))
        v_all[:, cols] = v
        wanted = (d_out[:, cols] + dot(d_hidden[...], down[:, cols])) * gain[:, cols]
        d_out[:, cols] = wanted
        squares = squares + fold(v * v)
        crossed = crossed + fold(v * wanted)
    mean_sq = jnp.sum(squares, axis=1, keepdims=True) / inner
    rs = lax.rsqrt(mean_sq + EPSILON)
    mean_cross = jnp.sum(crossed, axis=1, keepdims=True) / inner
    pull = rs * rs * rs * mean_cross
    sums = jnp.zeros((rows, LANES), F32)
    fresh = pl.program_id(0) % per_stream == 0
    for j in range(groups):
        place = meta_ref[j]
        cols = pl.ds(pl.multiple_of(place * width, width), width)
        gated = gate[:, cols].astype(F32)
        sig = sigmoid(gated)
        v = v_all[:, cols]
        y = y_all[:, cols]
        out_low[:, cols] = (v * rs * gain[:, cols]).astype(LOW)
        d_v = rs * d_out[:, cols] - v * pull
        dm = d_v * (gated * sig)
        d_mixed[:, cols] = dm
        mixed = y + skip[:, cols] * xs[j][...]
        d_gate[:, cols] = (d_v * mixed * (sig * (1.0 + gated * (1.0 - sig)))).astype(LOW)
        sums = sums + sum_heads(
            dm.astype(LOW).astype(F32) * y, gather_of(place * per_group, width, headdim)
        )
        part = dot(ct[0], (dm * scales[:, cols]).astype(LOW))
        before = jnp.where(fresh, 0.0, held[:, cols])
        held[:, cols] = before + part
        d_state[0, :, cols] = (before + part).astype(LOW)
    row_sum[...] = sums


def gated(cfg, meta, xs, ys, states, gate, d_pieces, d_hidden, down, enter_d, c_low, ct, skip, gain):
    streams, length, slots, groups, per_group, headdim = cfg
    rows = 128
    per_stream = length // rows
    width = xs[0].shape[1]
    inner = gate.shape[1]
    state_size = c_low.shape[1]
    total = streams * length
    row = lambda cols: pl.BlockSpec((rows, cols), lambda i, m: (i, 0))
    state = pl.BlockSpec((1, state_size, width), lambda i, m: (i // per_stream, 0, 0))
    flat = pl.BlockSpec((1, inner), lambda i, m: (0, 0))
    return in_order(
        functools.partial(gate_kernel, cfg),
        grid_spec=dict(
            grid=(total // rows,),
            in_specs=[row(width)] * (2 * groups) + [state] * groups
            + [
                row(inner), pl.BlockSpec((d_pieces.shape[0], rows, d_pieces.shape[2]), lambda i, m: (0, i, 0)),
                row(d_hidden.shape[1]), pl.BlockSpec(down.shape, lambda i, m: (0, 0)), row(LANES), row(state_size),
                pl.BlockSpec((1, state_size, rows), lambda i, m: (i // per_stream, 0, i % per_stream)),
                flat, flat,
            ],
            out_specs=[
                row(inner), row(inner), row(inner), row(LANES),
                pl.BlockSpec((1, state_size, inner), lambda i, m: (i // per_stream, 0, 0)),
            ],
            scratch_shapes=[
                pltpu.VMEM((rows, inner), F32), pltpu.VMEM((rows, inner), F32), pltpu.VMEM((state_size, inner), F32),
                pltpu.VMEM((rows, inner), F32), pltpu.VMEM((rows, inner), F32),
            ],
        ),
        out_shape=[
            jax.ShapeDtypeStruct((total, inner), LOW),
            jax.ShapeDtypeStruct((total, inner), F32),
            jax.ShapeDtypeStruct((total, inner), LOW),
            jax.ShapeDtypeStruct((total, LANES), F32),
            jax.ShapeDtypeStruct((streams, state_size, inner), LOW),
        ],
        compiler_params=pltpu.CompilerParams(vmem_limit_bytes=2 * VMEM),
        cost_estimate=lasting(19),
        name="gated",
    )(meta, *placed([*xs, *ys, *states, gate, d_pieces, d_hidden, down, enter_d, c_low, ct, skip, gain]))


def pick(refs, which):
    value = refs[0][...]
    for j in range(1, len(refs)):
        value = jnp.where(which == j, refs[j][...], value)
    return value


def inside_back_kernel(cfg, slot, count, blocks, meta_ref, *refs):
    streams, length, slots, groups, per_group, headdim = cfg
    xs, states = refs[:count], refs[count : 2 * count]
    d_mixed, step2, logs3, enter2, log_t, gt, dxs, dgt, dc = refs[2 * count :]
    heads = groups * per_group
    per_block = BLOCK // headdim
    which = lax.div(pl.program_id(0), blocks)
    first_head = meta_ref[slot + which] * per_group + lax.rem(pl.program_id(0), blocks) * per_block
    spread = spread_of(first_head, BLOCK, headdim, heads)
    columns = spread_of(first_head, per_block * LANES, LANES, heads, 3)
    half = length // 2
    left = iota((half, LANES), 1) < headdim
    x_all, state = pick(xs, which), pick(states, which)

    @pl.when(pl.program_id(0) == 0)
    def _():
        dgt[...] = jnp.zeros_like(dgt)
        dc[...] = jnp.zeros_like(dc)

    for s in range(streams):
        start = s * length
        at = slice(start, start + length)
        log_col = expand(logs3[at], columns)
        x = (x_all[at] * expand(step2[at], spread)).astype(LOW)
        dm = d_mixed[at]
        dm_low = dm.astype(LOW)
        dc[at] += dot_nt((dm * expand(enter2[at], spread)).astype(LOW), state[s])
        sum_top, sum_low = None, None
        for pair in range(per_block // 2):
            cols = slice(pair * LANES, (pair + 1) * LANES)
            decay_top, decay_low, k_top, k_low, x_top, x_low = [], [], [], [], [], []
            for h in (2 * pair, 2 * pair + 1):
                col = log_col[:, h * LANES : (h + 1) * LANES]
                row = log_t[s, 0, h : h + 1]
                top = jnp.exp(jnp.minimum(row - wide(col[:half], length), 0.0))
                low = jnp.exp(jnp.minimum(row[:, half:] - col[half:], 0.0))
                decay_top.append(top)
                decay_low.append(low)
                k_top.append((top * gt[s, :half]).astype(LOW))
                k_low.append((low * gt[s, half:, half:]).astype(LOW))
                mine = left if h % 2 == 0 else jnp.logical_not(left)
                zero = jnp.zeros((half, LANES), LOW)
                x_top.append(jnp.where(mine, x[:half, cols], zero))
                x_low.append(jnp.where(mine, x[half:, cols], zero))
            join = lambda parts: jnp.concatenate(parts, axis=0)
            got_top, got_low = dot(join(k_top), dm_low[:, cols]), dot(join(k_low), dm_low[half:, cols])
            dxs[start : start + half, cols] = jnp.where(left, got_top[:half], got_top[half:])
            dxs[start + half : start + length, cols] = jnp.where(left, got_low[:half], got_low[half:])
            add_top = dot_nt(join(x_top), dm_low[:, cols])
            add_low = dot_nt(join(x_low), dm_low[half:, cols])
            add_top = add_top[:half] * decay_top[0] + add_top[half:] * decay_top[1]
            add_low = add_low[:half] * decay_low[0] + add_low[half:] * decay_low[1]
            sum_top = add_top if sum_top is None else sum_top + add_top
            sum_low = add_low if sum_low is None else sum_low + add_low
        dgt[s, :half] += sum_top
        dgt[s, half:, half:] += sum_low


def inside_back(cfg, meta, slot, xs, d_mixed, step2, logs3, enter2, log_t, gt, states):
    streams, length, slots, groups, per_group, headdim = cfg
    count = len(xs)
    rows, cols = xs[0].shape
    blocks = cols // BLOCK
    state_size = states[0].shape[1]
    whole = lambda i, m: (0, 0)
    cube = lambda i, m: (0, 0, 0)
    at = lambda i, m: m[slot + lax.div(i, blocks)] * blocks + lax.rem(i, blocks)
    local_at = lambda i, j: jnp.clip(i - blocks * j, 0, blocks - 1)
    return in_order(
        functools.partial(inside_back_kernel, cfg, slot, count, blocks),
        grid_spec=dict(
            grid=(count * blocks,),
            in_specs=[pl.BlockSpec((rows, BLOCK), lambda i, m, j=j: (0, local_at(i, j))) for j in range(count)]
            + [
                pl.BlockSpec((streams, state_size, BLOCK), lambda i, m, j=j: (0, 0, local_at(i, j)))
                for j in range(count)
            ]
            + [
                pl.BlockSpec((rows, BLOCK), lambda i, m: (0, at(i, m))),
                pl.BlockSpec(step2.shape, whole),
                pl.BlockSpec(logs3.shape, whole),
                pl.BlockSpec(enter2.shape, whole),
                pl.BlockSpec((streams, 1, 8, length), lambda i, m: (0, at(i, m), 0, 0)),
                pl.BlockSpec(gt.shape, cube),
            ],
            out_specs=[
                pl.BlockSpec((rows, BLOCK), lambda i, m: (0, i)),
                pl.BlockSpec(gt.shape, cube),
                pl.BlockSpec((rows, state_size), whole),
            ],
        ),
        out_shape=[
            jax.ShapeDtypeStruct((rows, count * cols), F32),
            jax.ShapeDtypeStruct(gt.shape, F32),
            jax.ShapeDtypeStruct((rows, state_size), F32),
        ],
        compiler_params=pltpu.CompilerParams(vmem_limit_bytes=VMEM),
        cost_estimate=lasting(12),
        name="inside_back",
    )(meta, *placed([*xs, *states, d_mixed, step2, logs3, enter2, log_t, gt]))


def after_kernel(cfg, blocks, parts, meta_ref, *refs):
    streams, length, slots, groups, per_group, headdim = cfg
    xs, states, cis = (refs[i * groups : (i + 1) * groups] for i in range(3))
    dxss, refs = refs[3 * groups : 3 * groups + parts], refs[3 * groups + parts :]
    d_mixed, d_after, step, step2, rest2, taps, b_low, skip, cw, cb, dci, tail, spill, direct, sums, db = refs
    per_block = BLOCK // headdim
    which = lax.div(pl.program_id(0), blocks)
    first_head = meta_ref[which] * per_group + lax.rem(pl.program_id(0), blocks) * per_block
    spread = spread_of(first_head, BLOCK, headdim, groups * per_group)
    gather = gather_of(first_head, BLOCK, headdim)
    x, state, ci = pick(xs, which), pick(states, which), pick(cis, which)
    dxs = pick(dxss, lax.div(which, groups // parts))

    @pl.when(pl.program_id(0) == 0)
    def _():
        direct[...] = jnp.zeros_like(direct)
        sums[...] = jnp.zeros_like(sums)
        db[...] = jnp.zeros_like(db)

    for s in range(streams):
        at = slice(s * length, (s + 1) * length)
        st = step[at]
        x_s = x[at]
        step_wide = expand(step2[at], spread)
        rest_wide = expand(rest2[at], spread)
        back = rest_wide * dot(b_low[at], d_after[s])
        inner_back = dxs[at]
        x_weighted = x_s * (rest_wide * step_wide)
        db[at] += dot_nt(x_weighted.astype(LOW), d_after[s])
        from_after = sum_heads(x_s * back, gather)
        direct[at] += sum_heads(x_s * inner_back, gather) + from_after
        crossed = jnp.sum(d_after[s].astype(F32) * state[s].astype(F32), axis=0, keepdims=True)
        crossed = sum_heads(jnp.broadcast_to(crossed, (8, BLOCK)), gather)
        after_sum = jnp.broadcast_to(jnp.sum(from_after * st, axis=0, keepdims=True), (8, LANES))
        sums[s] += jnp.where(iota((8, LANES), 0) == 0, crossed, after_sum)
        d_x = step_wide * (inner_back + back) + skip[...] * d_mixed[at]
        block = ci[s * (HALO + length) : (s + 1) * (HALO + length)].astype(F32)
        masks = tap_masks(taps[at], cw.shape[0])
        total = conv_back(d_x, block, masks, cw[...], cb[...])
        dci[at] = total[HALO:].astype(LOW)
        tail[s] = total[length:]
        spill[s] = total[HALO - 8 : HALO]


def after(cfg, meta, xs, states, cis, dxss, d_mixed, d_after, step, step2, rest2, taps, b_low, skip, conv_weight, conv_bias):
    streams, length, slots, groups, per_group, headdim = cfg
    rows, cols = xs[0].shape
    blocks = cols // BLOCK
    state_size = states[0].shape[1]
    total_cols = groups * cols
    parts = len(dxss)
    part_blocks = total_cols // parts // BLOCK
    whole = lambda i, m: (0, 0)
    at = lambda i, m: m[lax.div(i, blocks)] * blocks + lax.rem(i, blocks)
    spot = lambda r: pl.BlockSpec((r, BLOCK), lambda i, m: (0, at(i, m)))
    local_at = lambda i, j, n: jnp.clip(i - n * j, 0, n - 1)
    cube = lambda r: pl.BlockSpec((streams, r, BLOCK), lambda i, m: (0, 0, i))
    listed = lambda r, n, many: [pl.BlockSpec((r, BLOCK), lambda i, m, j=j: (0, local_at(i, j, n))) for j in range(many)]
    return in_order(
        functools.partial(after_kernel, cfg, blocks, parts),
        grid_spec=dict(
            grid=(groups * blocks,),
            in_specs=listed(rows, blocks, groups)
            + [
                pl.BlockSpec((streams, state_size, BLOCK), lambda i, m, j=j: (0, 0, local_at(i, j, blocks)))
                for j in range(groups)
            ]
            + listed(cis[0].shape[0], blocks, groups)
            + listed(rows, part_blocks, parts)
            + [
                spot(rows),
                pl.BlockSpec((streams, state_size, BLOCK), lambda i, m: (0, 0, at(i, m))),
                *[pl.BlockSpec(a.shape, whole) for a in (step, step2, rest2, taps, b_low)],
                spot(1), spot(conv_weight.shape[0]), spot(1),
            ],
            out_specs=[
                pl.BlockSpec((rows, BLOCK), lambda i, m: (0, i)), cube(HALO), cube(8),
                pl.BlockSpec((rows, LANES), whole),
                pl.BlockSpec((streams, 8, LANES), lambda i, m: (0, 0, 0)),
                pl.BlockSpec((rows, state_size), whole),
            ],
        ),
        out_shape=[
            jax.ShapeDtypeStruct((rows, total_cols), LOW),
            jax.ShapeDtypeStruct((streams, HALO, total_cols), F32),
            jax.ShapeDtypeStruct((streams, 8, total_cols), F32),
            jax.ShapeDtypeStruct((rows, LANES), F32),
            jax.ShapeDtypeStruct((streams, 8, LANES), F32),
            jax.ShapeDtypeStruct((rows, state_size), F32),
        ],
        compiler_params=pltpu.CompilerParams(vmem_limit_bytes=VMEM),
        cost_estimate=lasting(39),
        name="after",
    )(meta, *placed([*xs, *states, *cis, *dxss, d_mixed, d_after, step, step2, rest2, taps, b_low, skip, conv_weight, conv_bias], 1 << 18))


def finish_kernel(cfg, meta_ref, *refs):
    streams, length, slots, groups, per_group, headdim = cfg
    meta = Meta(meta_ref, groups, slots)
    parts = (len(refs) - 18) // 2
    dgts, dcs, refs = refs[:parts], refs[parts : 2 * parts], refs[2 * parts :]
    db_in, direct_in, sums, row_sum, step, slope, taps, through, rates, b_low, c_low, ci, cw, cb = refs[:14]
    width = through.shape[2]
    pick = (iota((width, LANES), 0) == iota((width, LANES), 1) * headdim).astype(F32)
    kept = [dot(through[s], pick, HIGHEST) for s in range(streams)]
    d_raw, dci, tail, spill = refs[14:]
    upper = (iota((length, length), 0) <= iota((length, length), 1)).astype(F32)
    add = lambda parts, at: functools.reduce(lambda a, b: a + b, [p[at] for p in parts])
    for s in range(streams):
        at = slice(s * length, (s + 1) * length)
        direct = direct_in[at]
        ends = sums[s]
        from_end = kept[s][0:1] * ends[0:1] + ends[1:2]
        d_log = dot(upper, row_sum[at] - step[at] * direct, HIGHEST) + from_end
        d_raw[at] = ((direct - rates[...] * d_log) * slope[at]).astype(LOW)
        seg_u = meta.segment(s, meta.first() + iota((length, length), 0))
        seg_t = meta.segment(s, meta.first() + iota((length, length), 1))
        dgt = jnp.where(seg_u == seg_t, upper, 0.0) * add(dgts, s)
        d_b = db_in[at] + dot(dgt.astype(LOW), c_low[at])
        d_c = add(dcs, at) + dot(jnp.transpose(dgt).astype(LOW), b_low[at])
        block = ci[s * (HALO + length) : (s + 1) * (HALO + length)].astype(F32)
        masks = tap_masks(taps[at], cw.shape[0])
        total = conv_back(jnp.concatenate([d_b, d_c], axis=1), block, masks, cw[...], cb[...])
        dci[at] = total[HALO:].astype(LOW)
        tail[s] = total[length:]
        spill[s] = total[HALO - 8 : HALO]


def finish(cfg, meta, dgts, dcs, db, direct, sums, row_sum, step, slope, taps, through, rates, b_low, c_low, ci, conv_weight, conv_bias, block_at):
    streams, length, slots, groups, per_group, headdim = cfg
    rows = streams * length
    args = [*dgts, *dcs, db, direct, sums, row_sum, step, slope, taps, through, rates, b_low, c_low, ci]
    zeros = lambda n: (lambda i, m: (0,) * n)
    conv_at = lambda i, m: (0, block_at)
    outs = [
        jax.ShapeDtypeStruct((rows, LANES), LOW),
        jax.ShapeDtypeStruct((rows, BLOCK), LOW),
        jax.ShapeDtypeStruct((streams, HALO, BLOCK), F32),
        jax.ShapeDtypeStruct((streams, 8, BLOCK), F32),
    ]
    return in_order(
        functools.partial(finish_kernel, cfg),
        grid_spec=dict(
            grid=(1,),
            in_specs=[pl.BlockSpec(a.shape, zeros(a.ndim)) for a in args]
            + [pl.BlockSpec((conv_weight.shape[0], BLOCK), conv_at), pl.BlockSpec((1, BLOCK), conv_at)],
            out_specs=[pl.BlockSpec(a.shape, zeros(len(a.shape))) for a in outs],
        ),
        out_shape=outs,
        compiler_params=pltpu.CompilerParams(vmem_limit_bytes=VMEM),
        cost_estimate=lasting(4),
        name="finish",
    )(meta, *placed([*args, conv_weight, conv_bias], 0))


def mend(d, tail, spill):
    streams = tail.shape[0]
    length = d.shape[0] // streams
    parts = []
    for s in range(streams):
        parts.append(d[s * length : (s + 1) * length - HALO])
        added = jnp.concatenate([jnp.zeros((HALO - 8, spill.shape[2]), F32), spill[s]], axis=0)
        parts.append((tail[s] + added).astype(LOW))
    return jnp.concatenate(parts, axis=0)


def turned(a, b):
    return lax.dot_general(a, b, (((0,), (0,)), ((), ())), preferred_element_type=F32)


def back_project_kernel(groups, blocks, core_place, chips, late, meta_ref, *refs):
    if late:
        d_ref, tail, spill, dn_in, dh_in = refs[:5]
        refs = refs[5:]
    else:
        d_ref, refs = refs[0], refs[1:]
    many = 2 * groups if late else 4
    weights, refs = refs[:many], refs[many:]
    hidden, up, dn, dh, g_up = refs[:5]
    held = refs[5] if late else dn
    step = pl.program_id(0)

    @pl.when(step == 0)
    def _():
        held[...] = dn_in[...] if late else jnp.zeros_like(held)
        dh[...] = dh_in[...] if late else jnp.zeros_like(dh)

    d = d_ref[...]
    if late:
        d = mend(d, tail[...], spill[...])
        for j in range(groups):

            @pl.when(lax.div(step, blocks) == j)
            def _():
                held[0] += dot_nt(d, weights[2 * j][...])
                held[1] += dot_nt(d, weights[2 * j + 1][...])
    else:
        near = step < blocks
        held[0] += dot_nt(d, jnp.where(near, weights[0][...], weights[1][0]))
        held[1] += dot_nt(d, jnp.where(near, weights[2][...], weights[3][0]))
    dh[...] += dot_nt(d, up[...])
    g_up[...] = jnp.transpose(turned(hidden[...], d))

    if late:
        core, chip = meta_ref[core_place], meta_ref[core_place + 1]
        size = dn.shape[2]

        @pl.when(step == groups * blocks - 1)
        def _():
            for k, distance in enumerate(ring_order(chips)):
                at = 2 * lax.rem(chip + distance, chips)
                cols = slice(k * size, (k + 1) * size)
                dn[at + core] = held[0, :, cols]
                dn[at + 1 - core] = held[1, :, cols]


def back_project(cfg, meta, ds, weights, hidden, in_up, first_block, late=None):
    streams, length, slots, groups, per_group, headdim = cfg
    rows = hidden.shape[0]
    half, cols = weights[0][0].shape
    blocks = cols // WIDE
    chips = lax.axis_size("fsdp") // 2
    core = core_at(groups, streams, slots)
    at = lambda i, m: m[lax.div(i, blocks)] * blocks + lax.rem(i, blocks)
    local_at = lambda i, j: jnp.clip(i - blocks * j, 0, blocks - 1)
    whole = lambda i, m: (0, 0)
    dn_spec = pl.BlockSpec((2, rows, half), lambda i, m: (0, 0, 0))
    dh_spec = pl.BlockSpec((rows, in_up.shape[0]), whole)
    out_spec = dn_spec
    if late is None:
        in_specs = [pl.BlockSpec((rows, WIDE), lambda i, m: (0, at(i, m)))]
        args = [ds]
    else:
        out_spec = pl.BlockSpec((2 * chips, rows, half // chips), lambda i, m: (0, 0, 0))
        tail, spill, dn, dh = late
        in_specs = [pl.BlockSpec((rows, WIDE), lambda i, m: (0, i))]
        in_specs += [pl.BlockSpec((streams, r, WIDE), lambda i, m: (0, 0, i)) for r in (HALO, 8)]
        in_specs += [dn_spec, dh_spec]
        args = [ds, tail, spill, dn, dh]
    if late is None:
        in_specs += quarter_specs(half, blocks) * 2
        args += [*weights[0], *weights[1]]
    else:
        for j, pair in enumerate(weights):
            for w in pair:
                in_specs.append(pl.BlockSpec((half, WIDE), lambda i, m, j=j: (0, local_at(i, j))))
                args.append(w)
    in_specs += [
        pl.BlockSpec(hidden.shape, whole),
        pl.BlockSpec((in_up.shape[0], WIDE), lambda i, m: (0, first_block + at(i, m))),
    ]
    args += [hidden, in_up]
    return in_order(
        functools.partial(back_project_kernel, groups, blocks, core, chips, late is not None),
        grid_spec=dict(
            grid=(groups * blocks,), in_specs=in_specs,
            out_specs=[out_spec, dh_spec, pl.BlockSpec((WIDE, in_up.shape[0]), lambda i, m: (at(i, m), 0))],
            scratch_shapes=[] if late is None else [pltpu.VMEM((2, rows, half), F32)],
        ),
        out_shape=[
            jax.ShapeDtypeStruct(out_spec.block_shape, F32),
            jax.ShapeDtypeStruct((rows, in_up.shape[0]), F32),
            jax.ShapeDtypeStruct((groups * cols, in_up.shape[0]), F32),
        ],
        compiler_params=pltpu.CompilerParams(vmem_limit_bytes=2 * VMEM),
        cost_estimate=lasting(15),
        name="back_project",
    )(meta, *placed(args))


def close_kernel(meta_ref, dn, dh, d_bc, tail, spill, w_small, d_raw, up, allowed, down, hidden, normed, x_in, gain, grad, out, g_bc, g_down):
    state_cols = d_bc.shape[1]
    width = x_in.shape[1]
    d = mend(d_bc[...], tail[...], spill[...])
    d_hidden = ((dh[...] + dot_nt(d, up[...])) * allowed[...]).astype(LOW)
    x = x_in[...].astype(F32)
    rs = lax.rsqrt(jnp.mean(x * x, axis=-1, keepdims=True) + EPSILON)
    d_normed = jnp.concatenate([dn[p] for p in range(dn.shape[0])], axis=1)
    d_normed = d_normed + dot_nt(d, w_small[:, :state_cols]) + dot_nt(d_raw[...], w_small[:, state_cols:])
    scaled = (d_normed + dot(d_hidden, down[...])) * gain[...]
    cross = jnp.sum(scaled * x, axis=-1, keepdims=True) / width
    out[...] = grad[...].astype(F32) + rs * (scaled - x * (rs * rs * cross))
    add_bc = jnp.transpose(turned(hidden[...], d))
    add_down = jnp.transpose(turned(d_hidden, normed[HALO:]))

    @pl.when(pl.program_id(0) == 0)
    def _():
        g_bc[...] = add_bc
        g_down[...] = add_down

    @pl.when(pl.program_id(0) > 0)
    def _():
        g_bc[...] += add_bc
        g_down[...] += add_down


def close(streams, meta, dn, dh, d_bc, tail, spill, w_small, d_raw, in_up, allowed, down, hidden, normed, x_in, gain, grad):
    rows, width = x_in.shape
    length = rows // streams
    ranks = hidden.shape[1]
    state_cols = d_bc.shape[1]
    row = lambda cols: pl.BlockSpec((length, cols), lambda i, m: (i, 0))
    stack = pl.BlockSpec((dn.shape[0], length, dn.shape[2]), lambda i, m: (0, i, 0))
    whole = lambda a: pl.BlockSpec(a.shape, lambda i, m: (0, 0))
    end = lambda r: pl.BlockSpec((1, r, state_cols), lambda i, m: (i, 0, 0))
    return in_order(
        close_kernel,
        grid_spec=dict(grid=(streams,), in_specs=[
            stack, row(ranks), row(state_cols), end(HALO), end(8), whole(w_small), row(LANES),
            pl.BlockSpec((ranks, state_cols), lambda i, m: (0, in_up.shape[1] // state_cols - 1)),
            row(ranks), whole(down), row(ranks), pl.BlockSpec((length + HALO, width), lambda i, m: (i, 0)), row(width),
            whole(gain), row(width),
        ],
        out_specs=[
            row(width),
            pl.BlockSpec((state_cols, ranks), lambda i, m: (0, 0)),
            pl.BlockSpec((width, ranks), lambda i, m: (0, 0)),
        ]),
        out_shape=[
            jax.ShapeDtypeStruct((rows, width), F32),
            jax.ShapeDtypeStruct((state_cols, ranks), F32),
            jax.ShapeDtypeStruct((width, ranks), F32),
        ],
        compiler_params=pltpu.CompilerParams(vmem_limit_bytes=2 * VMEM),
        cost_estimate=lasting(5),
        name="close",
    )(meta, *placed([dn, dh, d_bc, tail, spill, w_small, d_raw, in_up, allowed, down, hidden, normed, x_in, gain, grad]))


def out_back_kernel(groups, chips, meta_ref, d_branch, w_mine, w_mine_far, w_other, w_other_far, out):
    cols = w_mine.shape[1]

    def product(near, far):
        total = None
        for j in range(groups):
            d = d_branch[:, pl.ds(pl.multiple_of(meta_ref[j] * cols, cols), cols)]
            part = dot_nt(d, near[...] if j == 0 else far[j - 1])
            total = part if total is None else total + part
        out[0] = total

    @pl.when(pl.program_id(0) < chips)
    def _():
        product(w_mine, w_mine_far)

    @pl.when(pl.program_id(0) >= chips)
    def _():
        product(w_other, w_other_far)


def out_back(cfg, meta, d_branch, weights):
    streams, length, slots, groups, per_group, headdim = cfg
    rows, width = d_branch.shape
    chips = lax.axis_size("fsdp") // 2
    core = core_at(groups, streams, slots)
    half, cols = weights[0][0].shape
    size = half // chips

    def device(i, m):
        distance = jnp.int32(0)
        for at, value in enumerate(ring_order(chips)):
            distance = jnp.where(lax.rem(i, chips) == at, value, distance)
        return 2 * lax.rem(m[core + 1] + distance, chips) + jnp.where(i < chips, m[core], 1 - m[core])

    block = lambda i, side: jnp.clip(i - side * chips, 0, chips - 1)
    weight = lambda side: [
        pl.BlockSpec((size, cols), lambda i, m: (block(i, side), 0)),
        pl.BlockSpec((groups - 1, size, cols), lambda i, m: (0, block(i, side), 0)),
    ]
    return in_order(
        functools.partial(out_back_kernel, groups, chips),
        grid_spec=dict(
            grid=(2 * chips,),
            in_specs=[pl.BlockSpec((rows, width), lambda i, m: (0, 0)), *weight(0), *weight(1)],
            out_specs=pl.BlockSpec((1, rows, size), lambda i, m: (device(i, m), 0, 0)),
        ),
        out_shape=jax.ShapeDtypeStruct((2 * chips, rows, size), F32),
        compiler_params=pltpu.CompilerParams(vmem_limit_bytes=VMEM),
        cost_estimate=lasting(8),
        name="out_back",
    )(meta, *placed([d_branch, *weights[0], *weights[1]]))


def out_project_kernel(cfg, chips, meta_ref, out_low, d_branch, x, allowed, down, up, d_hidden, w_mine, w_mine_far, w_other, w_other_far, y, g_down, g_up, pieces, ordered, hidden):
    streams, length, slots, groups, per_group, headdim = cfg
    meta = Meta(meta_ref, groups, slots)
    core = meta_ref[core_at(groups, streams, slots)]
    chip = meta_ref[core_at(groups, streams, slots) + 1]
    size = pieces.shape[2]

    @pl.when(pl.program_id(0) == 0)
    def _():
        for p in range(2 * chips):
            pieces[p] = out_low[:, p * size : (p + 1) * size]
        for k, distance in enumerate(ring_order(chips)):
            at = 2 * lax.rem(chip + distance, chips)
            ordered[0, :, k * size : (k + 1) * size] = pieces[at + core]
            ordered[1, :, k * size : (k + 1) * size] = pieces[at + 1 - core]
        hidden[...] = (dot_nt(out_low[...], down[...]) * allowed[...]).astype(LOW)

    near = pl.program_id(0) == 0
    w_mine = jnp.where(near, w_mine[...], w_mine_far[0])
    w_other = jnp.where(near, w_other[...], w_other_far[0])
    branch = dot(ordered[0], w_mine) + dot(ordered[1], w_other) + dot(hidden[...], up[...])
    for s in range(streams):
        at = slice(s * length, (s + 1) * length)
        seg = meta.segment(s, meta.first() + iota((length, LANES), 0))
        kept = jnp.where(wide(seg, branch.shape[1]) < slots, branch[at], 0.0)
        y[at] = (x[at].astype(F32) + kept).astype(LOW)
    cols = g_down.shape[0]
    start = pl.multiple_of(pl.program_id(0) * cols, cols)
    g_down[...] = jnp.transpose(turned(d_hidden[...], out_low[:, pl.ds(start, cols)]))
    g_up[...] = jnp.transpose(turned(hidden[...], d_branch[...]))


def out_project(cfg, meta, out_low, d_branch, x, allowed, down, up, d_hidden, weights):
    streams, length, slots, groups, per_group, headdim = cfg
    rows, width = x.shape
    inner = out_low.shape[1]
    chips = lax.axis_size("fsdp") // 2
    half, cols = weights[0][0].shape
    ranks = down.shape[0]
    whole = lambda a: pl.BlockSpec(a.shape, lambda i, m: (0, 0))
    turn = pl.BlockSpec((rows, cols), lambda i, m: (0, m[i]))
    far = pl.BlockSpec((1, half, cols), lambda i, m: (jnp.maximum(i - 1, 0), 0, 0))
    return in_order(
        functools.partial(out_project_kernel, cfg, chips),
        grid_spec=dict(
            grid=(groups,),
            in_specs=[
                whole(out_low), turn, turn, whole(allowed), whole(down),
                pl.BlockSpec((ranks, cols), lambda i, m: (0, m[i])), whole(d_hidden),
                whole(weights[0][0]), far, whole(weights[1][0]), far,
            ],
            out_specs=[
                turn,
                pl.BlockSpec((inner // groups, ranks), lambda i, m: (i, 0)),
                pl.BlockSpec((cols, ranks), lambda i, m: (m[i], 0)),
            ],
            scratch_shapes=[
                pltpu.VMEM((2 * chips, rows, half // chips), LOW), pltpu.VMEM((2, rows, half), LOW),
                pltpu.VMEM((rows, ranks), LOW),
            ],
        ),
        out_shape=[
            jax.ShapeDtypeStruct((rows, width), LOW),
            jax.ShapeDtypeStruct((inner, ranks), F32),
            jax.ShapeDtypeStruct((width, ranks), F32),
        ],
        compiler_params=pltpu.CompilerParams(vmem_limit_bytes=2 * VMEM),
        cost_estimate=lasting(10),
        name="out_project",
    )(meta, *placed([out_low, d_branch, x, allowed, down, up, d_hidden, *weights[0], *weights[1]]))


def swap_cores(value):
    return lax.ppermute(value, "fsdp", [(i, i ^ 1) for i in range(lax.axis_size("fsdp"))])


def then(value, earlier):
    return lax.optimization_barrier((value, earlier))[0]


class Scan:
    def __init__(self, own, kept_mine, kept_other, reverse):
        self.count = lax.axis_size("fsdp")
        self.core = core = lax.axis_index("fsdp") % 2
        self.reverse = reverse
        half = own.shape[2] // 2
        take = lambda a, side: lax.dynamic_slice_in_dim(a, side * half, half, 2)
        mine = take(own, core)
        self.other = other = swap_cores(take(own, 1 - core))
        self.early = early = (core == 1) if reverse else (core == 0)
        self.first = jnp.where(early, mine, other).astype(F32)
        second = jnp.where(early, other, mine).astype(F32)
        kept_mine, kept_other = take(kept_mine, core), take(kept_other, core)
        self.kept_first = jnp.where(early, kept_mine, kept_other)
        kept_second = jnp.where(early, kept_other, kept_mine)
        self.added = kept_second * self.first + second
        self.kept_both = self.kept_first * kept_second
        self.hops = self.count // 2 - 1
        self.entering = None

    def hop(self, number, earlier=None):
        send = self.added
        if self.entering is not None:
            send = self.kept_both * self.entering.astype(F32) + send
        send = send.astype(LOW)
        if earlier is not None:
            send = then(send, earlier)
        chip = self.hops - number if self.reverse else number
        route = [(2 * chip + c, 2 * (chip - 1 if self.reverse else chip + 1) + c) for c in (0, 1)]
        got = lax.ppermute(send, "fsdp", route)
        self.entering = got if self.entering is None else self.entering + got
        return got

    def end(self, earlier=None):
        entering = self.entering.astype(F32)
        entering_second = self.kept_first * entering + self.first
        keep = jnp.where(self.early, entering, entering_second).astype(LOW)
        send = jnp.where(self.early, entering_second, entering).astype(LOW)
        if earlier is not None:
            send = then(send, earlier)
        got = swap_cores(send)
        low, high = jnp.concatenate([keep, got], 2), jnp.concatenate([got, keep], 2)
        return jnp.where(self.core == 0, low, high)


def reduce_rows(parts, partial):
    count, replicas = lax.axis_size("fsdp"), lax.axis_size("dp")
    place, replica = lax.axis_index("fsdp"), lax.axis_index("dp")
    chips, chip, core = count // 2, place // 2, place % 2
    sizes = [p.shape[0] // (count * replicas) for p in parts]
    lanes = parts[0].shape[1]
    cut = [p.reshape(chips, 2, replicas, n, lanes) for p, n in zip(parts, sizes)]
    spare = -sum(sizes) % HALO
    if spare:
        cut.append(jnp.zeros((chips, 2, replicas, spare, lanes), F32))
    whole = jnp.concatenate(cut, axis=3)
    pick = lambda a, i, dim: lax.dynamic_index_in_dim(a, i, dim, False)
    total = pick(whole, core, 1) + swap_cores(pick(whole, 1 - core, 1))
    each = total.shape[2]
    partial = partial.reshape(replicas, -1, lanes)
    short = partial.shape[1]
    column = lambda r: jnp.concatenate([pick(total, r, 1).reshape(-1, lanes), pick(partial, r, 0)])
    mine = column(replica)
    for k in range(1, replicas):
        mine = mine + over_dp(column(replica ^ k).astype(LOW), k).astype(F32)
    mine, part_sum = mine[: chips * each].reshape(chips, each, lanes), mine[chips * each :]
    last = pick(mine, chip, 0)
    for k in range(1, chips):
        route = [(i, (i + 2 * k) % count) for i in range(count)]
        last = last + lax.ppermute(pick(mine, (chip + k) % chips, 0).astype(LOW), "fsdp", route).astype(F32)
    last = jnp.concatenate([last, part_sum])
    near = jnp.stack([last] + [over_dp(last, k) for k in range(1, replicas)])
    full = jnp.stack([pick(near, replica ^ a, 0) for a in range(replicas)])
    outs, start = [], 0
    for n in sizes:
        outs.append(full[:, start : start + n].reshape(replicas * n, lanes))
        start += n
    return *outs, full[:, each:].reshape(replicas * short, lanes)


def over_dp(value, bit):
    return lax.ppermute(value, "dp", [(i, i ^ bit) for i in range(lax.axis_size("dp"))])


def opposite(one, two):
    part = one.shape[1] // 2
    return jnp.concatenate([over_dp(one[:, :part], 2), over_dp(two[:, part:], 1)], axis=1)


def in_ring(every, token=0):
    count, place = every.shape[0], lax.axis_index("fsdp") + token
    take = lambda k, flip: lax.dynamic_index_in_dim(every, (place + 2 * k) % count ^ flip, 0, False)
    return [jnp.stack([take(k, flip) for k in ring_order(count // 2)]) for flip in (0, 1)]


def flat(chips):
    return chips.reshape(-1, chips.shape[2])


def share(near, mine, other):
    one, two = over_dp(mine[1:], 1), over_dp(mine[1:], 2)
    got = jnp.stack([flat(jnp.concatenate([a[None], b])) for a, b in zip(near[1:], (one, two, opposite(one, two)))])
    return (flat(mine), got), (flat(other), swap_cores(got))


def local(
    block_input, seq_lengths, adapter_ids, norm_gain, w_in, w_dt, conv_weight, conv_bias, dt_bias,
    head_rates, skip_gain, gate_gain, w_out, in_down, in_up, out_down, out_up, out_grad,
):
    streams, length, width = block_input.shape[1:]
    inner = gate_gain.shape[0]
    conv_cols = conv_weight.shape[1]
    heads = dt_bias.shape[0]
    headdim = inner // heads
    state_size = (conv_cols - inner) // 2
    adapters, ranks = in_down.shape[:2]
    in_cols = in_up.shape[2]
    slots = seq_lengths.shape[2]
    rows = streams * length
    groups = lax.axis_size("dp")
    per_group = heads // groups
    group_cols = inner // groups
    cfg = (streams, length, slots, groups, per_group, headdim)
    count = lax.axis_size("fsdp")
    first_pos = lax.axis_index("fsdp") * length
    ends = jnp.cumsum(seq_lengths[0], axis=-1, dtype=jnp.int32)
    place = lax.axis_index("fsdp")
    core, chip, chips = place % 2, place // 2, count // 2
    order = lax.axis_index("dp") ^ jnp.arange(groups, dtype=jnp.int32)
    meta = [order, first_pos[None], ends.reshape(-1), core[None], chip[None], adapter_ids.reshape(-1)]
    meta = jnp.concatenate(meta).astype(jnp.int32)
    ids_place = core_at(groups, streams, slots) + 2
    pad_heads = lambda a: jnp.pad(a, ((0, 0), (0, LANES - heads)))

    quarters = lambda a: [
        lax.dynamic_slice_in_dim(a, order[j] * group_cols, group_cols, 1) for j in range(groups)
    ]
    own_x, own_gate = quarters(w_in[:, inner : 2 * inner]), quarters(w_in[:, :inner])
    small = jnp.concatenate([w_in[:, 2 * inner :], pad_heads(w_dt)], axis=1)
    every = lax.all_gather(jnp.concatenate([own_x[0], small], axis=1), "fsdp")
    w_small = every[:, :, group_cols:].reshape(width, -1)
    every_gate = lax.all_gather(own_gate[0], "fsdp")
    out_cols = width // groups
    own_out = [lax.dynamic_slice_in_dim(w_out, order[j] * out_cols, out_cols, 1) for j in range(groups)]
    every_out = lax.all_gather(own_out[0], "fsdp")
    Order.waits = []
    devices = range(count)
    before = lax.ppermute(block_input[0, :, length - HALO :], "fsdp", [(i - 1, i) for i in devices if i > 0])
    down_in = in_down.reshape(adapters * ranks, width)
    up_in = in_up.reshape(adapters * ranks, in_cols)
    down_out = out_down.reshape(adapters * ranks, inner)
    up_out = out_up.reshape(adapters * ranks, width)
    x_rows, grad_rows = block_input.reshape(rows, width), out_grad.reshape(rows, width)
    normed_ext, nx_ext, hidden_ext, hidden_in, allowed, d_branch, d_hidden_out = prepare(
        cfg, meta, ids_place, ranks, x_rows, before.reshape(streams * HALO, width), norm_gain[None],
        down_in, grad_rows, up_out,
    )

    rates = pad_heads(head_rates[None])
    bias_row = conv_bias[None]
    (ci_bc, step, slope, taps, logs3, step2, enter2, rest2, weight2, log_t, through, g, gt, b_low, c_low, bt, ct) = decays(
        cfg, meta, normed_ext, hidden_ext, w_small, up_in, conv_weight, bias_row, pad_heads(dt_bias[None]), rates, heads
    )
    kept_mine = through[:, :1]
    kept_other = swap_cores(kept_mine)
    of_group = lambda a, j: lax.dynamic_slice_in_dim(a, order[j] * group_cols, group_cols, 2)

    w_x, ci, xs, ys, added = [], [], [], [], []

    def enter_group(j, weights):
        w_x.append(weights)
        ci_j, x_j, own = project(cfg, meta, j, nx_ext, hidden_ext, weights, up_in, conv_weight, bias_row, weight2, taps, bt)
        ci.append(ci_j)
        xs.append(x_j)
        added.append(own)

    def from_dp(j, far):
        mine = flat(jnp.concatenate([own_x[j][None], far]))
        return mine, swap_cores(mine)

    def scan_of(js):
        kept = [jnp.concatenate([of_group(a, j) for j in js], axis=2) for a in (kept_mine, kept_other)]
        return Scan(jnp.concatenate([added[j] for j in js], axis=2), *kept, False)

    pairs = lambda j: inside(cfg, meta, j, xs[j], step2, logs3, log_t, g)
    mine, other = in_ring(every[:, :, :group_cols])
    one, two = over_dp(mine[1:], 1), over_dp(mine[1:], 2)
    enter_group(0, (flat(mine), flat(other)))
    ys.append(pairs(0))
    weights_one, weights_two = from_dp(1, one), from_dp(2, two)
    enter_group(1, weights_one)
    gate_token = Order.token
    enter_group(2, weights_two)
    scans = [scan_of((0, 1))]
    scans[0].hop(0)
    last = opposite(one, two)
    enter_group(3, from_dp(3, last))
    w_gate = share(own_gate, *in_ring(every_gate, gate_token))
    scans.append(scan_of((2, 3)))
    scans[1].hop(0)
    scans[0].hop(1)
    ys.append(pairs(1))
    ys.append(pairs(2))
    w_o = share(own_out, *in_ring(every_out, Order.token))
    ys.append(pairs(3))
    scans[1].hop(1)
    for hop in range(2, chips - 1):
        scans[0].hop(hop)
        scans[1].hop(hop)
    gate = gate_project(cfg, meta, nx_ext, hidden_ext, w_gate, up_in)
    pair_states = [scan.end() for scan in scans]
    states = [pair_states[j // 2][:, :, (j % 2) * group_cols : (j % 2 + 1) * group_cols] for j in range(groups)]
    d_pieces = out_back(cfg, meta, d_branch, w_o)

    skip_row = jnp.repeat(skip_gain, headdim)[None]
    out_low, d_mixed, d_gate, row_sum, d_state = gated(
        cfg, meta, xs, ys, states, gate, d_pieces, d_hidden_out, down_out, enter2, c_low, ct, skip_row, gate_gain[None]
    )
    pieces = 2
    wide_cols = inner // pieces
    part = lambda a, j: a[:, :, j * wide_cols : (j + 1) * wide_cols]
    scans = [Scan(part(d_state, j), part(kept_mine, j), part(kept_other, j), True) for j in range(pieces)]
    arrived = [[scan.hop(0) for scan in scans]]

    wait_for(*[scan.other for scan in scans])

    block_output, g_out_down, g_out_up = out_project(
        cfg, meta, out_low, d_branch, x_rows, allowed, down_out, up_out, d_hidden_out, w_o
    )
    wait_for(*arrived[0])
    early = back_project(cfg, meta, d_gate, w_gate, hidden_in, up_in, 0)
    for hop in range(1, chips - 1):
        arrived.append([scan.hop(hop) for scan in scans])
    half_groups = groups // 2
    inside_parts = []
    for p in (0, 1):
        wait_for(*arrived[p + 1])
        js = slice(p * half_groups, (p + 1) * half_groups)
        inside_parts.append(
            inside_back(cfg, meta, p * half_groups, xs[js], d_mixed, step2, logs3, enter2, log_t, gt, states[js])
        )
    dxs, dgts, dcs = zip(*inside_parts)
    d_after = jnp.concatenate([scan.end() for scan in scans], axis=2)
    by_device = lambda a: a.reshape(count, a.shape[0] // count, a.shape[1])
    out_sums = jnp.concatenate([by_device(g_out_down), by_device(g_out_up)], axis=1)
    out_sums = lax.psum_scatter(then(out_sums, dxs[1]), "fsdp", scatter_dimension=0, tiled=False)
    dci, tail, spill, direct, sums, db = after(
        cfg, meta, xs, states, ci, dxs, d_mixed, d_after, step, step2, rest2, taps, b_low, skip_row, conv_weight, bias_row
    )
    to_earlier = lambda a: lax.ppermute(a, "fsdp", [(i, i - 1) for i in devices if i > 0])
    spill = to_earlier(spill)
    d_raw, dci_bc, tail_bc, spill_bc = finish(
        cfg, meta, dgts, dcs, db, direct, sums, row_sum, step, slope, taps, through, rates, b_low, c_low,
        ci_bc, conv_weight, bias_row, inner // BLOCK,
    )
    spill_bc = to_earlier(spill_bc)
    late = back_project(
        cfg, meta, dci, w_x, hidden_in, up_in, inner // WIDE, (tail, spill, early[0], early[1])
    )
    input_grad, g_bc, g_in_down = close(
        streams, meta, late[0], late[1], dci_bc, tail_bc, spill_bc, w_small, d_raw, up_in, allowed, down_in, hidden_in,
        normed_ext, x_rows, norm_gain[None], grad_rows,
    )
    in_down_sum, in_up_sum, out_sums = reduce_rows(
        [g_in_down, jnp.concatenate([early[2], late[2], g_bc], axis=0)], out_sums
    )
    out_sums = jnp.split(out_sums, [inner // count], axis=0)
    totals = [a.T.reshape(adapters, ranks, -1) for a in (in_down_sum, in_up_sum, *out_sums)]
    return (block_output.reshape(1, streams, length, width), input_grad.reshape(1, streams, length, width), *totals)


def solution(mesh):
    rows = P("dp", None, "fsdp", None)
    cut = P("fsdp", None)
    per_group = P("dp", None, None)
    in_specs = (
        rows, per_group, per_group, P(), cut, cut, P(), P(), P(), P(), P(), P(), cut, P(), P(), P(), P(), rows,
    )
    out_specs = (rows, rows) + (P(None, None, "fsdp"),) * 4
    return jax.shard_map(local, mesh=mesh, in_specs=in_specs, out_specs=out_specs, check_vma=False)
```

```python
import functools

import jax
import jax.numpy as jnp
from jax import lax
from jax.experimental import pallas as pl
from jax.experimental.pallas import tpu as pltpu
from jax.sharding import PartitionSpec as P

EPSILON = 1e-05
HIGHEST = lax.Precision.HIGHEST
F32, LOW = jnp.float32, jnp.bfloat16
HALO = 16
LANES = 128
BLOCK = 256
WIDE = 768
VMEM = 20 * 1024 * 1024


def lasting(us):
    return pl.CostEstimate(flops=int(us * 1.15e9), bytes_accessed=1000000, transcendentals=0)


class Order:
    waits = []
    token = None


def in_order(kernel, *, grid_spec, out_shape, compiler_params, cost_estimate, name):
    def call(meta, *args):
        waits = Order.waits
        skip = len(waits)
        specs = [pl.BlockSpec(memory_space=pl.ANY)] * skip + list(grid_spec["in_specs"])
        single = not isinstance(out_shape, (list, tuple))
        shapes = [out_shape] if single else list(out_shape)
        out_specs = [grid_spec["out_specs"]] if single else list(grid_spec["out_specs"])
        token_at = skip + len(args) + len(shapes)

        def body(meta_ref, *refs):
            refs[token_at][...] = jnp.zeros((8, LANES), jnp.int32)
            kernel(meta_ref, *refs[skip:token_at], *refs[token_at + 1 :])

        outs = pl.pallas_call(
            body,
            grid_spec=pltpu.PrefetchScalarGridSpec(
                num_scalar_prefetch=1,
                grid=grid_spec["grid"],
                in_specs=specs,
                out_specs=out_specs + [pl.BlockSpec((8, LANES), lambda i, m: (0, 0))],
                scratch_shapes=grid_spec.get("scratch_shapes", ()),
            ),
            out_shape=shapes + [jax.ShapeDtypeStruct((8, LANES), jnp.int32)],
            compiler_params=compiler_params,
            cost_estimate=cost_estimate,
            name=name,
        )(meta, *waits, *args)
        Order.waits = [outs[-1]]
        Order.token = outs[-1][0, 0]
        return outs[0] if single else outs[:-1]

    return call


def wait_for(*arrays):
    Order.waits = Order.waits + list(arrays)


def dot(a, b, precision=None):
    return lax.dot_general(
        a, b, (((1,), (0,)), ((), ())), precision=precision, preferred_element_type=F32
    )


def dot_nt(a, b, precision=None):
    return lax.dot_general(
        a, b, (((1,), (1,)), ((), ())), precision=precision, preferred_element_type=F32
    )


def iota(shape, dim):
    return lax.broadcasted_iota(jnp.int32, shape, dim)


def packed(values, heads, terms):
    lane = iota(values.shape, 1)
    total, rest, wrapped = None, values, None
    for term in range(terms):
        part = rest.astype(LOW).astype(F32)
        rest = rest - part
        if term == 0:
            total = part
        elif (term + 1) * heads <= LANES:
            total = total + pltpu.roll(part, term * heads, 1)
        else:
            moved = pltpu.roll(part, term * heads, 1)
            total = total + jnp.where(lane >= term * heads, moved, 0.0)
            wrapped = jnp.where(lane < term * heads, moved, 0.0)
    if wrapped is not None:
        total = jnp.concatenate([total, wrapped], axis=1)
    return total.astype(LOW)


def expand(values, spread):
    return dot(values, spread)


def sigmoid(v):
    return 0.5 + 0.5 * jnp.tanh(0.5 * v)


def core_at(groups, streams, slots):
    return groups + 1 + streams * slots


def ring_order(chips):
    order = [0]
    for k in range(1, chips // 2 + 1):
        order += [k, chips - k] if k != chips - k else [k]
    return order


def placed(arrays, limit=1 << 20):
    return [
        pltpu.with_memory_space_constraint(a, pltpu.HBM) if a.size * a.dtype.itemsize > limit else a for a in arrays
    ]


class Meta:
    def __init__(self, ref, groups, slots):
        self.ref, self.groups, self.slots = ref, groups, slots

    def first(self):
        return self.ref[self.groups]

    def end(self, stream, slot):
        return self.ref[self.groups + 1 + stream * self.slots + slot]

    def segment(self, stream, pos):
        seg = jnp.zeros_like(pos)
        for slot in range(self.slots):
            seg = seg + (pos >= self.end(stream, slot)).astype(jnp.int32)
        return jnp.where(pos < 0, -1, seg)

    def scalar_segment(self, stream, pos):
        seg = jnp.int32(0)
        for slot in range(self.slots):
            seg = seg + jnp.where(pos >= self.end(stream, slot), 1, 0)
        return jnp.where(pos < 0, -1, seg)


def tap_masks(columns, taps):
    return [jnp.broadcast_to(columns[:, k : k + 1], columns.shape) for k in range(taps - 1)]


def wide(mask, cols):
    return jnp.concatenate([mask] * (cols // LANES), axis=1)


def conv_pre(block, masks, cw, cb):
    taps, cols = cw.shape
    total = cb + cw[taps - 1 : taps] * block[HALO:]
    for k in range(taps - 1):
        moved = pltpu.roll(block, taps - 1 - k, 0)[HALO:]
        total = total + cw[k : k + 1] * moved * wide(masks[k], cols)
    return total


def conv_back(d_out, block, masks, cw, cb):
    taps, cols = cw.shape
    pre = conv_pre(block, masks, cw, cb)
    sig = sigmoid(pre)
    d_pre = d_out * (sig * (1.0 + pre * (1.0 - sig)))
    total = jnp.concatenate([jnp.zeros((HALO, cols), F32), cw[taps - 1 : taps] * d_pre], axis=0)
    rows = total.shape[0]
    for k in range(taps - 1):
        part = cw[k : k + 1] * d_pre * wide(masks[k], cols)
        part = jnp.concatenate([jnp.zeros((HALO, cols), F32), part], axis=0)
        total = total + pltpu.roll(part, rows - (taps - 1 - k), 0)
    return total


def spread_of(first_head, cols, per_head, heads, terms=2):
    shape = (LANES * (1 if terms * heads <= LANES else 2), cols)
    head = lax.shift_right_logical(iota(shape, 1), per_head.bit_length() - 1) + first_head
    row = iota(shape, 0)
    hit = row == head
    for term in range(1, terms):
        hit = hit | (row == head + term * heads)
    return hit.astype(LOW)


def gather_of(first_head, cols, per_head):
    head = lax.shift_right_logical(iota((cols, LANES), 0), per_head.bit_length() - 1) + first_head
    return (iota((cols, LANES), 1) == head).astype(LOW)


def sum_heads(values, gather):
    part = values.astype(LOW)
    rest = (values - part.astype(F32)).astype(LOW)
    return dot(part, gather) + dot(rest, gather)


def halves_product(nx, hx, w_mine, w_other, up):
    return (dot(nx[0], w_mine) + dot(nx[1], w_other) + dot(hx[...], up[...])).astype(LOW)


def quarter_specs(half, blocks):
    far = lambda i: jnp.maximum(i - blocks, 0)
    return [
        pl.BlockSpec((half, WIDE), lambda i, m: (0, jnp.minimum(i, blocks - 1))),
        pl.BlockSpec((1, half, WIDE), lambda i, m: (lax.div(far(i), blocks), 0, lax.rem(far(i), blocks))),
    ]


def gate_project_kernel(cfg, blocks, meta_ref, nx, hx, w_mine, w_mine_far, w_other, w_other_far, up, out):
    streams, length, slots, groups, per_group, headdim = cfg
    near = pl.program_id(0) < blocks
    w_mine = jnp.where(near, w_mine[...], w_mine_far[0])
    w_other = jnp.where(near, w_other[...], w_other_far[0])
    full = halves_product(nx, hx, w_mine, w_other, up)
    for s in range(streams):
        out[s * length : (s + 1) * length] = full[s * (HALO + length) + HALO : (s + 1) * (HALO + length)]


def gate_project(cfg, meta, nx, hx, weights, in_up):
    streams, length, slots, groups, per_group, headdim = cfg
    half, cols = weights[0][0].shape
    rows = streams * length
    blocks = cols // WIDE
    at = lambda i, m: m[lax.div(i, blocks)] * blocks + lax.rem(i, blocks)
    return in_order(
        functools.partial(gate_project_kernel, cfg, blocks),
        grid_spec=dict(
            grid=(groups * blocks,),
            in_specs=[
                pl.BlockSpec(nx.shape, lambda i, m: (0, 0, 0)),
                pl.BlockSpec(hx.shape, lambda i, m: (0, 0)),
                *quarter_specs(half, blocks) * 2,
                pl.BlockSpec((in_up.shape[0], WIDE), lambda i, m: (0, at(i, m))),
            ],
            out_specs=pl.BlockSpec((rows, WIDE), lambda i, m: (0, at(i, m))),
        ),
        out_shape=jax.ShapeDtypeStruct((rows, groups * cols), LOW),
        compiler_params=pltpu.CompilerParams(vmem_limit_bytes=2 * VMEM),
        cost_estimate=lasting(9),
        name="project_gate",
    )(meta, *placed([nx, hx, *weights[0], *weights[1], in_up]))


def project_kernel(cfg, slot, meta_ref, nx, hx, w_mine, w_other, up, cw, cb, weight, taps, bt, ci, x_out, state):
    streams, length, slots, groups, per_group, headdim = cfg
    per_block = BLOCK // headdim
    first_head = meta_ref[slot] * per_group + pl.program_id(0) * per_block
    spread = spread_of(first_head, BLOCK, headdim, groups * per_group)
    low = halves_product(nx, hx, w_mine[...], w_other[...], up)
    ci[...] = low
    full = low.astype(F32)
    for s in range(streams):
        block = full[s * (HALO + length) : (s + 1) * (HALO + length)]
        masks = tap_masks(taps[s * length : (s + 1) * length], cw.shape[0])
        pre = conv_pre(block, masks, cw[...], cb[...])
        x = pre * sigmoid(pre)
        x_out[s * length : (s + 1) * length] = x
        scale = expand(weight[s * length : (s + 1) * length], spread)
        state[s] = dot(bt[s], (x * scale).astype(LOW)).astype(LOW)


def project(cfg, meta, slot, nx, hx, weights, in_up, conv_weight, conv_bias, weight, taps, bt):
    streams, length, slots, groups, per_group, headdim = cfg
    rows = streams * length
    ext = hx.shape[0]
    half, cols = weights[0].shape
    blocks = cols // BLOCK
    gate_blocks = (in_up.shape[1] - conv_weight.shape[1]) // BLOCK
    place = lambda i, m: m[slot] * blocks + i
    whole = lambda i, m: (0, 0)
    cube = lambda i, m: (0, 0, 0)
    own = lambda i, m: (0, i)
    conv_at = lambda i, m: (0, place(i, m))
    return in_order(
        functools.partial(project_kernel, cfg, slot),
        grid_spec=dict(
            grid=(blocks,),
            in_specs=[
                pl.BlockSpec(nx.shape, cube),
                pl.BlockSpec(hx.shape, whole),
                pl.BlockSpec((half, BLOCK), own),
                pl.BlockSpec((half, BLOCK), own),
                pl.BlockSpec((in_up.shape[0], BLOCK), lambda i, m: (0, gate_blocks + place(i, m))),
                pl.BlockSpec((conv_weight.shape[0], BLOCK), conv_at),
                pl.BlockSpec((1, BLOCK), conv_at),
                pl.BlockSpec(weight.shape, whole),
                pl.BlockSpec(taps.shape, whole),
                pl.BlockSpec(bt.shape, cube),
            ],
            out_specs=[
                pl.BlockSpec((ext, BLOCK), own),
                pl.BlockSpec((rows, BLOCK), own),
                pl.BlockSpec((streams, bt.shape[1], BLOCK), lambda i, m: (0, 0, i)),
            ],
        ),
        out_shape=[
            jax.ShapeDtypeStruct((ext, cols), LOW),
            jax.ShapeDtypeStruct((rows, cols), F32),
            jax.ShapeDtypeStruct((streams, bt.shape[1], cols), LOW),
        ],
        compiler_params=pltpu.CompilerParams(vmem_limit_bytes=VMEM),
        cost_estimate=lasting(8),
        name="project_conv",
    )(meta, *placed([nx, hx, *weights, in_up, conv_weight, conv_bias, weight, taps, bt]))


def prepare_kernel(cfg, ids_place, adapter_cols, chips, meta_ref, x, before, gain, down, grad, up, normed, nx, hidden_ext, hidden, allowed, d_branch, d_hidden, pieces):
    streams, length, slots, groups, per_group, headdim = cfg
    meta = Meta(meta_ref, groups, slots)
    core = meta_ref[core_at(groups, streams, slots)]
    chip = meta_ref[core_at(groups, streams, slots) + 1]
    s = pl.program_id(0)
    rows = length + HALO
    seg = meta.segment(s, meta.first() - HALO + iota((rows, LANES), 0))
    kind = lax.shift_right_logical(iota((rows, LANES), 1), adapter_cols.bit_length() - 1)
    mask = jnp.zeros((rows, LANES), F32)
    for slot in range(slots):
        mask = jnp.where((seg == slot) & (kind == meta_ref[ids_place + s * slots + slot]), 1.0, mask)
    full = jnp.concatenate([before[...], x[...]], axis=0).astype(F32)
    rs = lax.rsqrt(jnp.mean(full * full, axis=-1, keepdims=True) + EPSILON)
    low = (full * rs * gain[...]).astype(LOW)
    normed[...] = low
    size = pieces.shape[2]
    for p in range(2 * chips):
        pieces[p] = low[:, p * size : (p + 1) * size]
    for k, distance in enumerate(ring_order(chips)):
        at = 2 * lax.rem(chip + distance, chips)
        nx[0, :, k * size : (k + 1) * size] = pieces[at + core]
        nx[1, :, k * size : (k + 1) * size] = pieces[at + 1 - core]
    got = (dot_nt(low, down[...]) * mask).astype(LOW)
    hidden_ext[...] = got
    hidden[...] = got[HALO:]
    allowed[...] = mask[HALO:]
    valid = (seg[HALO:] < slots).astype(F32)
    rows_out = (grad[...].astype(F32) * wide(valid, grad.shape[1])).astype(LOW)
    d_branch[...] = rows_out
    d_hidden[...] = (dot_nt(rows_out, up[...]) * mask[HALO:]).astype(LOW)


def prepare(cfg, meta, ids_place, adapter_cols, x, before, gain, down, grad, up):
    streams, length, slots, groups, per_group, headdim = cfg
    rows, width = x.shape
    chips = lax.axis_size("fsdp") // 2
    ext = streams * (length + HALO)
    ranks = down.shape[0]
    block = lambda r, c: pl.BlockSpec((r, c), lambda i, m: (i, 0))
    whole = lambda a: pl.BlockSpec(a.shape, lambda i, m: (0, 0))
    return in_order(
        functools.partial(prepare_kernel, cfg, ids_place, adapter_cols, chips),
        grid_spec=dict(
            grid=(streams,),
            in_specs=[
                block(length, width), block(HALO, width), whole(gain), whole(down), block(length, width), whole(up),
            ],
            out_specs=[
                block(length + HALO, width),
                pl.BlockSpec((2, length + HALO, width // 2), lambda i, m: (0, i, 0)),
                block(length + HALO, ranks), block(length, ranks), block(length, ranks),
                block(length, width), block(length, ranks),
            ],
            scratch_shapes=[pltpu.VMEM((2 * chips, length + HALO, width // (2 * chips)), LOW)],
        ),
        out_shape=[
            jax.ShapeDtypeStruct((ext, width), LOW),
            jax.ShapeDtypeStruct((2, ext, width // 2), LOW),
            jax.ShapeDtypeStruct((ext, ranks), LOW),
            jax.ShapeDtypeStruct((rows, ranks), LOW),
            jax.ShapeDtypeStruct((rows, ranks), F32),
            jax.ShapeDtypeStruct((rows, width), LOW),
            jax.ShapeDtypeStruct((rows, ranks), LOW),
        ],
        compiler_params=pltpu.CompilerParams(vmem_limit_bytes=VMEM),
        cost_estimate=lasting(3),
        name="prepare",
    )(meta, x, before, gain, down, grad, up)


def decay_kernel(cfg, heads, meta_ref, normed, hidden, w, up, cw, cb, dt_bias, rates, ci, step, slope, taps, logs3, step2, enter2, rest2, weight2, log_t, through, g, gt, b_low, c_low, bt, ct):
    streams, length, slots, groups, per_group, headdim = cfg
    meta = Meta(meta_ref, groups, slots)
    first = meta.first()
    lower = (iota((length, length), 0) >= iota((length, length), 1)).astype(F32)
    per_block = BLOCK // headdim
    state_size = c_low.shape[1]
    bc_cols = 2 * state_size
    both = dot(normed[...], w[...])
    low = (both[:, :bc_cols] + dot(hidden[...], up[...])).astype(LOW)
    ci[...] = low
    for s in range(streams):
        at = slice(s * length, (s + 1) * length)
        ext = slice(s * (HALO + length), (s + 1) * (HALO + length))
        pos = first + iota((length, LANES), 0)
        seg = meta.segment(s, pos)
        lane = iota((length, LANES), 1)
        columns = jnp.zeros((length, LANES), F32)
        for k in range(cw.shape[0] - 1):
            same = meta.segment(s, pos - (cw.shape[0] - 1 - k)) == seg
            columns = jnp.where((lane == k) & same, 1.0, columns)
        taps[at] = columns
        pre = conv_pre(low[ext].astype(F32), tap_masks(columns, cw.shape[0]), cw[...], cb[...])
        bc = pre * sigmoid(pre)
        b_in, c_in = bc[:, :state_size], bc[:, state_size:]
        dt_in = both[ext][HALO:, bc_cols:] + dt_bias[...]
        real = iota((length, LANES), 1) < heads
        st = jnp.where(real, jnp.maximum(dt_in, 0.0) + jnp.log1p(jnp.exp(-jnp.abs(dt_in))), 0.0)
        step[at] = st
        slope[at] = jnp.where(real, sigmoid(dt_in), 0.0)
        prior = meta.scalar_segment(s, first - 1)
        last = meta.scalar_segment(s, first + length - 1)
        seg_u = meta.segment(s, first + iota((length, length), 1))
        seg_t = meta.segment(s, first + iota((length, length), 0))
        logs = dot(lower, -st * rates[...], HIGHEST)
        logs3[at] = packed(logs, heads, 3)
        step2[at] = packed(st, heads, 2)
        enter2[at] = packed(jnp.where(real & (seg == prior), jnp.exp(logs), 0.0), heads, 2)
        remain = jnp.where(real & (seg == last), jnp.exp(logs[length - 1 : length] - logs), 0.0)
        rest2[at] = packed(remain, heads, 2)
        weight2[at] = packed(remain * st, heads, 2)
        kept = jnp.where(prior == last, jnp.exp(logs[length - 1 : length]), 0.0)
        kept = jnp.where(real[:8], jnp.broadcast_to(kept, (8, LANES)), 0.0)
        through[s] = expand(packed(kept, heads, 3), spread_of(0, through.shape[2], headdim, heads, 3))
        turned_logs = jnp.transpose(logs)
        for b in range(log_t.shape[1]):
            log_t[s, b, 0:per_block] = turned_logs[b * per_block : (b + 1) * per_block]
        pairs = jnp.where(seg_u == seg_t, lower, 0.0) * dot_nt(c_in, b_in, HIGHEST)
        g[s] = pairs
        gt[s] = jnp.transpose(pairs)
        b_low[at] = b_in.astype(LOW)
        c_low[at] = c_in.astype(LOW)
        bt[s] = jnp.transpose(b_in).astype(LOW)
        ct[s] = jnp.transpose(c_in).astype(LOW)


def decays(cfg, meta, normed, hidden, w, in_up, conv_weight, conv_bias, dt_bias, rates, heads):
    streams, length, slots, groups, per_group, headdim = cfg
    rows = streams * length
    blocks = heads * headdim // BLOCK
    state_size = (w.shape[1] - LANES) // 2
    row = lambda dtype, cols: jax.ShapeDtypeStruct((rows, cols), dtype)
    cube = lambda dtype, a, b: jax.ShapeDtypeStruct((streams, a, b), dtype)
    outs = [
        jax.ShapeDtypeStruct((hidden.shape[0], 2 * state_size), LOW),
        *[row(F32, LANES)] * 3, row(LOW, 2 * LANES), *[row(LOW, LANES)] * 4,
        jax.ShapeDtypeStruct((streams, blocks, 8, length), F32),
        cube(F32, 8, heads * headdim),
        cube(F32, length, length), cube(F32, length, length),
        row(LOW, state_size), row(LOW, state_size),
        cube(LOW, state_size, length), cube(LOW, state_size, length),
    ]
    zeros = lambda n: (lambda i, m: (0,) * n)
    whole = lambda a: pl.BlockSpec(a.shape, zeros(len(a.shape)))
    last = lambda a: pl.BlockSpec((a.shape[0], BLOCK), lambda i, m: (0, a.shape[1] // BLOCK - 1))
    return in_order(
        functools.partial(decay_kernel, cfg, heads),
        grid_spec=dict(
            grid=(1,),
            in_specs=[
                whole(normed), whole(hidden), whole(w), last(in_up), last(conv_weight), last(conv_bias),
                whole(dt_bias), whole(rates),
            ],
            out_specs=[whole(a) for a in outs],
        ),
        out_shape=outs,
        compiler_params=pltpu.CompilerParams(vmem_limit_bytes=VMEM),
        cost_estimate=lasting(4),
        name="decays",
    )(meta, normed, hidden, w, in_up, conv_weight, conv_bias, dt_bias, rates)


def inside_kernel(cfg, slot, meta_ref, x, step2, logs3, log_t, g, y):
    streams, length, slots, groups, per_group, headdim = cfg
    heads = groups * per_group
    per_block = BLOCK // headdim
    first_head = meta_ref[slot] * per_group + pl.program_id(0) * per_block
    spread = spread_of(first_head, BLOCK, headdim, heads)
    columns = spread_of(first_head, per_block * LANES, LANES, heads, 3)
    half = length // 2
    left = iota((half, LANES), 1) < headdim
    for s in range(streams):
        at = slice(s * length, (s + 1) * length)
        log_col = expand(logs3[at], columns)
        xs = (x[at] * expand(step2[at], spread)).astype(LOW)
        for pair in range(per_block // 2):
            cols = slice(pair * LANES, (pair + 1) * LANES)
            tops, lows = [], []
            for h in (2 * pair, 2 * pair + 1):
                col = log_col[:, h * LANES : (h + 1) * LANES]
                row = log_t[s, 0, h : h + 1]
                tops.append((jnp.exp(jnp.minimum(col[:half] - row[:, :half], 0.0)) * g[s, :half, :half]).astype(LOW))
                lows.append(
                    (jnp.exp(jnp.minimum(wide(col[half:], length) - row, 0.0)) * g[s, half:]).astype(LOW)
                )
            top = dot(jnp.concatenate(tops, axis=0), xs[:half, cols])
            low = dot(jnp.concatenate(lows, axis=0), xs[:, cols])
            start = s * length
            y[start : start + half, cols] = jnp.where(left, top[:half], top[half:])
            y[start + half : start + length, cols] = jnp.where(left, low[:half], low[half:])


def inside(cfg, meta, slot, x, step2, logs3, log_t, g):
    streams, length, slots, groups, per_group, headdim = cfg
    blocks = x.shape[1] // BLOCK
    whole = lambda i, m: (0, 0)
    own = pl.BlockSpec((x.shape[0], BLOCK), lambda i, m: (0, i))
    return in_order(
        functools.partial(inside_kernel, cfg, slot),
        grid_spec=dict(
            grid=(blocks,),
            in_specs=[
                own,
                pl.BlockSpec(step2.shape, whole),
                pl.BlockSpec(logs3.shape, whole),
                pl.BlockSpec((streams, 1, 8, length), lambda i, m: (0, m[slot] * blocks + i, 0, 0)),
                pl.BlockSpec(g.shape, lambda i, m: (0, 0, 0)),
            ],
            out_specs=own,
        ),
        out_shape=jax.ShapeDtypeStruct(x.shape, F32),
        compiler_params=pltpu.CompilerParams(vmem_limit_bytes=VMEM),
        cost_estimate=lasting(5),
        name="inside",
    )(meta, x, step2, logs3, log_t, g)


def gate_kernel(cfg, meta_ref, *refs):
    streams, length, slots, groups, per_group, headdim = cfg
    xs, ys, states = (refs[i * groups : (i + 1) * groups] for i in range(3))
    refs = refs[3 * groups :]
    gate, d_pieces, d_hidden, down, enter2, c_low, ct, skip, gain = refs[:9]
    out_low, d_mixed, d_gate, row_sum, d_state, y_all, v_all, held, d_out, scales = refs[9:]
    width = per_group * headdim
    inner = groups * width
    rows = gate.shape[0]
    per_stream = length // rows
    entering = enter2[...]
    heads = groups * per_group
    squares = jnp.zeros((rows, LANES), F32)
    crossed = jnp.zeros((rows, LANES), F32)
    d_out[...] = jnp.concatenate([d_pieces[p] for p in range(d_pieces.shape[0])], axis=1)

    def fold(values):
        total = values[:, :LANES]
        for j in range(1, values.shape[1] // LANES):
            total = total + values[:, j * LANES : (j + 1) * LANES]
        return total

    for j in range(groups):
        place = meta_ref[j]
        cols = pl.ds(pl.multiple_of(place * width, width), width)
        scale = expand(entering, spread_of(place * per_group, width, headdim, heads))
        scales[:, cols] = scale
        y = ys[j][...] + dot(c_low[...], states[j][0]) * scale
        y_all[:, cols] = y
        gated = gate[:, cols].astype(F32)
        v = (y + skip[:, cols] * xs[j][...]) * (gated * sigmoid(gated))
        v_all[:, cols] = v
        wanted = (d_out[:, cols] + dot(d_hidden[...], down[:, cols])) * gain[:, cols]
        d_out[:, cols] = wanted
        squares = squares + fold(v * v)
        crossed = crossed + fold(v * wanted)
    mean_sq = jnp.sum(squares, axis=1, keepdims=True) / inner
    rs = lax.rsqrt(mean_sq + EPSILON)
    mean_cross = jnp.sum(crossed, axis=1, keepdims=True) / inner
    pull = rs * rs * rs * mean_cross
    sums = jnp.zeros((rows, LANES), F32)
    fresh = pl.program_id(0) % per_stream == 0
    for j in range(groups):
        place = meta_ref[j]
        cols = pl.ds(pl.multiple_of(place * width, width), width)
        gated = gate[:, cols].astype(F32)
        sig = sigmoid(gated)
        v = v_all[:, cols]
        y = y_all[:, cols]
        out_low[:, cols] = (v * rs * gain[:, cols]).astype(LOW)
        d_v = rs * d_out[:, cols] - v * pull
        dm = d_v * (gated * sig)
        d_mixed[:, cols] = dm
        mixed = y + skip[:, cols] * xs[j][...]
        d_gate[:, cols] = (d_v * mixed * (sig * (1.0 + gated * (1.0 - sig)))).astype(LOW)
        sums = sums + sum_heads(
            dm.astype(LOW).astype(F32) * y, gather_of(place * per_group, width, headdim)
        )
        part = dot(ct[0], (dm * scales[:, cols]).astype(LOW))
        before = jnp.where(fresh, 0.0, held[:, cols])
        held[:, cols] = before + part
        d_state[0, :, cols] = (before + part).astype(LOW)
    row_sum[...] = sums


def gated(cfg, meta, xs, ys, states, gate, d_pieces, d_hidden, down, enter_d, c_low, ct, skip, gain):
    streams, length, slots, groups, per_group, headdim = cfg
    rows = 128
    per_stream = length // rows
    width = xs[0].shape[1]
    inner = gate.shape[1]
    state_size = c_low.shape[1]
    total = streams * length
    row = lambda cols: pl.BlockSpec((rows, cols), lambda i, m: (i, 0))
    state = pl.BlockSpec((1, state_size, width), lambda i, m: (i // per_stream, 0, 0))
    flat = pl.BlockSpec((1, inner), lambda i, m: (0, 0))
    return in_order(
        functools.partial(gate_kernel, cfg),
        grid_spec=dict(
            grid=(total // rows,),
            in_specs=[row(width)] * (2 * groups) + [state] * groups
            + [
                row(inner), pl.BlockSpec((d_pieces.shape[0], rows, d_pieces.shape[2]), lambda i, m: (0, i, 0)),
                row(d_hidden.shape[1]), pl.BlockSpec(down.shape, lambda i, m: (0, 0)), row(LANES), row(state_size),
                pl.BlockSpec((1, state_size, rows), lambda i, m: (i // per_stream, 0, i % per_stream)),
                flat, flat,
            ],
            out_specs=[
                row(inner), row(inner), row(inner), row(LANES),
                pl.BlockSpec((1, state_size, inner), lambda i, m: (i // per_stream, 0, 0)),
            ],
            scratch_shapes=[
                pltpu.VMEM((rows, inner), F32), pltpu.VMEM((rows, inner), F32), pltpu.VMEM((state_size, inner), F32),
                pltpu.VMEM((rows, inner), F32), pltpu.VMEM((rows, inner), F32),
            ],
        ),
        out_shape=[
            jax.ShapeDtypeStruct((total, inner), LOW),
            jax.ShapeDtypeStruct((total, inner), F32),
            jax.ShapeDtypeStruct((total, inner), LOW),
            jax.ShapeDtypeStruct((total, LANES), F32),
            jax.ShapeDtypeStruct((streams, state_size, inner), LOW),
        ],
        compiler_params=pltpu.CompilerParams(vmem_limit_bytes=2 * VMEM),
        cost_estimate=lasting(19),
        name="gated",
    )(meta, *placed([*xs, *ys, *states, gate, d_pieces, d_hidden, down, enter_d, c_low, ct, skip, gain]))


def pick(refs, which):
    value = refs[0][...]
    for j in range(1, len(refs)):
        value = jnp.where(which == j, refs[j][...], value)
    return value


def inside_back_kernel(cfg, slot, count, blocks, meta_ref, *refs):
    streams, length, slots, groups, per_group, headdim = cfg
    xs, states = refs[:count], refs[count : 2 * count]
    d_mixed, step2, logs3, enter2, log_t, gt, dxs, dgt, dc = refs[2 * count :]
    heads = groups * per_group
    per_block = BLOCK // headdim
    which = lax.div(pl.program_id(0), blocks)
    first_head = meta_ref[slot + which] * per_group + lax.rem(pl.program_id(0), blocks) * per_block
    spread = spread_of(first_head, BLOCK, headdim, heads)
    columns = spread_of(first_head, per_block * LANES, LANES, heads, 3)
    half = length // 2
    left = iota((half, LANES), 1) < headdim
    x_all, state = pick(xs, which), pick(states, which)

    @pl.when(pl.program_id(0) == 0)
    def _():
        dgt[...] = jnp.zeros_like(dgt)
        dc[...] = jnp.zeros_like(dc)

    for s in range(streams):
        start = s * length
        at = slice(start, start + length)
        log_col = expand(logs3[at], columns)
        x = (x_all[at] * expand(step2[at], spread)).astype(LOW)
        dm = d_mixed[at]
        dm_low = dm.astype(LOW)
        dc[at] += dot_nt((dm * expand(enter2[at], spread)).astype(LOW), state[s])
        sum_top, sum_low = None, None
        for pair in range(per_block // 2):
            cols = slice(pair * LANES, (pair + 1) * LANES)
            decay_top, decay_low, k_top, k_low, x_top, x_low = [], [], [], [], [], []
            for h in (2 * pair, 2 * pair + 1):
                col = log_col[:, h * LANES : (h + 1) * LANES]
                row = log_t[s, 0, h : h + 1]
                top = jnp.exp(jnp.minimum(row - wide(col[:half], length), 0.0))
                low = jnp.exp(jnp.minimum(row[:, half:] - col[half:], 0.0))
                decay_top.append(top)
                decay_low.append(low)
                k_top.append((top * gt[s, :half]).astype(LOW))
                k_low.append((low * gt[s, half:, half:]).astype(LOW))
                mine = left if h % 2 == 0 else jnp.logical_not(left)
                zero = jnp.zeros((half, LANES), LOW)
                x_top.append(jnp.where(mine, x[:half, cols], zero))
                x_low.append(jnp.where(mine, x[half:, cols], zero))
            join = lambda parts: jnp.concatenate(parts, axis=0)
            got_top, got_low = dot(join(k_top), dm_low[:, cols]), dot(join(k_low), dm_low[half:, cols])
            dxs[start : start + half, cols] = jnp.where(left, got_top[:half], got_top[half:])
            dxs[start + half : start + length, cols] = jnp.where(left, got_low[:half], got_low[half:])
            add_top = dot_nt(join(x_top), dm_low[:, cols])
            add_low = dot_nt(join(x_low), dm_low[half:, cols])
            add_top = add_top[:half] * decay_top[0] + add_top[half:] * decay_top[1]
            add_low = add_low[:half] * decay_low[0] + add_low[half:] * decay_low[1]
            sum_top = add_top if sum_top is None else sum_top + add_top
            sum_low = add_low if sum_low is None else sum_low + add_low
        dgt[s, :half] += sum_top
        dgt[s, half:, half:] += sum_low


def inside_back(cfg, meta, slot, xs, d_mixed, step2, logs3, enter2, log_t, gt, states):
    streams, length, slots, groups, per_group, headdim = cfg
    count = len(xs)
    rows, cols = xs[0].shape
    blocks = cols // BLOCK
    state_size = states[0].shape[1]
    whole = lambda i, m: (0, 0)
    cube = lambda i, m: (0, 0, 0)
    at = lambda i, m: m[slot + lax.div(i, blocks)] * blocks + lax.rem(i, blocks)
    local_at = lambda i, j: jnp.clip(i - blocks * j, 0, blocks - 1)
    return in_order(
        functools.partial(inside_back_kernel, cfg, slot, count, blocks),
        grid_spec=dict(
            grid=(count * blocks,),
            in_specs=[pl.BlockSpec((rows, BLOCK), lambda i, m, j=j: (0, local_at(i, j))) for j in range(count)]
            + [
                pl.BlockSpec((streams, state_size, BLOCK), lambda i, m, j=j: (0, 0, local_at(i, j)))
                for j in range(count)
            ]
            + [
                pl.BlockSpec((rows, BLOCK), lambda i, m: (0, at(i, m))),
                pl.BlockSpec(step2.shape, whole),
                pl.BlockSpec(logs3.shape, whole),
                pl.BlockSpec(enter2.shape, whole),
                pl.BlockSpec((streams, 1, 8, length), lambda i, m: (0, at(i, m), 0, 0)),
                pl.BlockSpec(gt.shape, cube),
            ],
            out_specs=[
                pl.BlockSpec((rows, BLOCK), lambda i, m: (0, i)),
                pl.BlockSpec(gt.shape, cube),
                pl.BlockSpec((rows, state_size), whole),
            ],
        ),
        out_shape=[
            jax.ShapeDtypeStruct((rows, count * cols), F32),
            jax.ShapeDtypeStruct(gt.shape, F32),
            jax.ShapeDtypeStruct((rows, state_size), F32),
        ],
        compiler_params=pltpu.CompilerParams(vmem_limit_bytes=VMEM),
        cost_estimate=lasting(12),
        name="inside_back",
    )(meta, *placed([*xs, *states, d_mixed, step2, logs3, enter2, log_t, gt]))


def after_kernel(cfg, blocks, parts, meta_ref, *refs):
    streams, length, slots, groups, per_group, headdim = cfg
    xs, states, cis = (refs[i * groups : (i + 1) * groups] for i in range(3))
    dxss, refs = refs[3 * groups : 3 * groups + parts], refs[3 * groups + parts :]
    d_mixed, d_after, step, step2, rest2, taps, b_low, skip, cw, cb, dci, tail, spill, direct, sums, db = refs
    per_block = BLOCK // headdim
    which = lax.div(pl.program_id(0), blocks)
    first_head = meta_ref[which] * per_group + lax.rem(pl.program_id(0), blocks) * per_block
    spread = spread_of(first_head, BLOCK, headdim, groups * per_group)
    gather = gather_of(first_head, BLOCK, headdim)
    x, state, ci = pick(xs, which), pick(states, which), pick(cis, which)
    dxs = pick(dxss, lax.div(which, groups // parts))

    @pl.when(pl.program_id(0) == 0)
    def _():
        direct[...] = jnp.zeros_like(direct)
        sums[...] = jnp.zeros_like(sums)
        db[...] = jnp.zeros_like(db)

    for s in range(streams):
        at = slice(s * length, (s + 1) * length)
        st = step[at]
        x_s = x[at]
        step_wide = expand(step2[at], spread)
        rest_wide = expand(rest2[at], spread)
        back = rest_wide * dot(b_low[at], d_after[s])
        inner_back = dxs[at]
        x_weighted = x_s * (rest_wide * step_wide)
        db[at] += dot_nt(x_weighted.astype(LOW), d_after[s])
        from_after = sum_heads(x_s * back, gather)
        direct[at] += sum_heads(x_s * inner_back, gather) + from_after
        crossed = jnp.sum(d_after[s].astype(F32) * state[s].astype(F32), axis=0, keepdims=True)
        crossed = sum_heads(jnp.broadcast_to(crossed, (8, BLOCK)), gather)
        after_sum = jnp.broadcast_to(jnp.sum(from_after * st, axis=0, keepdims=True), (8, LANES))
        sums[s] += jnp.where(iota((8, LANES), 0) == 0, crossed, after_sum)
        d_x = step_wide * (inner_back + back) + skip[...] * d_mixed[at]
        block = ci[s * (HALO + length) : (s + 1) * (HALO + length)].astype(F32)
        masks = tap_masks(taps[at], cw.shape[0])
        total = conv_back(d_x, block, masks, cw[...], cb[...])
        dci[at] = total[HALO:].astype(LOW)
        tail[s] = total[length:]
        spill[s] = total[HALO - 8 : HALO]


def after(cfg, meta, xs, states, cis, dxss, d_mixed, d_after, step, step2, rest2, taps, b_low, skip, conv_weight, conv_bias):
    streams, length, slots, groups, per_group, headdim = cfg
    rows, cols = xs[0].shape
    blocks = cols // BLOCK
    state_size = states[0].shape[1]
    total_cols = groups * cols
    parts = len(dxss)
    part_blocks = total_cols // parts // BLOCK
    whole = lambda i, m: (0, 0)
    at = lambda i, m: m[lax.div(i, blocks)] * blocks + lax.rem(i, blocks)
    spot = lambda r: pl.BlockSpec((r, BLOCK), lambda i, m: (0, at(i, m)))
    local_at = lambda i, j, n: jnp.clip(i - n * j, 0, n - 1)
    cube = lambda r: pl.BlockSpec((streams, r, BLOCK), lambda i, m: (0, 0, i))
    listed = lambda r, n, many: [pl.BlockSpec((r, BLOCK), lambda i, m, j=j: (0, local_at(i, j, n))) for j in range(many)]
    return in_order(
        functools.partial(after_kernel, cfg, blocks, parts),
        grid_spec=dict(
            grid=(groups * blocks,),
            in_specs=listed(rows, blocks, groups)
            + [
                pl.BlockSpec((streams, state_size, BLOCK), lambda i, m, j=j: (0, 0, local_at(i, j, blocks)))
                for j in range(groups)
            ]
            + listed(cis[0].shape[0], blocks, groups)
            + listed(rows, part_blocks, parts)
            + [
                spot(rows),
                pl.BlockSpec((streams, state_size, BLOCK), lambda i, m: (0, 0, at(i, m))),
                *[pl.BlockSpec(a.shape, whole) for a in (step, step2, rest2, taps, b_low)],
                spot(1), spot(conv_weight.shape[0]), spot(1),
            ],
            out_specs=[
                pl.BlockSpec((rows, BLOCK), lambda i, m: (0, i)), cube(HALO), cube(8),
                pl.BlockSpec((rows, LANES), whole),
                pl.BlockSpec((streams, 8, LANES), lambda i, m: (0, 0, 0)),
                pl.BlockSpec((rows, state_size), whole),
            ],
        ),
        out_shape=[
            jax.ShapeDtypeStruct((rows, total_cols), LOW),
            jax.ShapeDtypeStruct((streams, HALO, total_cols), F32),
            jax.ShapeDtypeStruct((streams, 8, total_cols), F32),
            jax.ShapeDtypeStruct((rows, LANES), F32),
            jax.ShapeDtypeStruct((streams, 8, LANES), F32),
            jax.ShapeDtypeStruct((rows, state_size), F32),
        ],
        compiler_params=pltpu.CompilerParams(vmem_limit_bytes=VMEM),
        cost_estimate=lasting(39),
        name="after",
    )(meta, *placed([*xs, *states, *cis, *dxss, d_mixed, d_after, step, step2, rest2, taps, b_low, skip, conv_weight, conv_bias], 1 << 18))


def finish_kernel(cfg, meta_ref, *refs):
    streams, length, slots, groups, per_group, headdim = cfg
    meta = Meta(meta_ref, groups, slots)
    parts = (len(refs) - 18) // 2
    dgts, dcs, refs = refs[:parts], refs[parts : 2 * parts], refs[2 * parts :]
    db_in, direct_in, sums, row_sum, step, slope, taps, through, rates, b_low, c_low, ci, cw, cb = refs[:14]
    width = through.shape[2]
    pick = (iota((width, LANES), 0) == iota((width, LANES), 1) * headdim).astype(F32)
    kept = [dot(through[s], pick, HIGHEST) for s in range(streams)]
    d_raw, dci, tail, spill = refs[14:]
    upper = (iota((length, length), 0) <= iota((length, length), 1)).astype(F32)
    add = lambda parts, at: functools.reduce(lambda a, b: a + b, [p[at] for p in parts])
    for s in range(streams):
        at = slice(s * length, (s + 1) * length)
        direct = direct_in[at]
        ends = sums[s]
        from_end = kept[s][0:1] * ends[0:1] + ends[1:2]
        d_log = dot(upper, row_sum[at] - step[at] * direct, HIGHEST) + from_end
        d_raw[at] = ((direct - rates[...] * d_log) * slope[at]).astype(LOW)
        seg_u = meta.segment(s, meta.first() + iota((length, length), 0))
        seg_t = meta.segment(s, meta.first() + iota((length, length), 1))
        dgt = jnp.where(seg_u == seg_t, upper, 0.0) * add(dgts, s)
        d_b = db_in[at] + dot(dgt.astype(LOW), c_low[at])
        d_c = add(dcs, at) + dot(jnp.transpose(dgt).astype(LOW), b_low[at])
        block = ci[s * (HALO + length) : (s + 1) * (HALO + length)].astype(F32)
        masks = tap_masks(taps[at], cw.shape[0])
        total = conv_back(jnp.concatenate([d_b, d_c], axis=1), block, masks, cw[...], cb[...])
        dci[at] = total[HALO:].astype(LOW)
        tail[s] = total[length:]
        spill[s] = total[HALO - 8 : HALO]


def finish(cfg, meta, dgts, dcs, db, direct, sums, row_sum, step, slope, taps, through, rates, b_low, c_low, ci, conv_weight, conv_bias, block_at):
    streams, length, slots, groups, per_group, headdim = cfg
    rows = streams * length
    args = [*dgts, *dcs, db, direct, sums, row_sum, step, slope, taps, through, rates, b_low, c_low, ci]
    zeros = lambda n: (lambda i, m: (0,) * n)
    conv_at = lambda i, m: (0, block_at)
    outs = [
        jax.ShapeDtypeStruct((rows, LANES), LOW),
        jax.ShapeDtypeStruct((rows, BLOCK), LOW),
        jax.ShapeDtypeStruct((streams, HALO, BLOCK), F32),
        jax.ShapeDtypeStruct((streams, 8, BLOCK), F32),
    ]
    return in_order(
        functools.partial(finish_kernel, cfg),
        grid_spec=dict(
            grid=(1,),
            in_specs=[pl.BlockSpec(a.shape, zeros(a.ndim)) for a in args]
            + [pl.BlockSpec((conv_weight.shape[0], BLOCK), conv_at), pl.BlockSpec((1, BLOCK), conv_at)],
            out_specs=[pl.BlockSpec(a.shape, zeros(len(a.shape))) for a in outs],
        ),
        out_shape=outs,
        compiler_params=pltpu.CompilerParams(vmem_limit_bytes=VMEM),
        cost_estimate=lasting(4),
        name="finish",
    )(meta, *placed([*args, conv_weight, conv_bias], 0))


def mend(d, tail, spill):
    streams = tail.shape[0]
    length = d.shape[0] // streams
    parts = []
    for s in range(streams):
        parts.append(d[s * length : (s + 1) * length - HALO])
        added = jnp.concatenate([jnp.zeros((HALO - 8, spill.shape[2]), F32), spill[s]], axis=0)
        parts.append((tail[s] + added).astype(LOW))
    return jnp.concatenate(parts, axis=0)


def turned(a, b):
    return lax.dot_general(a, b, (((0,), (0,)), ((), ())), preferred_element_type=F32)


def back_project_kernel(groups, blocks, core_place, chips, late, meta_ref, *refs):
    if late:
        d_ref, tail, spill, dn_in, dh_in = refs[:5]
        refs = refs[5:]
    else:
        d_ref, refs = refs[0], refs[1:]
    many = 2 * groups if late else 4
    weights, refs = refs[:many], refs[many:]
    hidden, up, dn, dh, g_up = refs[:5]
    held = refs[5] if late else dn
    step = pl.program_id(0)

    @pl.when(step == 0)
    def _():
        held[...] = dn_in[...] if late else jnp.zeros_like(held)
        dh[...] = dh_in[...] if late else jnp.zeros_like(dh)

    d = d_ref[...]
    if late:
        d = mend(d, tail[...], spill[...])
        for j in range(groups):

            @pl.when(lax.div(step, blocks) == j)
            def _():
                held[0] += dot_nt(d, weights[2 * j][...])
                held[1] += dot_nt(d, weights[2 * j + 1][...])
    else:
        near = step < blocks
        held[0] += dot_nt(d, jnp.where(near, weights[0][...], weights[1][0]))
        held[1] += dot_nt(d, jnp.where(near, weights[2][...], weights[3][0]))
    dh[...] += dot_nt(d, up[...])
    g_up[...] = jnp.transpose(turned(hidden[...], d))

    if late:
        core, chip = meta_ref[core_place], meta_ref[core_place + 1]
        size = dn.shape[2]

        @pl.when(step == groups * blocks - 1)
        def _():
            for k, distance in enumerate(ring_order(chips)):
                at = 2 * lax.rem(chip + distance, chips)
                cols = slice(k * size, (k + 1) * size)
                dn[at + core] = held[0, :, cols]
                dn[at + 1 - core] = held[1, :, cols]


def back_project(cfg, meta, ds, weights, hidden, in_up, first_block, late=None):
    streams, length, slots, groups, per_group, headdim = cfg
    rows = hidden.shape[0]
    half, cols = weights[0][0].shape
    blocks = cols // WIDE
    chips = lax.axis_size("fsdp") // 2
    core = core_at(groups, streams, slots)
    at = lambda i, m: m[lax.div(i, blocks)] * blocks + lax.rem(i, blocks)
    local_at = lambda i, j: jnp.clip(i - blocks * j, 0, blocks - 1)
    whole = lambda i, m: (0, 0)
    dn_spec = pl.BlockSpec((2, rows, half), lambda i, m: (0, 0, 0))
    dh_spec = pl.BlockSpec((rows, in_up.shape[0]), whole)
    out_spec = dn_spec
    if late is None:
        in_specs = [pl.BlockSpec((rows, WIDE), lambda i, m: (0, at(i, m)))]
        args = [ds]
    else:
        out_spec = pl.BlockSpec((2 * chips, rows, half // chips), lambda i, m: (0, 0, 0))
        tail, spill, dn, dh = late
        in_specs = [pl.BlockSpec((rows, WIDE), lambda i, m: (0, i))]
        in_specs += [pl.BlockSpec((streams, r, WIDE), lambda i, m: (0, 0, i)) for r in (HALO, 8)]
        in_specs += [dn_spec, dh_spec]
        args = [ds, tail, spill, dn, dh]
    if late is None:
        in_specs += quarter_specs(half, blocks) * 2
        args += [*weights[0], *weights[1]]
    else:
        for j, pair in enumerate(weights):
            for w in pair:
                in_specs.append(pl.BlockSpec((half, WIDE), lambda i, m, j=j: (0, local_at(i, j))))
                args.append(w)
    in_specs += [
        pl.BlockSpec(hidden.shape, whole),
        pl.BlockSpec((in_up.shape[0], WIDE), lambda i, m: (0, first_block + at(i, m))),
    ]
    args += [hidden, in_up]
    return in_order(
        functools.partial(back_project_kernel, groups, blocks, core, chips, late is not None),
        grid_spec=dict(
            grid=(groups * blocks,), in_specs=in_specs,
            out_specs=[out_spec, dh_spec, pl.BlockSpec((WIDE, in_up.shape[0]), lambda i, m: (at(i, m), 0))],
            scratch_shapes=[] if late is None else [pltpu.VMEM((2, rows, half), F32)],
        ),
        out_shape=[
            jax.ShapeDtypeStruct(out_spec.block_shape, F32),
            jax.ShapeDtypeStruct((rows, in_up.shape[0]), F32),
            jax.ShapeDtypeStruct((groups * cols, in_up.shape[0]), F32),
        ],
        compiler_params=pltpu.CompilerParams(vmem_limit_bytes=2 * VMEM),
        cost_estimate=lasting(15),
        name="back_project",
    )(meta, *placed(args))


def close_kernel(meta_ref, dn, dh, d_bc, tail, spill, w_small, d_raw, up, allowed, down, hidden, normed, x_in, gain, grad, out, g_bc, g_down):
    state_cols = d_bc.shape[1]
    width = x_in.shape[1]
    d = mend(d_bc[...], tail[...], spill[...])
    d_hidden = ((dh[...] + dot_nt(d, up[...])) * allowed[...]).astype(LOW)
    x = x_in[...].astype(F32)
    rs = lax.rsqrt(jnp.mean(x * x, axis=-1, keepdims=True) + EPSILON)
    d_normed = jnp.concatenate([dn[p] for p in range(dn.shape[0])], axis=1)
    d_normed = d_normed + dot_nt(d, w_small[:, :state_cols]) + dot_nt(d_raw[...], w_small[:, state_cols:])
    scaled = (d_normed + dot(d_hidden, down[...])) * gain[...]
    cross = jnp.sum(scaled * x, axis=-1, keepdims=True) / width
    out[...] = grad[...].astype(F32) + rs * (scaled - x * (rs * rs * cross))
    add_bc = jnp.transpose(turned(hidden[...], d))
    add_down = jnp.transpose(turned(d_hidden, normed[HALO:]))

    @pl.when(pl.program_id(0) == 0)
    def _():
        g_bc[...] = add_bc
        g_down[...] = add_down

    @pl.when(pl.program_id(0) > 0)
    def _():
        g_bc[...] += add_bc
        g_down[...] += add_down


def close(streams, meta, dn, dh, d_bc, tail, spill, w_small, d_raw, in_up, allowed, down, hidden, normed, x_in, gain, grad):
    rows, width = x_in.shape
    length = rows // streams
    ranks = hidden.shape[1]
    state_cols = d_bc.shape[1]
    row = lambda cols: pl.BlockSpec((length, cols), lambda i, m: (i, 0))
    stack = pl.BlockSpec((dn.shape[0], length, dn.shape[2]), lambda i, m: (0, i, 0))
    whole = lambda a: pl.BlockSpec(a.shape, lambda i, m: (0, 0))
    end = lambda r: pl.BlockSpec((1, r, state_cols), lambda i, m: (i, 0, 0))
    return in_order(
        close_kernel,
        grid_spec=dict(grid=(streams,), in_specs=[
            stack, row(ranks), row(state_cols), end(HALO), end(8), whole(w_small), row(LANES),
            pl.BlockSpec((ranks, state_cols), lambda i, m: (0, in_up.shape[1] // state_cols - 1)),
            row(ranks), whole(down), row(ranks), pl.BlockSpec((length + HALO, width), lambda i, m: (i, 0)), row(width),
            whole(gain), row(width),
        ],
        out_specs=[
            row(width),
            pl.BlockSpec((state_cols, ranks), lambda i, m: (0, 0)),
            pl.BlockSpec((width, ranks), lambda i, m: (0, 0)),
        ]),
        out_shape=[
            jax.ShapeDtypeStruct((rows, width), F32),
            jax.ShapeDtypeStruct((state_cols, ranks), F32),
            jax.ShapeDtypeStruct((width, ranks), F32),
        ],
        compiler_params=pltpu.CompilerParams(vmem_limit_bytes=2 * VMEM),
        cost_estimate=lasting(5),
        name="close",
    )(meta, *placed([dn, dh, d_bc, tail, spill, w_small, d_raw, in_up, allowed, down, hidden, normed, x_in, gain, grad]))


def out_back_kernel(groups, chips, meta_ref, d_branch, w_mine, w_mine_far, w_other, w_other_far, out, ordered):
    cols = w_mine.shape[1]

    @pl.when(pl.program_id(0) == 0)
    def _():
        for j in range(groups):
            ordered[:, j * cols : (j + 1) * cols] = d_branch[:, pl.ds(pl.multiple_of(meta_ref[j] * cols, cols), cols)]

    def product(near, far):
        w = jnp.concatenate([near[...]] + [far[j] for j in range(groups - 1)], axis=1)
        out[0] = dot_nt(ordered[...], w)

    @pl.when(pl.program_id(0) < chips)
    def _():
        product(w_mine, w_mine_far)

    @pl.when(pl.program_id(0) >= chips)
    def _():
        product(w_other, w_other_far)


def out_back(cfg, meta, d_branch, weights):
    streams, length, slots, groups, per_group, headdim = cfg
    rows, width = d_branch.shape
    chips = lax.axis_size("fsdp") // 2
    core = core_at(groups, streams, slots)
    half, cols = weights[0][0].shape
    size = half // chips

    def device(i, m):
        distance = jnp.int32(0)
        for at, value in enumerate(ring_order(chips)):
            distance = jnp.where(lax.rem(i, chips) == at, value, distance)
        return 2 * lax.rem(m[core + 1] + distance, chips) + jnp.where(i < chips, m[core], 1 - m[core])

    block = lambda i, side: jnp.clip(i - side * chips, 0, chips - 1)
    weight = lambda side: [
        pl.BlockSpec((size, cols), lambda i, m: (block(i, side), 0)),
        pl.BlockSpec((groups - 1, size, cols), lambda i, m: (0, block(i, side), 0)),
    ]
    return in_order(
        functools.partial(out_back_kernel, groups, chips),
        grid_spec=dict(
            grid=(2 * chips,),
            in_specs=[pl.BlockSpec((rows, width), lambda i, m: (0, 0)), *weight(0), *weight(1)],
            out_specs=pl.BlockSpec((1, rows, size), lambda i, m: (device(i, m), 0, 0)),
            scratch_shapes=[pltpu.VMEM((rows, width), LOW)],
        ),
        out_shape=jax.ShapeDtypeStruct((2 * chips, rows, size), F32),
        compiler_params=pltpu.CompilerParams(vmem_limit_bytes=VMEM),
        cost_estimate=lasting(8),
        name="out_back",
    )(meta, *placed([d_branch, *weights[0], *weights[1]]))


def out_project_kernel(cfg, chips, meta_ref, out_low, d_branch, x, allowed, down, up, d_hidden, w_mine, w_mine_far, w_other, w_other_far, y, g_down, g_up, pieces, ordered, hidden):
    streams, length, slots, groups, per_group, headdim = cfg
    meta = Meta(meta_ref, groups, slots)
    core = meta_ref[core_at(groups, streams, slots)]
    chip = meta_ref[core_at(groups, streams, slots) + 1]
    size = pieces.shape[2]

    @pl.when(pl.program_id(0) == 0)
    def _():
        for p in range(2 * chips):
            pieces[p] = out_low[:, p * size : (p + 1) * size]
        for k, distance in enumerate(ring_order(chips)):
            at = 2 * lax.rem(chip + distance, chips)
            ordered[0, :, k * size : (k + 1) * size] = pieces[at + core]
            ordered[1, :, k * size : (k + 1) * size] = pieces[at + 1 - core]
        hidden[...] = (dot_nt(out_low[...], down[...]) * allowed[...]).astype(LOW)

    near = pl.program_id(0) == 0
    w_mine = jnp.where(near, w_mine[...], w_mine_far[0])
    w_other = jnp.where(near, w_other[...], w_other_far[0])
    branch = dot(ordered[0], w_mine) + dot(ordered[1], w_other) + dot(hidden[...], up[...])
    for s in range(streams):
        at = slice(s * length, (s + 1) * length)
        seg = meta.segment(s, meta.first() + iota((length, LANES), 0))
        kept = jnp.where(wide(seg, branch.shape[1]) < slots, branch[at], 0.0)
        y[at] = (x[at].astype(F32) + kept).astype(LOW)
    cols = g_down.shape[0]
    start = pl.multiple_of(pl.program_id(0) * cols, cols)
    g_down[...] = jnp.transpose(turned(d_hidden[...], out_low[:, pl.ds(start, cols)]))
    g_up[...] = jnp.transpose(turned(hidden[...], d_branch[...]))


def out_project(cfg, meta, out_low, d_branch, x, allowed, down, up, d_hidden, weights):
    streams, length, slots, groups, per_group, headdim = cfg
    rows, width = x.shape
    inner = out_low.shape[1]
    chips = lax.axis_size("fsdp") // 2
    half, cols = weights[0][0].shape
    ranks = down.shape[0]
    whole = lambda a: pl.BlockSpec(a.shape, lambda i, m: (0, 0))
    turn = pl.BlockSpec((rows, cols), lambda i, m: (0, m[i]))
    far = pl.BlockSpec((1, half, cols), lambda i, m: (jnp.maximum(i - 1, 0), 0, 0))
    return in_order(
        functools.partial(out_project_kernel, cfg, chips),
        grid_spec=dict(
            grid=(groups,),
            in_specs=[
                whole(out_low), turn, turn, whole(allowed), whole(down),
                pl.BlockSpec((ranks, cols), lambda i, m: (0, m[i])), whole(d_hidden),
                whole(weights[0][0]), far, whole(weights[1][0]), far,
            ],
            out_specs=[
                turn,
                pl.BlockSpec((inner // groups, ranks), lambda i, m: (i, 0)),
                pl.BlockSpec((cols, ranks), lambda i, m: (m[i], 0)),
            ],
            scratch_shapes=[
                pltpu.VMEM((2 * chips, rows, half // chips), LOW), pltpu.VMEM((2, rows, half), LOW),
                pltpu.VMEM((rows, ranks), LOW),
            ],
        ),
        out_shape=[
            jax.ShapeDtypeStruct((rows, width), LOW),
            jax.ShapeDtypeStruct((inner, ranks), F32),
            jax.ShapeDtypeStruct((width, ranks), F32),
        ],
        compiler_params=pltpu.CompilerParams(vmem_limit_bytes=2 * VMEM),
        cost_estimate=lasting(10),
        name="out_project",
    )(meta, *placed([out_low, d_branch, x, allowed, down, up, d_hidden, *weights[0], *weights[1]]))


def swap_cores(value):
    return lax.ppermute(value, "fsdp", [(i, i ^ 1) for i in range(lax.axis_size("fsdp"))])


def then(value, earlier):
    return lax.optimization_barrier((value, earlier))[0]


class Scan:
    def __init__(self, own, kept_mine, kept_other, reverse):
        self.count = lax.axis_size("fsdp")
        self.core = core = lax.axis_index("fsdp") % 2
        self.reverse = reverse
        half = own.shape[2] // 2
        take = lambda a, side: lax.dynamic_slice_in_dim(a, side * half, half, 2)
        mine = take(own, core)
        self.other = other = swap_cores(take(own, 1 - core))
        self.early = early = (core == 1) if reverse else (core == 0)
        self.first = jnp.where(early, mine, other).astype(F32)
        second = jnp.where(early, other, mine).astype(F32)
        kept_mine, kept_other = take(kept_mine, core), take(kept_other, core)
        self.kept_first = jnp.where(early, kept_mine, kept_other)
        kept_second = jnp.where(early, kept_other, kept_mine)
        self.added = kept_second * self.first + second
        self.kept_both = self.kept_first * kept_second
        self.hops = self.count // 2 - 1
        self.entering = None

    def hop(self, number, earlier=None):
        send = self.added
        if self.entering is not None:
            send = self.kept_both * self.entering.astype(F32) + send
        send = send.astype(LOW)
        if earlier is not None:
            send = then(send, earlier)
        chip = self.hops - number if self.reverse else number
        route = [(2 * chip + c, 2 * (chip - 1 if self.reverse else chip + 1) + c) for c in (0, 1)]
        got = lax.ppermute(send, "fsdp", route)
        self.entering = got if self.entering is None else self.entering + got
        return got

    def end(self, earlier=None):
        entering = self.entering.astype(F32)
        entering_second = self.kept_first * entering + self.first
        keep = jnp.where(self.early, entering, entering_second).astype(LOW)
        send = jnp.where(self.early, entering_second, entering).astype(LOW)
        if earlier is not None:
            send = then(send, earlier)
        got = swap_cores(send)
        low, high = jnp.concatenate([keep, got], 2), jnp.concatenate([got, keep], 2)
        return jnp.where(self.core == 0, low, high)


def reduce_rows(parts, partial):
    count, replicas = lax.axis_size("fsdp"), lax.axis_size("dp")
    place, replica = lax.axis_index("fsdp"), lax.axis_index("dp")
    chips, chip, core = count // 2, place // 2, place % 2
    sizes = [p.shape[0] // (count * replicas) for p in parts]
    lanes = parts[0].shape[1]
    cut = [p.reshape(chips, 2, replicas, n, lanes) for p, n in zip(parts, sizes)]
    spare = -sum(sizes) % HALO
    if spare:
        cut.append(jnp.zeros((chips, 2, replicas, spare, lanes), F32))
    whole = jnp.concatenate(cut, axis=3)
    pick = lambda a, i, dim: lax.dynamic_index_in_dim(a, i, dim, False)
    total = pick(whole, core, 1) + swap_cores(pick(whole, 1 - core, 1))
    each = total.shape[2]
    partial = partial.reshape(replicas, -1, lanes)
    short = partial.shape[1]
    column = lambda r: jnp.concatenate([pick(total, r, 1).reshape(-1, lanes), pick(partial, r, 0)])
    mine = column(replica)
    for k in range(1, replicas):
        mine = mine + over_dp(column(replica ^ k).astype(LOW), k).astype(F32)
    mine, part_sum = mine[: chips * each].reshape(chips, each, lanes), mine[chips * each :]
    last = pick(mine, chip, 0)
    for k in range(1, chips):
        route = [(i, (i + 2 * k) % count) for i in range(count)]
        last = last + lax.ppermute(pick(mine, (chip + k) % chips, 0).astype(LOW), "fsdp", route).astype(F32)
    last = jnp.concatenate([last, part_sum]).astype(LOW)
    near = jnp.stack([last] + [over_dp(last, k) for k in range(1, replicas)])
    full = jnp.stack([pick(near, replica ^ a, 0) for a in range(replicas)])
    full = full.astype(F32)
    outs, start = [], 0
    for n in sizes:
        outs.append(full[:, start : start + n].reshape(replicas * n, lanes))
        start += n
    return *outs, full[:, each:].reshape(replicas * short, lanes)


def over_dp(value, bit):
    return lax.ppermute(value, "dp", [(i, i ^ bit) for i in range(lax.axis_size("dp"))])


def after_token(value, token):
    return value + token.astype(value.dtype)


class Share:
    def __init__(self, near, mine, other):
        self.near, self.mine, self.other = near, mine, other
        self.one, self.two = over_dp(mine[1:], 1), over_dp(mine[1:], 2)
        part = mine.shape[1] // 2
        self.halves = self.one[:, :part], self.two[:, part:]
        self.last = over_dp(self.halves[0], 2), over_dp(self.halves[1], 1)

    def join(self, j, token=None):
        far, near = (None, self.one, self.two, None)[j], self.near[j]
        if far is None:
            far = jnp.concatenate(self.last, axis=1)
        if token is not None:
            near, far = after_token(near, token), after_token(far, token)
        return flat(jnp.concatenate([near[None], far]))

    def end(self):
        got = jnp.stack([self.join(j) for j in range(1, len(self.near))])
        return (flat(self.mine), got), (flat(self.other), swap_cores(got))


def in_ring(every, token=0):
    count, place = every.shape[0], lax.axis_index("fsdp") + token
    take = lambda k, flip: lax.dynamic_index_in_dim(every, (place + 2 * k) % count ^ flip, 0, False)
    return [jnp.stack([take(k, flip) for k in ring_order(count // 2)]) for flip in (0, 1)]


def flat(chips):
    return chips.reshape(-1, chips.shape[2])


def local(
    block_input, seq_lengths, adapter_ids, norm_gain, w_in, w_dt, conv_weight, conv_bias, dt_bias,
    head_rates, skip_gain, gate_gain, w_out, in_down, in_up, out_down, out_up, out_grad,
):
    streams, length, width = block_input.shape[1:]
    inner = gate_gain.shape[0]
    conv_cols = conv_weight.shape[1]
    heads = dt_bias.shape[0]
    headdim = inner // heads
    state_size = (conv_cols - inner) // 2
    adapters, ranks = in_down.shape[:2]
    in_cols = in_up.shape[2]
    slots = seq_lengths.shape[2]
    rows = streams * length
    groups = lax.axis_size("dp")
    per_group = heads // groups
    group_cols = inner // groups
    cfg = (streams, length, slots, groups, per_group, headdim)
    count = lax.axis_size("fsdp")
    first_pos = lax.axis_index("fsdp") * length
    ends = jnp.cumsum(seq_lengths[0], axis=-1, dtype=jnp.int32)
    place = lax.axis_index("fsdp")
    core, chip, chips = place % 2, place // 2, count // 2
    order = lax.axis_index("dp") ^ jnp.arange(groups, dtype=jnp.int32)
    meta = [order, first_pos[None], ends.reshape(-1), core[None], chip[None], adapter_ids.reshape(-1)]
    meta = jnp.concatenate(meta).astype(jnp.int32)
    ids_place = core_at(groups, streams, slots) + 2
    pad_heads = lambda a: jnp.pad(a, ((0, 0), (0, LANES - heads)))

    quarters = lambda a: [
        lax.dynamic_slice_in_dim(a, order[j] * group_cols, group_cols, 1) for j in range(groups)
    ]
    own_x, own_gate = quarters(w_in[:, inner : 2 * inner]), quarters(w_in[:, :inner])
    small = jnp.concatenate([w_in[:, 2 * inner :], pad_heads(w_dt)], axis=1)
    every = lax.all_gather(jnp.concatenate([own_x[0], small], axis=1), "fsdp")
    w_small = every[:, :, group_cols:].reshape(width, -1)
    every_gate = lax.all_gather(own_gate[0], "fsdp")
    out_cols = width // groups
    own_out = [lax.dynamic_slice_in_dim(w_out, order[j] * out_cols, out_cols, 1) for j in range(groups)]
    every_out = lax.all_gather(own_out[0], "fsdp")
    Order.waits = []
    devices = range(count)
    before = lax.ppermute(block_input[0, :, length - HALO :], "fsdp", [(i - 1, i) for i in devices if i > 0])
    down_in = in_down.reshape(adapters * ranks, width)
    up_in = in_up.reshape(adapters * ranks, in_cols)
    down_out = out_down.reshape(adapters * ranks, inner)
    up_out = out_up.reshape(adapters * ranks, width)
    x_rows, grad_rows = block_input.reshape(rows, width), out_grad.reshape(rows, width)
    normed_ext, nx_ext, hidden_ext, hidden_in, allowed, d_branch, d_hidden_out = prepare(
        cfg, meta, ids_place, ranks, x_rows, before.reshape(streams * HALO, width), norm_gain[None],
        down_in, grad_rows, up_out,
    )

    rates = pad_heads(head_rates[None])
    bias_row = conv_bias[None]
    (ci_bc, step, slope, taps, logs3, step2, enter2, rest2, weight2, log_t, through, g, gt, b_low, c_low, bt, ct) = decays(
        cfg, meta, normed_ext, hidden_ext, w_small, up_in, conv_weight, bias_row, pad_heads(dt_bias[None]), rates, heads
    )
    kept_mine = through[:, :1]
    kept_other = swap_cores(kept_mine)
    of_group = lambda a, j: lax.dynamic_slice_in_dim(a, order[j] * group_cols, group_cols, 2)

    w_x, ci, xs, ys, added = [], [], [], [], []

    def enter_group(j, weights):
        w_x.append(weights)
        ci_j, x_j, own = project(cfg, meta, j, nx_ext, hidden_ext, weights, up_in, conv_weight, bias_row, weight2, taps, bt)
        ci.append(ci_j)
        xs.append(x_j)
        added.append(own)

    def scan_of(js):
        kept = [jnp.concatenate([of_group(a, j) for j in js], axis=2) for a in (kept_mine, kept_other)]
        return Scan(jnp.concatenate([added[j] for j in js], axis=2), *kept, False)

    pairs = lambda j: inside(cfg, meta, j, xs[j], step2, logs3, log_t, g)
    x_share = Share(own_x, *in_ring(every[:, :, :group_cols]))
    enter_group(0, (flat(x_share.mine), flat(x_share.other)))
    ys.append(pairs(0))
    near = [x_share.join(j) for j in (1, 2)]
    near = [(w, swap_cores(w)) for w in near]
    wait_for(*x_share.halves)
    enter_group(1, near[0])
    gate_share = Share(own_gate, *in_ring(every_gate, Order.token))
    enter_group(2, near[1])
    scans = [scan_of((0, 1))]
    got = scans[0].hop(0)
    last = x_share.join(3, Order.token)
    wait_for(last, scans[0].other)
    enter_group(3, (last, swap_cores(last)))
    out_share = Share(own_out, *in_ring(every_out, Order.token))
    scans.append(scan_of((2, 3)))
    wait_for(got, scans[1].other)
    ys.append(pairs(1))
    got = [scans[0].hop(1), scans[1].hop(0)]
    wait_for(*gate_share.halves, *got)
    ys.append(pairs(2))
    got = [scans[0].hop(2), scans[1].hop(1)]
    w_gate = gate_share.end()
    wait_for(*got)
    ys.append(pairs(3))
    got = [scans[1].hop(2)]
    for hop in range(3, chips - 1):
        got = [scans[0].hop(hop), scans[1].hop(hop)]
    wait_for(*out_share.halves)
    gate = gate_project(cfg, meta, nx_ext, hidden_ext, w_gate, up_in)
    w_o = out_share.end()
    wait_for(*got)
    pair_states = [scan.end() for scan in scans]
    states = [pair_states[j // 2][:, :, (j % 2) * group_cols : (j % 2 + 1) * group_cols] for j in range(groups)]
    d_pieces = out_back(cfg, meta, d_branch, w_o)

    skip_row = jnp.repeat(skip_gain, headdim)[None]
    out_low, d_mixed, d_gate, row_sum, d_state = gated(
        cfg, meta, xs, ys, states, gate, d_pieces, d_hidden_out, down_out, enter2, c_low, ct, skip_row, gate_gain[None]
    )
    pieces = 2
    wide_cols = inner // pieces
    part = lambda a, j: a[:, :, j * wide_cols : (j + 1) * wide_cols]
    scans = [Scan(part(d_state, j), part(kept_mine, j), part(kept_other, j), True) for j in range(pieces)]
    arrived = [[scan.hop(0) for scan in scans]]

    wait_for(*[scan.other for scan in scans])

    block_output, g_out_down, g_out_up = out_project(
        cfg, meta, out_low, d_branch, x_rows, allowed, down_out, up_out, d_hidden_out, w_o
    )
    wait_for(*arrived[0])
    early = back_project(cfg, meta, d_gate, w_gate, hidden_in, up_in, 0)
    for hop in range(1, chips - 1):
        arrived.append([scan.hop(hop) for scan in scans])
    half_groups = groups // 2
    inside_parts = []
    for p in (0, 1):
        wait_for(*arrived[p + 1])
        js = slice(p * half_groups, (p + 1) * half_groups)
        inside_parts.append(
            inside_back(cfg, meta, p * half_groups, xs[js], d_mixed, step2, logs3, enter2, log_t, gt, states[js])
        )
    dxs, dgts, dcs = zip(*inside_parts)
    d_after = jnp.concatenate([scan.end() for scan in scans], axis=2)
    by_device = lambda a: a.reshape(count, a.shape[0] // count, a.shape[1])
    out_sums = jnp.concatenate([by_device(g_out_down), by_device(g_out_up)], axis=1)
    out_sums = lax.psum_scatter(then(out_sums, dxs[1]), "fsdp", scatter_dimension=0, tiled=False)
    dci, tail, spill, direct, sums, db = after(
        cfg, meta, xs, states, ci, dxs, d_mixed, d_after, step, step2, rest2, taps, b_low, skip_row, conv_weight, bias_row
    )
    to_earlier = lambda a: lax.ppermute(a, "fsdp", [(i, i - 1) for i in devices if i > 0])
    spill = to_earlier(spill)
    d_raw, dci_bc, tail_bc, spill_bc = finish(
        cfg, meta, dgts, dcs, db, direct, sums, row_sum, step, slope, taps, through, rates, b_low, c_low,
        ci_bc, conv_weight, bias_row, inner // BLOCK,
    )
    spill_bc = to_earlier(spill_bc)
    late = back_project(
        cfg, meta, dci, w_x, hidden_in, up_in, inner // WIDE, (tail, spill, early[0], early[1])
    )
    input_grad, g_bc, g_in_down = close(
        streams, meta, late[0], late[1], dci_bc, tail_bc, spill_bc, w_small, d_raw, up_in, allowed, down_in, hidden_in,
        normed_ext, x_rows, norm_gain[None], grad_rows,
    )
    in_down_sum, in_up_sum, out_sums = reduce_rows(
        [g_in_down, jnp.concatenate([early[2], late[2], g_bc], axis=0)], out_sums
    )
    out_sums = jnp.split(out_sums, [inner // count], axis=0)
    totals = [a.T.reshape(adapters, ranks, -1) for a in (in_down_sum, in_up_sum, *out_sums)]
    return (block_output.reshape(1, streams, length, width), input_grad.reshape(1, streams, length, width), *totals)


def solution(mesh):
    rows = P("dp", None, "fsdp", None)
    cut = P("fsdp", None)
    per_group = P("dp", None, None)
    in_specs = (
        rows, per_group, per_group, P(), cut, cut, P(), P(), P(), P(), P(), P(), cut, P(), P(), P(), P(), rows,
    )
    out_specs = (rows, rows) + (P(None, None, "fsdp"),) * 4
    return jax.shard_map(local, mesh=mesh, in_specs=in_specs, out_specs=out_specs, check_vma=False)
```

```python
import functools

import jax
import jax.numpy as jnp
from jax import lax
from jax.experimental import pallas as pl
from jax.experimental.pallas import tpu as pltpu
from jax.sharding import PartitionSpec as P

EPSILON = 1e-05
HIGHEST = lax.Precision.HIGHEST
F32, LOW = jnp.float32, jnp.bfloat16
HALO = 16
LANES = 128
BLOCK = 256
WIDE = 768
VMEM = 16 * 1024 * 1024


def lasting(us):
    return pl.CostEstimate(flops=int(us * 1.15e9), bytes_accessed=1000000, transcendentals=0)


class Order:
    waits = []
    token = None


def in_order(kernel, *, grid_spec, out_shape, compiler_params, cost_estimate, name):
    def call(meta, *args):
        waits = Order.waits
        skip = len(waits)
        specs = [pl.BlockSpec(memory_space=pl.ANY)] * skip + list(grid_spec["in_specs"])
        single = not isinstance(out_shape, (list, tuple))
        shapes = [out_shape] if single else list(out_shape)
        out_specs = [grid_spec["out_specs"]] if single else list(grid_spec["out_specs"])
        token_at = skip + len(args) + len(shapes)

        def body(meta_ref, *refs):
            refs[token_at][...] = jnp.zeros((8, LANES), jnp.int32)
            kernel(meta_ref, *refs[skip:token_at], *refs[token_at + 1 :])

        outs = pl.pallas_call(
            body,
            grid_spec=pltpu.PrefetchScalarGridSpec(
                num_scalar_prefetch=1,
                grid=grid_spec["grid"],
                in_specs=specs,
                out_specs=out_specs + [pl.BlockSpec((8, LANES), lambda i, m: (0, 0))],
                scratch_shapes=grid_spec.get("scratch_shapes", ()),
            ),
            out_shape=shapes + [jax.ShapeDtypeStruct((8, LANES), jnp.int32)],
            compiler_params=compiler_params,
            cost_estimate=cost_estimate,
            name=name,
        )(meta, *waits, *args)
        Order.waits = [outs[-1]]
        Order.token = outs[-1][0, 0]
        return outs[0] if single else outs[:-1]

    return call


def wait_for(*arrays):
    Order.waits = Order.waits + list(arrays)


def dot(a, b, precision=None):
    return lax.dot_general(
        a, b, (((1,), (0,)), ((), ())), precision=precision, preferred_element_type=F32
    )


def dot_nt(a, b, precision=None):
    return lax.dot_general(
        a, b, (((1,), (1,)), ((), ())), precision=precision, preferred_element_type=F32
    )


def iota(shape, dim):
    return lax.broadcasted_iota(jnp.int32, shape, dim)


def packed(values, heads, terms):
    lane = iota(values.shape, 1)
    total, rest, wrapped = None, values, None
    for term in range(terms):
        part = rest.astype(LOW).astype(F32)
        rest = rest - part
        if term == 0:
            total = part
        elif (term + 1) * heads <= LANES:
            total = total + pltpu.roll(part, term * heads, 1)
        else:
            moved = pltpu.roll(part, term * heads, 1)
            total = total + jnp.where(lane >= term * heads, moved, 0.0)
            wrapped = jnp.where(lane < term * heads, moved, 0.0)
    if wrapped is not None:
        total = jnp.concatenate([total, wrapped], axis=1)
    return total.astype(LOW)


def expand(values, spread):
    return dot(values, spread)


def sigmoid(v):
    return 0.5 + 0.5 * jnp.tanh(0.5 * v)


def core_at(groups, streams, slots):
    return groups + 1 + streams * slots


def ring_order(chips):
    order = [0]
    for k in range(1, chips // 2 + 1):
        order += [k, chips - k] if k != chips - k else [k]
    return order


def placed(arrays, limit=1 << 20):
    return [
        pltpu.with_memory_space_constraint(a, pltpu.HBM) if a.size * a.dtype.itemsize > limit else a for a in arrays
    ]


class Meta:
    def __init__(self, ref, groups, slots):
        self.ref, self.groups, self.slots = ref, groups, slots

    def first(self):
        return self.ref[self.groups]

    def end(self, stream, slot):
        return self.ref[self.groups + 1 + stream * self.slots + slot]

    def segment(self, stream, pos):
        seg = jnp.zeros_like(pos)
        for slot in range(self.slots):
            seg = seg + (pos >= self.end(stream, slot)).astype(jnp.int32)
        return jnp.where(pos < 0, -1, seg)

    def scalar_segment(self, stream, pos):
        seg = jnp.int32(0)
        for slot in range(self.slots):
            seg = seg + jnp.where(pos >= self.end(stream, slot), 1, 0)
        return jnp.where(pos < 0, -1, seg)


def tap_masks(columns, taps):
    return [jnp.broadcast_to(columns[:, k : k + 1], columns.shape) for k in range(taps - 1)]


def wide(mask, cols):
    return jnp.concatenate([mask] * (cols // LANES), axis=1)


def conv_pre(block, masks, cw, cb):
    taps, cols = cw.shape
    total = cb + cw[taps - 1 : taps] * block[HALO:]
    for k in range(taps - 1):
        moved = pltpu.roll(block, taps - 1 - k, 0)[HALO:]
        total = total + cw[k : k + 1] * moved * wide(masks[k], cols)
    return total


def conv_back(d_out, block, masks, cw, cb):
    taps, cols = cw.shape
    pre = conv_pre(block, masks, cw, cb)
    sig = sigmoid(pre)
    d_pre = d_out * (sig * (1.0 + pre * (1.0 - sig)))
    total = jnp.concatenate([jnp.zeros((HALO, cols), F32), cw[taps - 1 : taps] * d_pre], axis=0)
    rows = total.shape[0]
    for k in range(taps - 1):
        part = cw[k : k + 1] * d_pre * wide(masks[k], cols)
        part = jnp.concatenate([jnp.zeros((HALO, cols), F32), part], axis=0)
        total = total + pltpu.roll(part, rows - (taps - 1 - k), 0)
    return total


def spread_of(first_head, cols, per_head, heads, terms=2):
    shape = (LANES * (1 if terms * heads <= LANES else 2), cols)
    head = lax.shift_right_logical(iota(shape, 1), per_head.bit_length() - 1) + first_head
    row = iota(shape, 0)
    hit = row == head
    for term in range(1, terms):
        hit = hit | (row == head + term * heads)
    return hit.astype(LOW)


def gather_of(first_head, cols, per_head):
    head = lax.shift_right_logical(iota((cols, LANES), 0), per_head.bit_length() - 1) + first_head
    return (iota((cols, LANES), 1) == head).astype(LOW)


def sum_heads(values, gather):
    part = values.astype(LOW)
    rest = (values - part.astype(F32)).astype(LOW)
    return dot(part, gather) + dot(rest, gather)


def halves_product(nx, hx, w_mine, w_other, up):
    return (dot(nx[0], w_mine) + dot(nx[1], w_other) + dot(hx[...], up[...])).astype(LOW)


def quarter_specs(half, blocks):
    far = lambda i: jnp.maximum(i - blocks, 0)
    return [
        pl.BlockSpec((half, WIDE), lambda i, m: (0, jnp.minimum(i, blocks - 1))),
        pl.BlockSpec((1, half, WIDE), lambda i, m: (lax.div(far(i), blocks), 0, lax.rem(far(i), blocks))),
    ]


def gate_project_kernel(cfg, blocks, meta_ref, nx, hx, w_mine, w_mine_far, w_other, w_other_far, up, out):
    streams, length, slots, groups, per_group, headdim = cfg
    near = pl.program_id(0) < blocks
    w_mine = jnp.where(near, w_mine[...], w_mine_far[0])
    w_other = jnp.where(near, w_other[...], w_other_far[0])
    full = halves_product(nx, hx, w_mine, w_other, up)
    for s in range(streams):
        out[s * length : (s + 1) * length] = full[s * (HALO + length) + HALO : (s + 1) * (HALO + length)]


def gate_project(cfg, meta, nx, hx, weights, in_up):
    streams, length, slots, groups, per_group, headdim = cfg
    half, cols = weights[0][0].shape
    rows = streams * length
    blocks = cols // WIDE
    at = lambda i, m: m[lax.div(i, blocks)] * blocks + lax.rem(i, blocks)
    return in_order(
        functools.partial(gate_project_kernel, cfg, blocks),
        grid_spec=dict(
            grid=(groups * blocks,),
            in_specs=[
                pl.BlockSpec(nx.shape, lambda i, m: (0, 0, 0)),
                pl.BlockSpec(hx.shape, lambda i, m: (0, 0)),
                *quarter_specs(half, blocks) * 2,
                pl.BlockSpec((in_up.shape[0], WIDE), lambda i, m: (0, at(i, m))),
            ],
            out_specs=pl.BlockSpec((rows, WIDE), lambda i, m: (0, at(i, m))),
        ),
        out_shape=jax.ShapeDtypeStruct((rows, groups * cols), LOW),
        compiler_params=pltpu.CompilerParams(vmem_limit_bytes=2 * VMEM),
        cost_estimate=lasting(9),
        name="project_gate",
    )(meta, *placed([nx, hx, *weights[0], *weights[1], in_up]))


def project_kernel(cfg, slot, meta_ref, nx, hx, w_mine, w_other, up, cw, cb, weight, taps, bt, ci, x_out, state):
    streams, length, slots, groups, per_group, headdim = cfg
    per_block = BLOCK // headdim
    first_head = meta_ref[slot] * per_group + pl.program_id(0) * per_block
    spread = spread_of(first_head, BLOCK, headdim, groups * per_group)
    low = halves_product(nx, hx, w_mine[...], w_other[...], up)
    ci[...] = low
    full = low.astype(F32)
    for s in range(streams):
        block = full[s * (HALO + length) : (s + 1) * (HALO + length)]
        masks = tap_masks(taps[s * length : (s + 1) * length], cw.shape[0])
        pre = conv_pre(block, masks, cw[...], cb[...])
        x = pre * sigmoid(pre)
        x_out[s * length : (s + 1) * length] = x
        scale = expand(weight[s * length : (s + 1) * length], spread)
        state[s] = dot(bt[s], (x * scale).astype(LOW)).astype(LOW)


def project(cfg, meta, slot, nx, hx, weights, in_up, conv_weight, conv_bias, weight, taps, bt):
    streams, length, slots, groups, per_group, headdim = cfg
    rows = streams * length
    ext = hx.shape[0]
    half, cols = weights[0].shape
    blocks = cols // BLOCK
    gate_blocks = (in_up.shape[1] - conv_weight.shape[1]) // BLOCK
    place = lambda i, m: m[slot] * blocks + i
    whole = lambda i, m: (0, 0)
    cube = lambda i, m: (0, 0, 0)
    own = lambda i, m: (0, i)
    conv_at = lambda i, m: (0, place(i, m))
    return in_order(
        functools.partial(project_kernel, cfg, slot),
        grid_spec=dict(
            grid=(blocks,),
            in_specs=[
                pl.BlockSpec(nx.shape, cube),
                pl.BlockSpec(hx.shape, whole),
                pl.BlockSpec((half, BLOCK), own),
                pl.BlockSpec((half, BLOCK), own),
                pl.BlockSpec((in_up.shape[0], BLOCK), lambda i, m: (0, gate_blocks + place(i, m))),
                pl.BlockSpec((conv_weight.shape[0], BLOCK), conv_at),
                pl.BlockSpec((1, BLOCK), conv_at),
                pl.BlockSpec(weight.shape, whole),
                pl.BlockSpec(taps.shape, whole),
                pl.BlockSpec(bt.shape, cube),
            ],
            out_specs=[
                pl.BlockSpec((ext, BLOCK), own),
                pl.BlockSpec((rows, BLOCK), own),
                pl.BlockSpec((streams, bt.shape[1], BLOCK), lambda i, m: (0, 0, i)),
            ],
        ),
        out_shape=[
            jax.ShapeDtypeStruct((ext, cols), LOW),
            jax.ShapeDtypeStruct((rows, cols), F32),
            jax.ShapeDtypeStruct((streams, bt.shape[1], cols), LOW),
        ],
        compiler_params=pltpu.CompilerParams(vmem_limit_bytes=VMEM),
        cost_estimate=lasting(8),
        name="project_conv",
    )(meta, *placed([nx, hx, *weights, in_up, conv_weight, conv_bias, weight, taps, bt]))


def prepare_kernel(cfg, ids_place, adapter_cols, chips, meta_ref, x, before, gain, down, grad, up, normed, nx, hidden_ext, hidden, allowed, d_branch, d_hidden, pieces):
    streams, length, slots, groups, per_group, headdim = cfg
    meta = Meta(meta_ref, groups, slots)
    core = meta_ref[core_at(groups, streams, slots)]
    chip = meta_ref[core_at(groups, streams, slots) + 1]
    s = pl.program_id(0)
    rows = length + HALO
    seg = meta.segment(s, meta.first() - HALO + iota((rows, LANES), 0))
    kind = lax.shift_right_logical(iota((rows, LANES), 1), adapter_cols.bit_length() - 1)
    mask = jnp.zeros((rows, LANES), F32)
    for slot in range(slots):
        mask = jnp.where((seg == slot) & (kind == meta_ref[ids_place + s * slots + slot]), 1.0, mask)
    full = jnp.concatenate([before[...], x[...]], axis=0).astype(F32)
    rs = lax.rsqrt(jnp.mean(full * full, axis=-1, keepdims=True) + EPSILON)
    low = (full * rs * gain[...]).astype(LOW)
    normed[...] = low
    size = pieces.shape[2]
    for p in range(2 * chips):
        pieces[p] = low[:, p * size : (p + 1) * size]
    for k, distance in enumerate(ring_order(chips)):
        at = 2 * lax.rem(chip + distance, chips)
        nx[0, :, k * size : (k + 1) * size] = pieces[at + core]
        nx[1, :, k * size : (k + 1) * size] = pieces[at + 1 - core]
    got = (dot_nt(low, down[...]) * mask).astype(LOW)
    hidden_ext[...] = got
    hidden[...] = got[HALO:]
    allowed[...] = mask[HALO:]
    valid = (seg[HALO:] < slots).astype(F32)
    rows_out = (grad[...].astype(F32) * wide(valid, grad.shape[1])).astype(LOW)
    d_branch[...] = rows_out
    d_hidden[...] = (dot_nt(rows_out, up[...]) * mask[HALO:]).astype(LOW)


def prepare(cfg, meta, ids_place, adapter_cols, x, before, gain, down, grad, up):
    streams, length, slots, groups, per_group, headdim = cfg
    rows, width = x.shape
    chips = lax.axis_size("fsdp") // 2
    ext = streams * (length + HALO)
    ranks = down.shape[0]
    block = lambda r, c: pl.BlockSpec((r, c), lambda i, m: (i, 0))
    whole = lambda a: pl.BlockSpec(a.shape, lambda i, m: (0, 0))
    return in_order(
        functools.partial(prepare_kernel, cfg, ids_place, adapter_cols, chips),
        grid_spec=dict(
            grid=(streams,),
            in_specs=[
                block(length, width), block(HALO, width), whole(gain), whole(down), block(length, width), whole(up),
            ],
            out_specs=[
                block(length + HALO, width),
                pl.BlockSpec((2, length + HALO, width // 2), lambda i, m: (0, i, 0)),
                block(length + HALO, ranks), block(length, ranks), block(length, ranks),
                block(length, width), block(length, ranks),
            ],
            scratch_shapes=[pltpu.VMEM((2 * chips, length + HALO, width // (2 * chips)), LOW)],
        ),
        out_shape=[
            jax.ShapeDtypeStruct((ext, width), LOW),
            jax.ShapeDtypeStruct((2, ext, width // 2), LOW),
            jax.ShapeDtypeStruct((ext, ranks), LOW),
            jax.ShapeDtypeStruct((rows, ranks), LOW),
            jax.ShapeDtypeStruct((rows, ranks), F32),
            jax.ShapeDtypeStruct((rows, width), LOW),
            jax.ShapeDtypeStruct((rows, ranks), LOW),
        ],
        compiler_params=pltpu.CompilerParams(vmem_limit_bytes=VMEM),
        cost_estimate=lasting(3),
        name="prepare",
    )(meta, x, before, gain, down, grad, up)


def decay_kernel(cfg, heads, meta_ref, normed, hidden, w, up, cw, cb, dt_bias, rates, ci, step, slope, taps, logs3, step2, enter2, rest2, weight2, log_t, through, g, gt, b_low, c_low, bt, ct):
    streams, length, slots, groups, per_group, headdim = cfg
    meta = Meta(meta_ref, groups, slots)
    first = meta.first()
    lower = (iota((length, length), 0) >= iota((length, length), 1)).astype(F32)
    per_block = BLOCK // headdim
    state_size = c_low.shape[1]
    bc_cols = 2 * state_size
    both = dot(normed[...], w[...])
    low = (both[:, :bc_cols] + dot(hidden[...], up[...])).astype(LOW)
    ci[...] = low
    for s in range(streams):
        at = slice(s * length, (s + 1) * length)
        ext = slice(s * (HALO + length), (s + 1) * (HALO + length))
        pos = first + iota((length, LANES), 0)
        seg = meta.segment(s, pos)
        lane = iota((length, LANES), 1)
        columns = jnp.zeros((length, LANES), F32)
        for k in range(cw.shape[0] - 1):
            same = meta.segment(s, pos - (cw.shape[0] - 1 - k)) == seg
            columns = jnp.where((lane == k) & same, 1.0, columns)
        taps[at] = columns
        pre = conv_pre(low[ext].astype(F32), tap_masks(columns, cw.shape[0]), cw[...], cb[...])
        bc = pre * sigmoid(pre)
        b_in, c_in = bc[:, :state_size], bc[:, state_size:]
        dt_in = both[ext][HALO:, bc_cols:] + dt_bias[...]
        real = iota((length, LANES), 1) < heads
        st = jnp.where(real, jnp.maximum(dt_in, 0.0) + jnp.log1p(jnp.exp(-jnp.abs(dt_in))), 0.0)
        step[at] = st
        slope[at] = jnp.where(real, sigmoid(dt_in), 0.0)
        prior = meta.scalar_segment(s, first - 1)
        last = meta.scalar_segment(s, first + length - 1)
        seg_u = meta.segment(s, first + iota((length, length), 1))
        seg_t = meta.segment(s, first + iota((length, length), 0))
        logs = dot(lower, -st * rates[...], HIGHEST)
        logs3[at] = packed(logs, heads, 3)
        step2[at] = packed(st, heads, 2)
        enter2[at] = packed(jnp.where(real & (seg == prior), jnp.exp(logs), 0.0), heads, 2)
        remain = jnp.where(real & (seg == last), jnp.exp(logs[length - 1 : length] - logs), 0.0)
        rest2[at] = packed(remain, heads, 2)
        weight2[at] = packed(remain * st, heads, 2)
        kept = jnp.where(prior == last, jnp.exp(logs[length - 1 : length]), 0.0)
        kept = jnp.where(real[:8], jnp.broadcast_to(kept, (8, LANES)), 0.0)
        through[s] = expand(packed(kept, heads, 3), spread_of(0, through.shape[2], headdim, heads, 3))
        turned_logs = jnp.transpose(logs)
        for b in range(log_t.shape[1]):
            log_t[s, b, 0:per_block] = turned_logs[b * per_block : (b + 1) * per_block]
        pairs = jnp.where(seg_u == seg_t, lower, 0.0) * dot_nt(c_in, b_in, HIGHEST)
        g[s] = pairs
        gt[s] = jnp.transpose(pairs)
        b_low[at] = b_in.astype(LOW)
        c_low[at] = c_in.astype(LOW)
        bt[s] = jnp.transpose(b_in).astype(LOW)
        ct[s] = jnp.transpose(c_in).astype(LOW)


def decays(cfg, meta, normed, hidden, w, in_up, conv_weight, conv_bias, dt_bias, rates, heads):
    streams, length, slots, groups, per_group, headdim = cfg
    rows = streams * length
    blocks = heads * headdim // BLOCK
    state_size = (w.shape[1] - LANES) // 2
    row = lambda dtype, cols: jax.ShapeDtypeStruct((rows, cols), dtype)
    cube = lambda dtype, a, b: jax.ShapeDtypeStruct((streams, a, b), dtype)
    outs = [
        jax.ShapeDtypeStruct((hidden.shape[0], 2 * state_size), LOW),
        *[row(F32, LANES)] * 3, row(LOW, 2 * LANES), *[row(LOW, LANES)] * 4,
        jax.ShapeDtypeStruct((streams, blocks, 8, length), F32),
        cube(F32, 8, heads * headdim),
        cube(F32, length, length), cube(F32, length, length),
        row(LOW, state_size), row(LOW, state_size),
        cube(LOW, state_size, length), cube(LOW, state_size, length),
    ]
    zeros = lambda n: (lambda i, m: (0,) * n)
    whole = lambda a: pl.BlockSpec(a.shape, zeros(len(a.shape)))
    last = lambda a: pl.BlockSpec((a.shape[0], BLOCK), lambda i, m: (0, a.shape[1] // BLOCK - 1))
    return in_order(
        functools.partial(decay_kernel, cfg, heads),
        grid_spec=dict(
            grid=(1,),
            in_specs=[
                whole(normed), whole(hidden), whole(w), last(in_up), last(conv_weight), last(conv_bias),
                whole(dt_bias), whole(rates),
            ],
            out_specs=[whole(a) for a in outs],
        ),
        out_shape=outs,
        compiler_params=pltpu.CompilerParams(vmem_limit_bytes=VMEM),
        cost_estimate=lasting(4),
        name="decays",
    )(meta, normed, hidden, w, in_up, conv_weight, conv_bias, dt_bias, rates)


def inside_kernel(cfg, slot, meta_ref, x, step2, logs3, log_t, g, y):
    streams, length, slots, groups, per_group, headdim = cfg
    heads = groups * per_group
    per_block = BLOCK // headdim
    first_head = meta_ref[slot] * per_group + pl.program_id(0) * per_block
    spread = spread_of(first_head, BLOCK, headdim, heads)
    columns = spread_of(first_head, per_block * LANES, LANES, heads, 3)
    half = length // 2
    left = iota((half, LANES), 1) < headdim
    for s in range(streams):
        at = slice(s * length, (s + 1) * length)
        log_col = expand(logs3[at], columns)
        xs = (x[at] * expand(step2[at], spread)).astype(LOW)
        for pair in range(per_block // 2):
            cols = slice(pair * LANES, (pair + 1) * LANES)
            tops, lows = [], []
            for h in (2 * pair, 2 * pair + 1):
                col = log_col[:, h * LANES : (h + 1) * LANES]
                row = log_t[s, 0, h : h + 1]
                tops.append((jnp.exp(jnp.minimum(col[:half] - row[:, :half], 0.0)) * g[s, :half, :half]).astype(LOW))
                lows.append(
                    (jnp.exp(jnp.minimum(wide(col[half:], length) - row, 0.0)) * g[s, half:]).astype(LOW)
                )
            top = dot(jnp.concatenate(tops, axis=0), xs[:half, cols])
            low = dot(jnp.concatenate(lows, axis=0), xs[:, cols])
            start = s * length
            y[start : start + half, cols] = jnp.where(left, top[:half], top[half:])
            y[start + half : start + length, cols] = jnp.where(left, low[:half], low[half:])


def inside(cfg, meta, slot, x, step2, logs3, log_t, g):
    streams, length, slots, groups, per_group, headdim = cfg
    blocks = x.shape[1] // BLOCK
    whole = lambda i, m: (0, 0)
    own = pl.BlockSpec((x.shape[0], BLOCK), lambda i, m: (0, i))
    return in_order(
        functools.partial(inside_kernel, cfg, slot),
        grid_spec=dict(
            grid=(blocks,),
            in_specs=[
                own,
                pl.BlockSpec(step2.shape, whole),
                pl.BlockSpec(logs3.shape, whole),
                pl.BlockSpec((streams, 1, 8, length), lambda i, m: (0, m[slot] * blocks + i, 0, 0)),
                pl.BlockSpec(g.shape, lambda i, m: (0, 0, 0)),
            ],
            out_specs=own,
        ),
        out_shape=jax.ShapeDtypeStruct(x.shape, F32),
        compiler_params=pltpu.CompilerParams(vmem_limit_bytes=VMEM),
        cost_estimate=lasting(5),
        name="inside",
    )(meta, x, step2, logs3, log_t, g)


def gate_kernel(cfg, meta_ref, *refs):
    streams, length, slots, groups, per_group, headdim = cfg
    xs, ys, states = (refs[i * groups : (i + 1) * groups] for i in range(3))
    refs = refs[3 * groups :]
    gate, d_pieces, d_hidden, down, enter2, c_low, ct, skip, gain = refs[:9]
    out_low, d_mixed, d_gate, row_sum, d_state, y_all, v_all, held, d_out, scales = refs[9:]
    width = per_group * headdim
    inner = groups * width
    rows = gate.shape[0]
    per_stream = length // rows
    entering = enter2[...]
    heads = groups * per_group
    squares = jnp.zeros((rows, LANES), F32)
    crossed = jnp.zeros((rows, LANES), F32)
    d_out[...] = jnp.concatenate([d_pieces[p] for p in range(d_pieces.shape[0])], axis=1)

    def fold(values):
        total = values[:, :LANES]
        for j in range(1, values.shape[1] // LANES):
            total = total + values[:, j * LANES : (j + 1) * LANES]
        return total

    for j in range(groups):
        place = meta_ref[j]
        cols = pl.ds(pl.multiple_of(place * width, width), width)
        scale = expand(entering, spread_of(place * per_group, width, headdim, heads))
        scales[:, cols] = scale
        y = ys[j][...] + dot(c_low[...], states[j][0]) * scale
        y_all[:, cols] = y
        gated = gate[:, cols].astype(F32)
        v = (y + skip[:, cols] * xs[j][...]) * (gated * sigmoid(gated))
        v_all[:, cols] = v
        wanted = (d_out[:, cols] + dot(d_hidden[...], down[:, cols])) * gain[:, cols]
        d_out[:, cols] = wanted
        squares = squares + fold(v * v)
        crossed = crossed + fold(v * wanted)
    mean_sq = jnp.sum(squares, axis=1, keepdims=True) / inner
    rs = lax.rsqrt(mean_sq + EPSILON)
    mean_cross = jnp.sum(crossed, axis=1, keepdims=True) / inner
    pull = rs * rs * rs * mean_cross
    sums = jnp.zeros((rows, LANES), F32)
    fresh = pl.program_id(0) % per_stream == 0
    for j in range(groups):
        place = meta_ref[j]
        cols = pl.ds(pl.multiple_of(place * width, width), width)
        gated = gate[:, cols].astype(F32)
        sig = sigmoid(gated)
        v = v_all[:, cols]
        y = y_all[:, cols]
        out_low[:, cols] = (v * rs * gain[:, cols]).astype(LOW)
        d_v = rs * d_out[:, cols] - v * pull
        dm = d_v * (gated * sig)
        d_mixed[:, cols] = dm
        mixed = y + skip[:, cols] * xs[j][...]
        d_gate[:, cols] = (d_v * mixed * (sig * (1.0 + gated * (1.0 - sig)))).astype(LOW)
        sums = sums + sum_heads(
            dm.astype(LOW).astype(F32) * y, gather_of(place * per_group, width, headdim)
        )
        part = dot(ct[0], (dm * scales[:, cols]).astype(LOW))
        before = jnp.where(fresh, 0.0, held[:, cols])
        held[:, cols] = before + part
        d_state[0, :, cols] = (before + part).astype(LOW)
    row_sum[...] = sums


def gated(cfg, meta, xs, ys, states, gate, d_pieces, d_hidden, down, enter_d, c_low, ct, skip, gain):
    streams, length, slots, groups, per_group, headdim = cfg
    rows = 128
    per_stream = length // rows
    width = xs[0].shape[1]
    inner = gate.shape[1]
    state_size = c_low.shape[1]
    total = streams * length
    row = lambda cols: pl.BlockSpec((rows, cols), lambda i, m: (i, 0))
    state = pl.BlockSpec((1, state_size, width), lambda i, m: (i // per_stream, 0, 0))
    flat = pl.BlockSpec((1, inner), lambda i, m: (0, 0))
    return in_order(
        functools.partial(gate_kernel, cfg),
        grid_spec=dict(
            grid=(total // rows,),
            in_specs=[row(width)] * (2 * groups) + [state] * groups
            + [
                row(inner), pl.BlockSpec((d_pieces.shape[0], rows, d_pieces.shape[2]), lambda i, m: (0, i, 0)),
                row(d_hidden.shape[1]), pl.BlockSpec(down.shape, lambda i, m: (0, 0)), row(LANES), row(state_size),
                pl.BlockSpec((1, state_size, rows), lambda i, m: (i // per_stream, 0, i % per_stream)),
                flat, flat,
            ],
            out_specs=[
                row(inner), row(inner), row(inner), row(LANES),
                pl.BlockSpec((1, state_size, inner), lambda i, m: (i // per_stream, 0, 0)),
            ],
            scratch_shapes=[
                pltpu.VMEM((rows, inner), F32), pltpu.VMEM((rows, inner), F32), pltpu.VMEM((state_size, inner), F32),
                pltpu.VMEM((rows, inner), F32), pltpu.VMEM((rows, inner), F32),
            ],
        ),
        out_shape=[
            jax.ShapeDtypeStruct((total, inner), LOW),
            jax.ShapeDtypeStruct((total, inner), F32),
            jax.ShapeDtypeStruct((total, inner), LOW),
            jax.ShapeDtypeStruct((total, LANES), F32),
            jax.ShapeDtypeStruct((streams, state_size, inner), LOW),
        ],
        compiler_params=pltpu.CompilerParams(vmem_limit_bytes=2 * VMEM),
        cost_estimate=lasting(19),
        name="gated",
    )(meta, *placed([*xs, *ys, *states, gate, d_pieces, d_hidden, down, enter_d, c_low, ct, skip, gain], 8 << 20))


def pick(refs, which):
    value = refs[0][...]
    for j in range(1, len(refs)):
        value = jnp.where(which == j, refs[j][...], value)
    return value


def inside_back_kernel(cfg, slot, count, blocks, meta_ref, *refs):
    streams, length, slots, groups, per_group, headdim = cfg
    xs, states = refs[:count], refs[count : 2 * count]
    d_mixed, step2, logs3, enter2, log_t, gt, dxs, dgt, dc = refs[2 * count :]
    heads = groups * per_group
    per_block = BLOCK // headdim
    which = lax.div(pl.program_id(0), blocks)
    first_head = meta_ref[slot + which] * per_group + lax.rem(pl.program_id(0), blocks) * per_block
    spread = spread_of(first_head, BLOCK, headdim, heads)
    columns = spread_of(first_head, per_block * LANES, LANES, heads, 3)
    half = length // 2
    left = iota((half, LANES), 1) < headdim
    x_all, state = pick(xs, which), pick(states, which)

    @pl.when(pl.program_id(0) == 0)
    def _():
        dgt[...] = jnp.zeros_like(dgt)
        dc[...] = jnp.zeros_like(dc)

    for s in range(streams):
        start = s * length
        at = slice(start, start + length)
        log_col = expand(logs3[at], columns)
        x = (x_all[at] * expand(step2[at], spread)).astype(LOW)
        dm = d_mixed[at]
        dm_low = dm.astype(LOW)
        dc[at] += dot_nt((dm * expand(enter2[at], spread)).astype(LOW), state[s])
        sum_top, sum_low = None, None
        for pair in range(per_block // 2):
            cols = slice(pair * LANES, (pair + 1) * LANES)
            decay_top, decay_low, k_top, k_low, x_top, x_low = [], [], [], [], [], []
            for h in (2 * pair, 2 * pair + 1):
                col = log_col[:, h * LANES : (h + 1) * LANES]
                row = log_t[s, 0, h : h + 1]
                top = jnp.exp(jnp.minimum(row - wide(col[:half], length), 0.0))
                low = jnp.exp(jnp.minimum(row[:, half:] - col[half:], 0.0))
                decay_top.append(top)
                decay_low.append(low)
                k_top.append((top * gt[s, :half]).astype(LOW))
                k_low.append((low * gt[s, half:, half:]).astype(LOW))
                mine = left if h % 2 == 0 else jnp.logical_not(left)
                zero = jnp.zeros((half, LANES), LOW)
                x_top.append(jnp.where(mine, x[:half, cols], zero))
                x_low.append(jnp.where(mine, x[half:, cols], zero))
            join = lambda parts: jnp.concatenate(parts, axis=0)
            got_top, got_low = dot(join(k_top), dm_low[:, cols]), dot(join(k_low), dm_low[half:, cols])
            dxs[start : start + half, cols] = jnp.where(left, got_top[:half], got_top[half:])
            dxs[start + half : start + length, cols] = jnp.where(left, got_low[:half], got_low[half:])
            add_top = dot_nt(join(x_top), dm_low[:, cols])
            add_low = dot_nt(join(x_low), dm_low[half:, cols])
            add_top = add_top[:half] * decay_top[0] + add_top[half:] * decay_top[1]
            add_low = add_low[:half] * decay_low[0] + add_low[half:] * decay_low[1]
            sum_top = add_top if sum_top is None else sum_top + add_top
            sum_low = add_low if sum_low is None else sum_low + add_low
        dgt[s, :half] += sum_top
        dgt[s, half:, half:] += sum_low


def inside_back(cfg, meta, slot, xs, d_mixed, step2, logs3, enter2, log_t, gt, states):
    streams, length, slots, groups, per_group, headdim = cfg
    count = len(xs)
    rows, cols = xs[0].shape
    blocks = cols // BLOCK
    state_size = states[0].shape[1]
    whole = lambda i, m: (0, 0)
    cube = lambda i, m: (0, 0, 0)
    at = lambda i, m: m[slot + lax.div(i, blocks)] * blocks + lax.rem(i, blocks)
    local_at = lambda i, j: jnp.clip(i - blocks * j, 0, blocks - 1)
    return in_order(
        functools.partial(inside_back_kernel, cfg, slot, count, blocks),
        grid_spec=dict(
            grid=(count * blocks,),
            in_specs=[pl.BlockSpec((rows, BLOCK), lambda i, m, j=j: (0, local_at(i, j))) for j in range(count)]
            + [
                pl.BlockSpec((streams, state_size, BLOCK), lambda i, m, j=j: (0, 0, local_at(i, j)))
                for j in range(count)
            ]
            + [
                pl.BlockSpec((rows, BLOCK), lambda i, m: (0, at(i, m))),
                pl.BlockSpec(step2.shape, whole),
                pl.BlockSpec(logs3.shape, whole),
                pl.BlockSpec(enter2.shape, whole),
                pl.BlockSpec((streams, 1, 8, length), lambda i, m: (0, at(i, m), 0, 0)),
                pl.BlockSpec(gt.shape, cube),
            ],
            out_specs=[
                pl.BlockSpec((rows, BLOCK), lambda i, m: (0, i)),
                pl.BlockSpec(gt.shape, cube),
                pl.BlockSpec((rows, state_size), whole),
            ],
        ),
        out_shape=[
            jax.ShapeDtypeStruct((rows, count * cols), F32),
            jax.ShapeDtypeStruct(gt.shape, F32),
            jax.ShapeDtypeStruct((rows, state_size), F32),
        ],
        compiler_params=pltpu.CompilerParams(vmem_limit_bytes=VMEM),
        cost_estimate=lasting(12),
        name="inside_back",
    )(meta, *placed([*xs, *states, d_mixed, step2, logs3, enter2, log_t, gt]))


def after_kernel(cfg, blocks, parts, meta_ref, *refs):
    streams, length, slots, groups, per_group, headdim = cfg
    xs, states, cis = (refs[i * groups : (i + 1) * groups] for i in range(3))
    dxss, refs = refs[3 * groups : 3 * groups + parts], refs[3 * groups + parts :]
    d_mixed, d_after, step, step2, rest2, taps, b_low, skip, cw, cb, dci, tail, spill, direct, sums, db = refs
    per_block = BLOCK // headdim
    which = lax.div(pl.program_id(0), blocks)
    first_head = meta_ref[which] * per_group + lax.rem(pl.program_id(0), blocks) * per_block
    spread = spread_of(first_head, BLOCK, headdim, groups * per_group)
    gather = gather_of(first_head, BLOCK, headdim)
    x, state, ci = pick(xs, which), pick(states, which), pick(cis, which)
    dxs = pick(dxss, lax.div(which, groups // parts))

    @pl.when(pl.program_id(0) == 0)
    def _():
        direct[...] = jnp.zeros_like(direct)
        sums[...] = jnp.zeros_like(sums)
        db[...] = jnp.zeros_like(db)

    for s in range(streams):
        at = slice(s * length, (s + 1) * length)
        st = step[at]
        x_s = x[at]
        step_wide = expand(step2[at], spread)
        rest_wide = expand(rest2[at], spread)
        back = rest_wide * dot(b_low[at], d_after[s])
        inner_back = dxs[at]
        x_weighted = x_s * (rest_wide * step_wide)
        db[at] += dot_nt(x_weighted.astype(LOW), d_after[s])
        from_after = dot((x_s * back).astype(LOW), gather)
        direct[at] += dot((x_s * inner_back).astype(LOW), gather) + from_after
        crossed = jnp.sum(d_after[s].astype(F32) * state[s].astype(F32), axis=0, keepdims=True)
        crossed = sum_heads(jnp.broadcast_to(crossed, (8, BLOCK)), gather)
        after_sum = jnp.broadcast_to(jnp.sum(from_after * st, axis=0, keepdims=True), (8, LANES))
        sums[s] += jnp.where(iota((8, LANES), 0) == 0, crossed, after_sum)
        d_x = step_wide * (inner_back + back) + skip[...] * d_mixed[at]
        block = ci[s * (HALO + length) : (s + 1) * (HALO + length)].astype(F32)
        masks = tap_masks(taps[at], cw.shape[0])
        total = conv_back(d_x, block, masks, cw[...], cb[...])
        dci[at] = total[HALO:].astype(LOW)
        tail[s] = total[length:]
        spill[s] = total[HALO - 8 : HALO]


def after(cfg, meta, xs, states, cis, dxss, d_mixed, d_after, step, step2, rest2, taps, b_low, skip, conv_weight, conv_bias):
    streams, length, slots, groups, per_group, headdim = cfg
    rows, cols = xs[0].shape
    blocks = cols // BLOCK
    state_size = states[0].shape[1]
    total_cols = groups * cols
    parts = len(dxss)
    part_blocks = total_cols // parts // BLOCK
    whole = lambda i, m: (0, 0)
    at = lambda i, m: m[lax.div(i, blocks)] * blocks + lax.rem(i, blocks)
    spot = lambda r: pl.BlockSpec((r, BLOCK), lambda i, m: (0, at(i, m)))
    local_at = lambda i, j, n: jnp.clip(i - n * j, 0, n - 1)
    cube = lambda r: pl.BlockSpec((streams, r, BLOCK), lambda i, m: (0, 0, i))
    listed = lambda r, n, many: [pl.BlockSpec((r, BLOCK), lambda i, m, j=j: (0, local_at(i, j, n))) for j in range(many)]
    return in_order(
        functools.partial(after_kernel, cfg, blocks, parts),
        grid_spec=dict(
            grid=(groups * blocks,),
            in_specs=listed(rows, blocks, groups)
            + [
                pl.BlockSpec((streams, state_size, BLOCK), lambda i, m, j=j: (0, 0, local_at(i, j, blocks)))
                for j in range(groups)
            ]
            + listed(cis[0].shape[0], blocks, groups)
            + listed(rows, part_blocks, parts)
            + [
                spot(rows),
                pl.BlockSpec((streams, state_size, BLOCK), lambda i, m: (0, 0, at(i, m))),
                *[pl.BlockSpec(a.shape, whole) for a in (step, step2, rest2, taps, b_low)],
                spot(1), spot(conv_weight.shape[0]), spot(1),
            ],
            out_specs=[
                pl.BlockSpec((rows, BLOCK), lambda i, m: (0, i)), cube(HALO), cube(8),
                pl.BlockSpec((rows, LANES), whole),
                pl.BlockSpec((streams, 8, LANES), lambda i, m: (0, 0, 0)),
                pl.BlockSpec((rows, state_size), whole),
            ],
        ),
        out_shape=[
            jax.ShapeDtypeStruct((rows, total_cols), LOW),
            jax.ShapeDtypeStruct((streams, HALO, total_cols), F32),
            jax.ShapeDtypeStruct((streams, 8, total_cols), F32),
            jax.ShapeDtypeStruct((rows, LANES), F32),
            jax.ShapeDtypeStruct((streams, 8, LANES), F32),
            jax.ShapeDtypeStruct((rows, state_size), F32),
        ],
        compiler_params=pltpu.CompilerParams(vmem_limit_bytes=VMEM),
        cost_estimate=lasting(39),
        name="after",
    )(meta, *placed([*xs, *states, *cis, *dxss, d_mixed, d_after, step, step2, rest2, taps, b_low, skip, conv_weight, conv_bias], 1 << 18))


def finish_kernel(cfg, meta_ref, *refs):
    streams, length, slots, groups, per_group, headdim = cfg
    meta = Meta(meta_ref, groups, slots)
    parts = (len(refs) - 18) // 2
    dgts, dcs, refs = refs[:parts], refs[parts : 2 * parts], refs[2 * parts :]
    db_in, direct_in, sums, row_sum, step, slope, taps, through, rates, b_low, c_low, ci, cw, cb = refs[:14]
    width = through.shape[2]
    pick = (iota((width, LANES), 0) == iota((width, LANES), 1) * headdim).astype(F32)
    kept = [dot(through[s], pick, HIGHEST) for s in range(streams)]
    d_raw, dci, tail, spill = refs[14:]
    upper = (iota((length, length), 0) <= iota((length, length), 1)).astype(F32)
    add = lambda parts, at: functools.reduce(lambda a, b: a + b, [p[at] for p in parts])
    for s in range(streams):
        at = slice(s * length, (s + 1) * length)
        direct = direct_in[at]
        ends = sums[s]
        from_end = kept[s][0:1] * ends[0:1] + ends[1:2]
        d_log = dot(upper, row_sum[at] - step[at] * direct, HIGHEST) + from_end
        d_raw[at] = ((direct - rates[...] * d_log) * slope[at]).astype(LOW)
        seg_u = meta.segment(s, meta.first() + iota((length, length), 0))
        seg_t = meta.segment(s, meta.first() + iota((length, length), 1))
        dgt = jnp.where(seg_u == seg_t, upper, 0.0) * add(dgts, s)
        d_b = db_in[at] + dot(dgt.astype(LOW), c_low[at])
        d_c = add(dcs, at) + dot(jnp.transpose(dgt).astype(LOW), b_low[at])
        block = ci[s * (HALO + length) : (s + 1) * (HALO + length)].astype(F32)
        masks = tap_masks(taps[at], cw.shape[0])
        total = conv_back(jnp.concatenate([d_b, d_c], axis=1), block, masks, cw[...], cb[...])
        dci[at] = total[HALO:].astype(LOW)
        tail[s] = total[length:]
        spill[s] = total[HALO - 8 : HALO]


def finish(cfg, meta, dgts, dcs, db, direct, sums, row_sum, step, slope, taps, through, rates, b_low, c_low, ci, conv_weight, conv_bias, block_at):
    streams, length, slots, groups, per_group, headdim = cfg
    rows = streams * length
    args = [*dgts, *dcs, db, direct, sums, row_sum, step, slope, taps, through, rates, b_low, c_low, ci]
    zeros = lambda n: (lambda i, m: (0,) * n)
    conv_at = lambda i, m: (0, block_at)
    outs = [
        jax.ShapeDtypeStruct((rows, LANES), LOW),
        jax.ShapeDtypeStruct((rows, BLOCK), LOW),
        jax.ShapeDtypeStruct((streams, HALO, BLOCK), F32),
        jax.ShapeDtypeStruct((streams, 8, BLOCK), F32),
    ]
    return in_order(
        functools.partial(finish_kernel, cfg),
        grid_spec=dict(
            grid=(1,),
            in_specs=[pl.BlockSpec(a.shape, zeros(a.ndim)) for a in args]
            + [pl.BlockSpec((conv_weight.shape[0], BLOCK), conv_at), pl.BlockSpec((1, BLOCK), conv_at)],
            out_specs=[pl.BlockSpec(a.shape, zeros(len(a.shape))) for a in outs],
        ),
        out_shape=outs,
        compiler_params=pltpu.CompilerParams(vmem_limit_bytes=VMEM),
        cost_estimate=lasting(4),
        name="finish",
    )(meta, *placed([*args, conv_weight, conv_bias]))


def mend(d, tail, spill):
    streams = tail.shape[0]
    length = d.shape[0] // streams
    parts = []
    for s in range(streams):
        parts.append(d[s * length : (s + 1) * length - HALO])
        added = jnp.concatenate([jnp.zeros((HALO - 8, spill.shape[2]), F32), spill[s]], axis=0)
        parts.append((tail[s] + added).astype(LOW))
    return jnp.concatenate(parts, axis=0)


def turned(a, b):
    return lax.dot_general(a, b, (((0,), (0,)), ((), ())), preferred_element_type=F32)


def back_project_kernel(groups, blocks, core_place, chips, late, meta_ref, *refs):
    if late:
        d_ref, tail, spill, dn_in, dh_in = refs[:5]
        refs = refs[5:]
    else:
        d_ref, refs = refs[0], refs[1:]
    many = 2 * groups if late else 4
    weights, refs = refs[:many], refs[many:]
    hidden, up, dn, dh, g_up = refs[:5]
    held = refs[5] if late else dn
    step = pl.program_id(0)

    @pl.when(step == 0)
    def _():
        held[...] = dn_in[...] if late else jnp.zeros_like(held)
        dh[...] = dh_in[...] if late else jnp.zeros_like(dh)

    d = d_ref[...]
    if late:
        d = mend(d, tail[...], spill[...])
        for j in range(groups):

            @pl.when(lax.div(step, blocks) == j)
            def _():
                held[0] += dot_nt(d, weights[2 * j][...])
                held[1] += dot_nt(d, weights[2 * j + 1][...])
    else:
        near = step < blocks
        held[0] += dot_nt(d, jnp.where(near, weights[0][...], weights[1][0]))
        held[1] += dot_nt(d, jnp.where(near, weights[2][...], weights[3][0]))
    dh[...] += dot_nt(d, up[...])
    g_up[...] = jnp.transpose(turned(hidden[...], d))

    if late:
        core, chip = meta_ref[core_place], meta_ref[core_place + 1]
        size = dn.shape[2]

        @pl.when(step == groups * blocks - 1)
        def _():
            for k, distance in enumerate(ring_order(chips)):
                at = 2 * lax.rem(chip + distance, chips)
                cols = slice(k * size, (k + 1) * size)
                dn[at + core] = held[0, :, cols]
                dn[at + 1 - core] = held[1, :, cols]


def back_project(cfg, meta, ds, weights, hidden, in_up, first_block, late=None):
    streams, length, slots, groups, per_group, headdim = cfg
    rows = hidden.shape[0]
    half, cols = weights[0][0].shape
    blocks = cols // WIDE
    chips = lax.axis_size("fsdp") // 2
    core = core_at(groups, streams, slots)
    at = lambda i, m: m[lax.div(i, blocks)] * blocks + lax.rem(i, blocks)
    local_at = lambda i, j: jnp.clip(i - blocks * j, 0, blocks - 1)
    whole = lambda i, m: (0, 0)
    dn_spec = pl.BlockSpec((2, rows, half), lambda i, m: (0, 0, 0))
    dh_spec = pl.BlockSpec((rows, in_up.shape[0]), whole)
    out_spec = dn_spec
    if late is None:
        in_specs = [pl.BlockSpec((rows, WIDE), lambda i, m: (0, at(i, m)))]
        args = [ds]
    else:
        out_spec = pl.BlockSpec((2 * chips, rows, half // chips), lambda i, m: (0, 0, 0))
        tail, spill, dn, dh = late
        in_specs = [pl.BlockSpec((rows, WIDE), lambda i, m: (0, i))]
        in_specs += [pl.BlockSpec((streams, r, WIDE), lambda i, m: (0, 0, i)) for r in (HALO, 8)]
        in_specs += [dn_spec, dh_spec]
        args = [ds, tail, spill, dn, dh]
    if late is None:
        in_specs += quarter_specs(half, blocks) * 2
        args += [*weights[0], *weights[1]]
    else:
        for j, pair in enumerate(weights):
            for w in pair:
                in_specs.append(pl.BlockSpec((half, WIDE), lambda i, m, j=j: (0, local_at(i, j))))
                args.append(w)
    in_specs += [
        pl.BlockSpec(hidden.shape, whole),
        pl.BlockSpec((in_up.shape[0], WIDE), lambda i, m: (0, first_block + at(i, m))),
    ]
    args += [hidden, in_up]
    return in_order(
        functools.partial(back_project_kernel, groups, blocks, core, chips, late is not None),
        grid_spec=dict(
            grid=(groups * blocks,), in_specs=in_specs,
            out_specs=[out_spec, dh_spec, pl.BlockSpec((WIDE, in_up.shape[0]), lambda i, m: (at(i, m), 0))],
            scratch_shapes=[] if late is None else [pltpu.VMEM((2, rows, half), F32)],
        ),
        out_shape=[
            jax.ShapeDtypeStruct(out_spec.block_shape, F32),
            jax.ShapeDtypeStruct((rows, in_up.shape[0]), F32),
            jax.ShapeDtypeStruct((groups * cols, in_up.shape[0]), F32),
        ],
        compiler_params=pltpu.CompilerParams(vmem_limit_bytes=2 * VMEM),
        cost_estimate=lasting(15),
        name="back_project",
    )(meta, *placed(args))


def close_kernel(meta_ref, dn, dh, d_bc, tail, spill, w_small, d_raw, up, allowed, down, hidden, normed, x_in, gain, grad, out, g_bc, g_down):
    state_cols = d_bc.shape[1]
    width = x_in.shape[1]
    d = mend(d_bc[...], tail[...], spill[...])
    d_hidden = ((dh[...] + dot_nt(d, up[...])) * allowed[...]).astype(LOW)
    x = x_in[...].astype(F32)
    rs = lax.rsqrt(jnp.mean(x * x, axis=-1, keepdims=True) + EPSILON)
    d_normed = jnp.concatenate([dn[p] for p in range(dn.shape[0])], axis=1)
    d_normed = d_normed + dot_nt(d, w_small[:, :state_cols]) + dot_nt(d_raw[...], w_small[:, state_cols:])
    scaled = (d_normed + dot(d_hidden, down[...])) * gain[...]
    cross = jnp.sum(scaled * x, axis=-1, keepdims=True) / width
    out[...] = grad[...].astype(F32) + rs * (scaled - x * (rs * rs * cross))
    add_bc = jnp.transpose(turned(hidden[...], d))
    add_down = jnp.transpose(turned(d_hidden, normed[HALO:]))

    @pl.when(pl.program_id(0) == 0)
    def _():
        g_bc[...] = add_bc
        g_down[...] = add_down

    @pl.when(pl.program_id(0) > 0)
    def _():
        g_bc[...] += add_bc
        g_down[...] += add_down


def close(streams, meta, dn, dh, d_bc, tail, spill, w_small, d_raw, in_up, allowed, down, hidden, normed, x_in, gain, grad):
    rows, width = x_in.shape
    length = rows // streams
    ranks = hidden.shape[1]
    state_cols = d_bc.shape[1]
    row = lambda cols: pl.BlockSpec((length, cols), lambda i, m: (i, 0))
    stack = pl.BlockSpec((dn.shape[0], length, dn.shape[2]), lambda i, m: (0, i, 0))
    whole = lambda a: pl.BlockSpec(a.shape, lambda i, m: (0, 0))
    end = lambda r: pl.BlockSpec((1, r, state_cols), lambda i, m: (i, 0, 0))
    return in_order(
        close_kernel,
        grid_spec=dict(grid=(streams,), in_specs=[
            stack, row(ranks), row(state_cols), end(HALO), end(8), whole(w_small), row(LANES),
            pl.BlockSpec((ranks, state_cols), lambda i, m: (0, in_up.shape[1] // state_cols - 1)),
            row(ranks), whole(down), row(ranks), pl.BlockSpec((length + HALO, width), lambda i, m: (i, 0)), row(width),
            whole(gain), row(width),
        ],
        out_specs=[
            row(width),
            pl.BlockSpec((state_cols, ranks), lambda i, m: (0, 0)),
            pl.BlockSpec((width, ranks), lambda i, m: (0, 0)),
        ]),
        out_shape=[
            jax.ShapeDtypeStruct((rows, width), F32),
            jax.ShapeDtypeStruct((state_cols, ranks), F32),
            jax.ShapeDtypeStruct((width, ranks), F32),
        ],
        compiler_params=pltpu.CompilerParams(vmem_limit_bytes=2 * VMEM),
        cost_estimate=lasting(5),
        name="close",
    )(meta, *placed([dn, dh, d_bc, tail, spill, w_small, d_raw, in_up, allowed, down, hidden, normed, x_in, gain, grad], 8 << 20))


def out_back_kernel(groups, chips, meta_ref, d_branch, w_mine, w_mine_far, w_other, w_other_far, out, ordered):
    cols = w_mine.shape[1]

    @pl.when(pl.program_id(0) == 0)
    def _():
        for j in range(groups):
            ordered[:, j * cols : (j + 1) * cols] = d_branch[:, pl.ds(pl.multiple_of(meta_ref[j] * cols, cols), cols)]

    def product(near, far):
        w = jnp.concatenate([near[...]] + [far[j] for j in range(groups - 1)], axis=1)
        out[0] = dot_nt(ordered[...], w)

    @pl.when(pl.program_id(0) < chips)
    def _():
        product(w_mine, w_mine_far)

    @pl.when(pl.program_id(0) >= chips)
    def _():
        product(w_other, w_other_far)


def out_back(cfg, meta, d_branch, weights):
    streams, length, slots, groups, per_group, headdim = cfg
    rows, width = d_branch.shape
    chips = lax.axis_size("fsdp") // 2
    core = core_at(groups, streams, slots)
    half, cols = weights[0][0].shape
    size = half // chips

    def device(i, m):
        distance = jnp.int32(0)
        for at, value in enumerate(ring_order(chips)):
            distance = jnp.where(lax.rem(i, chips) == at, value, distance)
        return 2 * lax.rem(m[core + 1] + distance, chips) + jnp.where(i < chips, m[core], 1 - m[core])

    block = lambda i, side: jnp.clip(i - side * chips, 0, chips - 1)
    weight = lambda side: [
        pl.BlockSpec((size, cols), lambda i, m: (block(i, side), 0)),
        pl.BlockSpec((groups - 1, size, cols), lambda i, m: (0, block(i, side), 0)),
    ]
    return in_order(
        functools.partial(out_back_kernel, groups, chips),
        grid_spec=dict(
            grid=(2 * chips,),
            in_specs=[pl.BlockSpec((rows, width), lambda i, m: (0, 0)), *weight(0), *weight(1)],
            out_specs=pl.BlockSpec((1, rows, size), lambda i, m: (device(i, m), 0, 0)),
            scratch_shapes=[pltpu.VMEM((rows, width), LOW)],
        ),
        out_shape=jax.ShapeDtypeStruct((2 * chips, rows, size), F32),
        compiler_params=pltpu.CompilerParams(vmem_limit_bytes=VMEM),
        cost_estimate=lasting(8),
        name="out_back",
    )(meta, *placed([d_branch, *weights[0], *weights[1]]))


def out_project_kernel(cfg, chips, meta_ref, out_low, d_branch, x, allowed, down, up, d_hidden, w_mine, w_mine_far, w_other, w_other_far, y, g_down, g_up, pieces, ordered, hidden):
    streams, length, slots, groups, per_group, headdim = cfg
    meta = Meta(meta_ref, groups, slots)
    core = meta_ref[core_at(groups, streams, slots)]
    chip = meta_ref[core_at(groups, streams, slots) + 1]
    size = pieces.shape[2]

    @pl.when(pl.program_id(0) == 0)
    def _():
        for p in range(2 * chips):
            pieces[p] = out_low[:, p * size : (p + 1) * size]
        for k, distance in enumerate(ring_order(chips)):
            at = 2 * lax.rem(chip + distance, chips)
            ordered[0, :, k * size : (k + 1) * size] = pieces[at + core]
            ordered[1, :, k * size : (k + 1) * size] = pieces[at + 1 - core]
        hidden[...] = (dot_nt(out_low[...], down[...]) * allowed[...]).astype(LOW)

    near = pl.program_id(0) == 0
    w_mine = jnp.where(near, w_mine[...], w_mine_far[0])
    w_other = jnp.where(near, w_other[...], w_other_far[0])
    branch = dot(ordered[0], w_mine) + dot(ordered[1], w_other) + dot(hidden[...], up[...])
    for s in range(streams):
        at = slice(s * length, (s + 1) * length)
        seg = meta.segment(s, meta.first() + iota((length, LANES), 0))
        kept = jnp.where(wide(seg, branch.shape[1]) < slots, branch[at], 0.0)
        y[at] = (x[at].astype(F32) + kept).astype(LOW)
    cols = g_down.shape[0]
    start = pl.multiple_of(pl.program_id(0) * cols, cols)
    g_down[...] = jnp.transpose(turned(d_hidden[...], out_low[:, pl.ds(start, cols)]))
    g_up[...] = jnp.transpose(turned(hidden[...], d_branch[...]))


def out_project(cfg, meta, out_low, d_branch, x, allowed, down, up, d_hidden, weights):
    streams, length, slots, groups, per_group, headdim = cfg
    rows, width = x.shape
    inner = out_low.shape[1]
    chips = lax.axis_size("fsdp") // 2
    half, cols = weights[0][0].shape
    ranks = down.shape[0]
    whole = lambda a: pl.BlockSpec(a.shape, lambda i, m: (0, 0))
    turn = pl.BlockSpec((rows, cols), lambda i, m: (0, m[i]))
    far = pl.BlockSpec((1, half, cols), lambda i, m: (jnp.maximum(i - 1, 0), 0, 0))
    return in_order(
        functools.partial(out_project_kernel, cfg, chips),
        grid_spec=dict(
            grid=(groups,),
            in_specs=[
                whole(out_low), turn, turn, whole(allowed), whole(down),
                pl.BlockSpec((ranks, cols), lambda i, m: (0, m[i])), whole(d_hidden),
                whole(weights[0][0]), far, whole(weights[1][0]), far,
            ],
            out_specs=[
                turn,
                pl.BlockSpec((inner // groups, ranks), lambda i, m: (i, 0)),
                pl.BlockSpec((cols, ranks), lambda i, m: (m[i], 0)),
            ],
            scratch_shapes=[
                pltpu.VMEM((2 * chips, rows, half // chips), LOW), pltpu.VMEM((2, rows, half), LOW),
                pltpu.VMEM((rows, ranks), LOW),
            ],
        ),
        out_shape=[
            jax.ShapeDtypeStruct((rows, width), LOW),
            jax.ShapeDtypeStruct((inner, ranks), F32),
            jax.ShapeDtypeStruct((width, ranks), F32),
        ],
        compiler_params=pltpu.CompilerParams(vmem_limit_bytes=2 * VMEM),
        cost_estimate=lasting(10),
        name="out_project",
    )(meta, out_low, d_branch, x, allowed, down, up, d_hidden, *placed([*weights[0], *weights[1]]))


def swap_cores(value):
    return lax.ppermute(value, "fsdp", [(i, i ^ 1) for i in range(lax.axis_size("fsdp"))])


def then(value, earlier):
    return lax.optimization_barrier((value, earlier))[0]


class Scan:
    def __init__(self, own, kept_mine, kept_other, reverse):
        self.count = lax.axis_size("fsdp")
        self.core = core = lax.axis_index("fsdp") % 2
        self.reverse = reverse
        half = own.shape[2] // 2
        take = lambda a, side: lax.dynamic_slice_in_dim(a, side * half, half, 2)
        mine = take(own, core)
        self.other = other = swap_cores(take(own, 1 - core))
        self.early = early = (core == 1) if reverse else (core == 0)
        self.first = jnp.where(early, mine, other).astype(F32)
        second = jnp.where(early, other, mine).astype(F32)
        kept_mine, kept_other = take(kept_mine, core), take(kept_other, core)
        self.kept_first = jnp.where(early, kept_mine, kept_other)
        kept_second = jnp.where(early, kept_other, kept_mine)
        self.added = kept_second * self.first + second
        self.kept_both = self.kept_first * kept_second
        self.hops = self.count // 2 - 1
        self.entering = None

    def hop(self, number, earlier=None):
        send = self.added
        if self.entering is not None:
            send = self.kept_both * self.entering.astype(F32) + send
        send = send.astype(LOW)
        if earlier is not None:
            send = then(send, earlier)
        chip = self.hops - number if self.reverse else number
        route = [(2 * chip + c, 2 * (chip - 1 if self.reverse else chip + 1) + c) for c in (0, 1)]
        got = lax.ppermute(send, "fsdp", route)
        self.entering = got if self.entering is None else self.entering + got
        return got

    def end(self, earlier=None):
        entering = self.entering.astype(F32)
        entering_second = self.kept_first * entering + self.first
        keep = jnp.where(self.early, entering, entering_second).astype(LOW)
        send = jnp.where(self.early, entering_second, entering).astype(LOW)
        if earlier is not None:
            send = then(send, earlier)
        got = swap_cores(send)
        low, high = jnp.concatenate([keep, got], 2), jnp.concatenate([got, keep], 2)
        return jnp.where(self.core == 0, low, high)


def reduce_rows(parts, partial):
    count, replicas = lax.axis_size("fsdp"), lax.axis_size("dp")
    place, replica = lax.axis_index("fsdp"), lax.axis_index("dp")
    chips, chip, core = count // 2, place // 2, place % 2
    sizes = [p.shape[0] // (count * replicas) for p in parts]
    lanes = parts[0].shape[1]
    cut = [p.reshape(chips, 2, replicas, n, lanes) for p, n in zip(parts, sizes)]
    spare = -sum(sizes) % HALO
    if spare:
        cut.append(jnp.zeros((chips, 2, replicas, spare, lanes), F32))
    whole = jnp.concatenate(cut, axis=3)
    pick = lambda a, i, dim: lax.dynamic_index_in_dim(a, i, dim, False)
    total = pick(whole, core, 1) + swap_cores(pick(whole, 1 - core, 1))
    each = total.shape[2]
    partial = partial.reshape(replicas, -1, lanes)
    short = partial.shape[1]
    column = lambda r: jnp.concatenate([pick(total, r, 1).reshape(-1, lanes), pick(partial, r, 0)])
    mine = column(replica)
    for k in range(1, replicas):
        mine = mine + over_dp(column(replica ^ k).astype(LOW), k).astype(F32)
    mine, part_sum = mine[: chips * each].reshape(chips, each, lanes), mine[chips * each :]
    last = pick(mine, chip, 0)
    for k in range(1, chips):
        route = [(i, (i + 2 * k) % count) for i in range(count)]
        last = last + lax.ppermute(pick(mine, (chip + k) % chips, 0).astype(LOW), "fsdp", route).astype(F32)
    last = jnp.concatenate([last, part_sum]).astype(LOW)
    near = jnp.stack([last] + [over_dp(last, k) for k in range(1, replicas)])
    full = jnp.stack([pick(near, replica ^ a, 0) for a in range(replicas)])
    full = full.astype(F32)
    outs, start = [], 0
    for n in sizes:
        outs.append(full[:, start : start + n].reshape(replicas * n, lanes))
        start += n
    return *outs, full[:, each:].reshape(replicas * short, lanes)


def over_dp(value, bit):
    return lax.ppermute(value, "dp", [(i, i ^ bit) for i in range(lax.axis_size("dp"))])


def after_token(value, token):
    return value + token.astype(value.dtype)


class Share:
    def __init__(self, near, mine, other):
        self.near, self.mine, self.other = near, mine, other
        self.one, self.two = over_dp(mine[1:], 1), over_dp(mine[1:], 2)
        part = mine.shape[1] // 2
        self.halves = self.one[:, :part], self.two[:, part:]
        self.last = over_dp(self.halves[0], 2), over_dp(self.halves[1], 1)

    def join(self, j, token=None):
        far, near = (None, self.one, self.two, None)[j], self.near[j]
        if far is None:
            far = jnp.concatenate(self.last, axis=1)
        if token is not None:
            near, far = after_token(near, token), after_token(far, token)
        return flat(jnp.concatenate([near[None], far]))

    def end(self):
        got = jnp.stack([self.join(j) for j in range(1, len(self.near))])
        return (flat(self.mine), got), (flat(self.other), swap_cores(got))


def in_ring(every, token=0):
    count, place = every.shape[0], lax.axis_index("fsdp") + token
    take = lambda k, flip: lax.dynamic_index_in_dim(every, (place + 2 * k) % count ^ flip, 0, False)
    return [jnp.stack([take(k, flip) for k in ring_order(count // 2)]) for flip in (0, 1)]


def flat(chips):
    return chips.reshape(-1, chips.shape[2])


def local(
    block_input, seq_lengths, adapter_ids, norm_gain, w_in, w_dt, conv_weight, conv_bias, dt_bias,
    head_rates, skip_gain, gate_gain, w_out, in_down, in_up, out_down, out_up, out_grad,
):
    streams, length, width = block_input.shape[1:]
    inner = gate_gain.shape[0]
    conv_cols = conv_weight.shape[1]
    heads = dt_bias.shape[0]
    headdim = inner // heads
    state_size = (conv_cols - inner) // 2
    adapters, ranks = in_down.shape[:2]
    in_cols = in_up.shape[2]
    slots = seq_lengths.shape[2]
    rows = streams * length
    groups = lax.axis_size("dp")
    per_group = heads // groups
    group_cols = inner // groups
    cfg = (streams, length, slots, groups, per_group, headdim)
    count = lax.axis_size("fsdp")
    first_pos = lax.axis_index("fsdp") * length
    ends = jnp.cumsum(seq_lengths[0], axis=-1, dtype=jnp.int32)
    place = lax.axis_index("fsdp")
    core, chip, chips = place % 2, place // 2, count // 2
    order = lax.axis_index("dp") ^ jnp.arange(groups, dtype=jnp.int32)
    meta = [order, first_pos[None], ends.reshape(-1), core[None], chip[None], adapter_ids.reshape(-1)]
    meta = jnp.concatenate(meta).astype(jnp.int32)
    ids_place = core_at(groups, streams, slots) + 2
    pad_heads = lambda a: jnp.pad(a, ((0, 0), (0, LANES - heads)))

    quarters = lambda a: [
        lax.dynamic_slice_in_dim(a, order[j] * group_cols, group_cols, 1) for j in range(groups)
    ]
    own_x, own_gate = quarters(w_in[:, inner : 2 * inner]), quarters(w_in[:, :inner])
    small = jnp.concatenate([w_in[:, 2 * inner :], pad_heads(w_dt)], axis=1)
    every = lax.all_gather(jnp.concatenate([own_x[0], small], axis=1), "fsdp")
    w_small = every[:, :, group_cols:].reshape(width, -1)
    every_gate = lax.all_gather(own_gate[0], "fsdp")
    out_cols = width // groups
    own_out = [lax.dynamic_slice_in_dim(w_out, order[j] * out_cols, out_cols, 1) for j in range(groups)]
    every_out = lax.all_gather(own_out[0], "fsdp")
    Order.waits = [own_gate[0], own_out[0]]
    devices = range(count)
    before = lax.ppermute(block_input[0, :, length - HALO :], "fsdp", [(i - 1, i) for i in devices if i > 0])
    down_in = in_down.reshape(adapters * ranks, width)
    up_in = in_up.reshape(adapters * ranks, in_cols)
    down_out = out_down.reshape(adapters * ranks, inner)
    up_out = out_up.reshape(adapters * ranks, width)
    x_rows, grad_rows = block_input.reshape(rows, width), out_grad.reshape(rows, width)
    normed_ext, nx_ext, hidden_ext, hidden_in, allowed, d_branch, d_hidden_out = prepare(
        cfg, meta, ids_place, ranks, x_rows, before.reshape(streams * HALO, width), norm_gain[None],
        down_in, grad_rows, up_out,
    )

    rates = pad_heads(head_rates[None])
    bias_row = conv_bias[None]
    (ci_bc, step, slope, taps, logs3, step2, enter2, rest2, weight2, log_t, through, g, gt, b_low, c_low, bt, ct) = decays(
        cfg, meta, normed_ext, hidden_ext, w_small, up_in, conv_weight, bias_row, pad_heads(dt_bias[None]), rates, heads
    )
    kept_mine = through[:, :1]
    kept_other = swap_cores(kept_mine)
    of_group = lambda a, j: lax.dynamic_slice_in_dim(a, order[j] * group_cols, group_cols, 2)

    w_x, ci, xs, ys, added = [], [], [], [], []

    def enter_group(j, weights):
        w_x.append(weights)
        ci_j, x_j, own = project(cfg, meta, j, nx_ext, hidden_ext, weights, up_in, conv_weight, bias_row, weight2, taps, bt)
        ci.append(ci_j)
        xs.append(x_j)
        added.append(own)

    def scan_of(js):
        kept = [jnp.concatenate([of_group(a, j) for j in js], axis=2) for a in (kept_mine, kept_other)]
        return Scan(jnp.concatenate([added[j] for j in js], axis=2), *kept, False)

    pairs = lambda j: inside(cfg, meta, j, xs[j], step2, logs3, log_t, g)
    x_share = Share(own_x, *in_ring(every[:, :, :group_cols]))
    enter_group(0, (flat(x_share.mine), flat(x_share.other)))
    ys.append(pairs(0))
    near = [x_share.join(j) for j in (1, 2)]
    near = [(w, swap_cores(w)) for w in near]
    wait_for(*x_share.halves)
    enter_group(1, near[0])
    gate_share = Share(own_gate, *in_ring(every_gate, Order.token))
    enter_group(2, near[1])
    scans = [scan_of((0, 1))]
    got = scans[0].hop(0)
    last = x_share.join(3, Order.token)
    wait_for(last, scans[0].other)
    enter_group(3, (last, swap_cores(last)))
    out_share = Share(own_out, *in_ring(every_out, Order.token))
    scans.append(scan_of((2, 3)))
    wait_for(got, scans[1].other)
    ys.append(pairs(1))
    got = [scans[0].hop(1), scans[1].hop(0)]
    wait_for(*gate_share.halves, *got)
    ys.append(pairs(2))
    got = [scans[0].hop(2), scans[1].hop(1)]
    w_gate = gate_share.end()
    wait_for(*got)
    ys.append(pairs(3))
    got = [scans[1].hop(2)]
    for hop in range(3, chips - 1):
        got = [scans[0].hop(hop), scans[1].hop(hop)]
    wait_for(*out_share.halves)
    gate = gate_project(cfg, meta, nx_ext, hidden_ext, w_gate, up_in)
    w_o = out_share.end()
    wait_for(*got)
    pair_states = [scan.end() for scan in scans]
    states = [pair_states[j // 2][:, :, (j % 2) * group_cols : (j % 2 + 1) * group_cols] for j in range(groups)]
    d_pieces = out_back(cfg, meta, d_branch, w_o)

    skip_row = jnp.repeat(skip_gain, headdim)[None]
    out_low, d_mixed, d_gate, row_sum, d_state = gated(
        cfg, meta, xs, ys, states, gate, d_pieces, d_hidden_out, down_out, enter2, c_low, ct, skip_row, gate_gain[None]
    )
    pieces = 2
    wide_cols = inner // pieces
    part = lambda a, j: a[:, :, j * wide_cols : (j + 1) * wide_cols]
    scans = [Scan(part(d_state, j), part(kept_mine, j), part(kept_other, j), True) for j in range(pieces)]
    arrived = [[scan.hop(0) for scan in scans]]

    wait_for(*[scan.other for scan in scans])

    block_output, g_out_down, g_out_up = out_project(
        cfg, meta, out_low, d_branch, x_rows, allowed, down_out, up_out, d_hidden_out, w_o
    )
    wait_for(*arrived[0])
    early = back_project(cfg, meta, d_gate, w_gate, hidden_in, up_in, 0)
    for hop in range(1, chips - 1):
        arrived.append([scan.hop(hop) for scan in scans])
    half_groups = groups // 2
    inside_parts = []
    for p in (0, 1):
        wait_for(*arrived[p + 1])
        js = slice(p * half_groups, (p + 1) * half_groups)
        inside_parts.append(
            inside_back(cfg, meta, p * half_groups, xs[js], d_mixed, step2, logs3, enter2, log_t, gt, states[js])
        )
    dxs, dgts, dcs = zip(*inside_parts)
    d_after = jnp.concatenate([scan.end() for scan in scans], axis=2)
    by_device = lambda a: a.reshape(count, a.shape[0] // count, a.shape[1])
    out_sums = jnp.concatenate([by_device(g_out_down), by_device(g_out_up)], axis=1)
    out_sums = lax.psum_scatter(then(out_sums, dxs[1]), "fsdp", scatter_dimension=0, tiled=False)
    dci, tail, spill, direct, sums, db = after(
        cfg, meta, xs, states, ci, dxs, d_mixed, d_after, step, step2, rest2, taps, b_low, skip_row, conv_weight, bias_row
    )
    to_earlier = lambda a: lax.ppermute(a, "fsdp", [(i, i - 1) for i in devices if i > 0])
    spill = to_earlier(spill)
    d_raw, dci_bc, tail_bc, spill_bc = finish(
        cfg, meta, dgts, dcs, db, direct, sums, row_sum, step, slope, taps, through, rates, b_low, c_low,
        ci_bc, conv_weight, bias_row, inner // BLOCK,
    )
    spill_bc = to_earlier(spill_bc)
    late = back_project(
        cfg, meta, dci, w_x, hidden_in, up_in, inner // WIDE, (tail, spill, early[0], early[1])
    )
    input_grad, g_bc, g_in_down = close(
        streams, meta, late[0], late[1], dci_bc, tail_bc, spill_bc, w_small, d_raw, up_in, allowed, down_in, hidden_in,
        normed_ext, x_rows, norm_gain[None], grad_rows,
    )
    in_down_sum, in_up_sum, out_sums = reduce_rows(
        [g_in_down, jnp.concatenate([early[2], late[2], g_bc], axis=0)], out_sums
    )
    out_sums = jnp.split(out_sums, [inner // count], axis=0)
    totals = [a.T.reshape(adapters, ranks, -1) for a in (in_down_sum, in_up_sum, *out_sums)]
    return (block_output.reshape(1, streams, length, width), input_grad.reshape(1, streams, length, width), *totals)


def solution(mesh):
    rows = P("dp", None, "fsdp", None)
    cut = P("fsdp", None)
    per_group = P("dp", None, None)
    in_specs = (
        rows, per_group, per_group, P(), cut, cut, P(), P(), P(), P(), P(), P(), cut, P(), P(), P(), P(), rows,
    )
    out_specs = (rows, rows) + (P(None, None, "fsdp"),) * 4
    return jax.shard_map(local, mesh=mesh, in_specs=in_specs, out_specs=out_specs, check_vma=False)
```

```python
import functools

import jax
import jax.numpy as jnp
from jax import lax
from jax.experimental import pallas as pl
from jax.experimental.pallas import tpu as pltpu
from jax.sharding import PartitionSpec as P

EPSILON = 1e-05
HIGHEST = lax.Precision.HIGHEST
F32, LOW = jnp.float32, jnp.bfloat16
HALO = 16
LANES = 128
BLOCK = 256
WIDE = 768
VMEM = 16 * 1024 * 1024


def lasting(us):
    return pl.CostEstimate(flops=int(us * 1.15e9), bytes_accessed=1000000, transcendentals=0)


class Order:
    waits = []
    token = None


def in_order(kernel, *, grid_spec, out_shape, compiler_params, cost_estimate, name):
    def call(meta, *args):
        waits = Order.waits
        skip = len(waits)
        specs = [pl.BlockSpec(memory_space=pl.ANY)] * skip + list(grid_spec["in_specs"])
        single = not isinstance(out_shape, (list, tuple))
        shapes = [out_shape] if single else list(out_shape)
        out_specs = [grid_spec["out_specs"]] if single else list(grid_spec["out_specs"])
        token_at = skip + len(args) + len(shapes)

        def body(meta_ref, *refs):
            refs[token_at][...] = jnp.zeros((8, LANES), jnp.int32)
            kernel(meta_ref, *refs[skip:token_at], *refs[token_at + 1 :])

        outs = pl.pallas_call(
            body,
            grid_spec=pltpu.PrefetchScalarGridSpec(
                num_scalar_prefetch=1,
                grid=grid_spec["grid"],
                in_specs=specs,
                out_specs=out_specs + [pl.BlockSpec((8, LANES), lambda i, m: (0, 0))],
                scratch_shapes=grid_spec.get("scratch_shapes", ()),
            ),
            out_shape=shapes + [jax.ShapeDtypeStruct((8, LANES), jnp.int32)],
            compiler_params=compiler_params,
            cost_estimate=cost_estimate,
            name=name,
        )(meta, *waits, *args)
        Order.waits = [outs[-1]]
        Order.token = outs[-1][0, 0]
        return outs[0] if single else outs[:-1]

    return call


def wait_for(*arrays):
    Order.waits = Order.waits + list(arrays)


def dot(a, b, precision=None):
    return lax.dot_general(
        a, b, (((1,), (0,)), ((), ())), precision=precision, preferred_element_type=F32
    )


def dot_nt(a, b, precision=None):
    return lax.dot_general(
        a, b, (((1,), (1,)), ((), ())), precision=precision, preferred_element_type=F32
    )


def iota(shape, dim):
    return lax.broadcasted_iota(jnp.int32, shape, dim)


def packed(values, heads, terms):
    lane = iota(values.shape, 1)
    total, rest, wrapped = None, values, None
    for term in range(terms):
        part = rest.astype(LOW).astype(F32)
        rest = rest - part
        if term == 0:
            total = part
        elif (term + 1) * heads <= LANES:
            total = total + pltpu.roll(part, term * heads, 1)
        else:
            moved = pltpu.roll(part, term * heads, 1)
            total = total + jnp.where(lane >= term * heads, moved, 0.0)
            wrapped = jnp.where(lane < term * heads, moved, 0.0)
    if wrapped is not None:
        total = jnp.concatenate([total, wrapped], axis=1)
    return total.astype(LOW)


def expand(values, spread):
    return dot(values, spread)


def sigmoid(v):
    return 0.5 + 0.5 * jnp.tanh(0.5 * v)


def core_at(groups, streams, slots):
    return groups + 1 + streams * slots


def ring_order(chips):
    order = [0]
    for k in range(1, chips // 2 + 1):
        order += [k, chips - k] if k != chips - k else [k]
    return order


def placed(arrays, limit=1 << 20):
    return [
        pltpu.with_memory_space_constraint(a, pltpu.HBM) if a.size * a.dtype.itemsize > limit else a for a in arrays
    ]


class Meta:
    def __init__(self, ref, groups, slots):
        self.ref, self.groups, self.slots = ref, groups, slots

    def first(self):
        return self.ref[self.groups]

    def end(self, stream, slot):
        return self.ref[self.groups + 1 + stream * self.slots + slot]

    def segment(self, stream, pos):
        seg = jnp.zeros_like(pos)
        for slot in range(self.slots):
            seg = seg + (pos >= self.end(stream, slot)).astype(jnp.int32)
        return jnp.where(pos < 0, -1, seg)

    def scalar_segment(self, stream, pos):
        seg = jnp.int32(0)
        for slot in range(self.slots):
            seg = seg + jnp.where(pos >= self.end(stream, slot), 1, 0)
        return jnp.where(pos < 0, -1, seg)


def tap_masks(columns, taps):
    return [jnp.broadcast_to(columns[:, k : k + 1], columns.shape) for k in range(taps - 1)]


def wide(mask, cols):
    return jnp.concatenate([mask] * (cols // LANES), axis=1)


def conv_pre(block, masks, cw, cb):
    taps, cols = cw.shape
    total = cb + cw[taps - 1 : taps] * block[HALO:]
    for k in range(taps - 1):
        moved = pltpu.roll(block, taps - 1 - k, 0)[HALO:]
        total = total + cw[k : k + 1] * moved * wide(masks[k], cols)
    return total


def conv_back(d_out, block, masks, cw, cb):
    taps, cols = cw.shape
    pre = conv_pre(block, masks, cw, cb)
    sig = sigmoid(pre)
    d_pre = d_out * (sig * (1.0 + pre * (1.0 - sig)))
    total = jnp.concatenate([jnp.zeros((HALO, cols), F32), cw[taps - 1 : taps] * d_pre], axis=0)
    rows = total.shape[0]
    for k in range(taps - 1):
        part = cw[k : k + 1] * d_pre * wide(masks[k], cols)
        part = jnp.concatenate([jnp.zeros((HALO, cols), F32), part], axis=0)
        total = total + pltpu.roll(part, rows - (taps - 1 - k), 0)
    return total


def spread_of(first_head, cols, per_head, heads, terms=2):
    shape = (LANES * (1 if terms * heads <= LANES else 2), cols)
    head = lax.shift_right_logical(iota(shape, 1), per_head.bit_length() - 1) + first_head
    row = iota(shape, 0)
    hit = row == head
    for term in range(1, terms):
        hit = hit | (row == head + term * heads)
    return hit.astype(LOW)


def gather_of(first_head, cols, per_head):
    head = lax.shift_right_logical(iota((cols, LANES), 0), per_head.bit_length() - 1) + first_head
    return (iota((cols, LANES), 1) == head).astype(LOW)


def sum_heads(values, gather):
    part = values.astype(LOW)
    rest = (values - part.astype(F32)).astype(LOW)
    return dot(part, gather) + dot(rest, gather)


def halves_product(nx, hx, w_mine, w_other, up):
    return (dot(nx[0], w_mine) + dot(nx[1], w_other) + dot(hx[...], up[...])).astype(LOW)


def quarter_specs(half, blocks):
    far = lambda i: jnp.maximum(i - blocks, 0)
    return [
        pl.BlockSpec((half, WIDE), lambda i, m: (0, jnp.minimum(i, blocks - 1))),
        pl.BlockSpec((1, half, WIDE), lambda i, m: (lax.div(far(i), blocks), 0, lax.rem(far(i), blocks))),
    ]


def gate_project_kernel(cfg, blocks, meta_ref, nx, hx, w_mine, w_mine_far, w_other, w_other_far, up, out):
    streams, length, slots, groups, per_group, headdim = cfg
    near = pl.program_id(0) < blocks
    w_mine = jnp.where(near, w_mine[...], w_mine_far[0])
    w_other = jnp.where(near, w_other[...], w_other_far[0])
    full = halves_product(nx, hx, w_mine, w_other, up)
    for s in range(streams):
        out[s * length : (s + 1) * length] = full[s * (HALO + length) + HALO : (s + 1) * (HALO + length)]


def gate_project(cfg, meta, nx, hx, weights, in_up):
    streams, length, slots, groups, per_group, headdim = cfg
    half, cols = weights[0][0].shape
    rows = streams * length
    blocks = cols // WIDE
    at = lambda i, m: m[lax.div(i, blocks)] * blocks + lax.rem(i, blocks)
    return in_order(
        functools.partial(gate_project_kernel, cfg, blocks),
        grid_spec=dict(
            grid=(groups * blocks,),
            in_specs=[
                pl.BlockSpec(nx.shape, lambda i, m: (0, 0, 0)),
                pl.BlockSpec(hx.shape, lambda i, m: (0, 0)),
                *quarter_specs(half, blocks) * 2,
                pl.BlockSpec((in_up.shape[0], WIDE), lambda i, m: (0, at(i, m))),
            ],
            out_specs=pl.BlockSpec((rows, WIDE), lambda i, m: (0, at(i, m))),
        ),
        out_shape=jax.ShapeDtypeStruct((rows, groups * cols), LOW),
        compiler_params=pltpu.CompilerParams(vmem_limit_bytes=2 * VMEM),
        cost_estimate=lasting(9),
        name="project_gate",
    )(meta, *placed([nx, hx, *weights[0], *weights[1], in_up]))


def project_kernel(cfg, slot, meta_ref, nx, hx, w_mine, w_other, up, cw, cb, weight, taps, bt, ci, x_out, state):
    streams, length, slots, groups, per_group, headdim = cfg
    per_block = BLOCK // headdim
    first_head = meta_ref[slot] * per_group + pl.program_id(0) * per_block
    spread = spread_of(first_head, BLOCK, headdim, groups * per_group)
    low = halves_product(nx, hx, w_mine[...], w_other[...], up)
    ci[...] = low
    full = low.astype(F32)
    for s in range(streams):
        block = full[s * (HALO + length) : (s + 1) * (HALO + length)]
        masks = tap_masks(taps[s * length : (s + 1) * length], cw.shape[0])
        pre = conv_pre(block, masks, cw[...], cb[...])
        x = pre * sigmoid(pre)
        x_out[s * length : (s + 1) * length] = x
        scale = expand(weight[s * length : (s + 1) * length], spread)
        state[s] = dot(bt[s], (x * scale).astype(LOW)).astype(LOW)


def project(cfg, meta, slot, nx, hx, weights, in_up, conv_weight, conv_bias, weight, taps, bt):
    streams, length, slots, groups, per_group, headdim = cfg
    rows = streams * length
    ext = hx.shape[0]
    half, cols = weights[0].shape
    blocks = cols // BLOCK
    gate_blocks = (in_up.shape[1] - conv_weight.shape[1]) // BLOCK
    place = lambda i, m: m[slot] * blocks + i
    whole = lambda i, m: (0, 0)
    cube = lambda i, m: (0, 0, 0)
    own = lambda i, m: (0, i)
    conv_at = lambda i, m: (0, place(i, m))
    return in_order(
        functools.partial(project_kernel, cfg, slot),
        grid_spec=dict(
            grid=(blocks,),
            in_specs=[
                pl.BlockSpec(nx.shape, cube),
                pl.BlockSpec(hx.shape, whole),
                pl.BlockSpec((half, BLOCK), own),
                pl.BlockSpec((half, BLOCK), own),
                pl.BlockSpec((in_up.shape[0], BLOCK), lambda i, m: (0, gate_blocks + place(i, m))),
                pl.BlockSpec((conv_weight.shape[0], BLOCK), conv_at),
                pl.BlockSpec((1, BLOCK), conv_at),
                pl.BlockSpec(weight.shape, whole),
                pl.BlockSpec(taps.shape, whole),
                pl.BlockSpec(bt.shape, cube),
            ],
            out_specs=[
                pl.BlockSpec((ext, BLOCK), own),
                pl.BlockSpec((rows, BLOCK), own),
                pl.BlockSpec((streams, bt.shape[1], BLOCK), lambda i, m: (0, 0, i)),
            ],
        ),
        out_shape=[
            jax.ShapeDtypeStruct((ext, cols), LOW),
            jax.ShapeDtypeStruct((rows, cols), F32),
            jax.ShapeDtypeStruct((streams, bt.shape[1], cols), LOW),
        ],
        compiler_params=pltpu.CompilerParams(vmem_limit_bytes=VMEM),
        cost_estimate=lasting(8),
        name="project_conv",
    )(meta, *placed([nx, hx, *weights, in_up, conv_weight, conv_bias, weight, taps, bt]))


def prepare_kernel(cfg, ids_place, adapter_cols, chips, meta_ref, x, before, gain, down, grad, up, normed, nx, hidden_ext, hidden, allowed, d_branch, d_hidden, pieces):
    streams, length, slots, groups, per_group, headdim = cfg
    meta = Meta(meta_ref, groups, slots)
    core = meta_ref[core_at(groups, streams, slots)]
    chip = meta_ref[core_at(groups, streams, slots) + 1]
    s = pl.program_id(0)
    rows = length + HALO
    seg = meta.segment(s, meta.first() - HALO + iota((rows, LANES), 0))
    kind = lax.shift_right_logical(iota((rows, LANES), 1), adapter_cols.bit_length() - 1)
    mask = jnp.zeros((rows, LANES), F32)
    for slot in range(slots):
        mask = jnp.where((seg == slot) & (kind == meta_ref[ids_place + s * slots + slot]), 1.0, mask)
    full = jnp.concatenate([before[...], x[...]], axis=0).astype(F32)
    rs = lax.rsqrt(jnp.mean(full * full, axis=-1, keepdims=True) + EPSILON)
    low = (full * rs * gain[...]).astype(LOW)
    normed[...] = low
    size = pieces.shape[2]
    for p in range(2 * chips):
        pieces[p] = low[:, p * size : (p + 1) * size]
    for k, distance in enumerate(ring_order(chips)):
        at = 2 * lax.rem(chip + distance, chips)
        nx[0, :, k * size : (k + 1) * size] = pieces[at + core]
        nx[1, :, k * size : (k + 1) * size] = pieces[at + 1 - core]
    got = (dot_nt(low, down[...]) * mask).astype(LOW)
    hidden_ext[...] = got
    hidden[...] = got[HALO:]
    allowed[...] = mask[HALO:]
    valid = (seg[HALO:] < slots).astype(F32)
    rows_out = (grad[...].astype(F32) * wide(valid, grad.shape[1])).astype(LOW)
    d_branch[...] = rows_out
    d_hidden[...] = (dot_nt(rows_out, up[...]) * mask[HALO:]).astype(LOW)


def prepare(cfg, meta, ids_place, adapter_cols, x, before, gain, down, grad, up):
    streams, length, slots, groups, per_group, headdim = cfg
    rows, width = x.shape
    chips = lax.axis_size("fsdp") // 2
    ext = streams * (length + HALO)
    ranks = down.shape[0]
    block = lambda r, c: pl.BlockSpec((r, c), lambda i, m: (i, 0))
    whole = lambda a: pl.BlockSpec(a.shape, lambda i, m: (0, 0))
    return in_order(
        functools.partial(prepare_kernel, cfg, ids_place, adapter_cols, chips),
        grid_spec=dict(
            grid=(streams,),
            in_specs=[
                block(length, width), block(HALO, width), whole(gain), whole(down), block(length, width), whole(up),
            ],
            out_specs=[
                block(length + HALO, width),
                pl.BlockSpec((2, length + HALO, width // 2), lambda i, m: (0, i, 0)),
                block(length + HALO, ranks), block(length, ranks), block(length, ranks),
                block(length, width), block(length, ranks),
            ],
            scratch_shapes=[pltpu.VMEM((2 * chips, length + HALO, width // (2 * chips)), LOW)],
        ),
        out_shape=[
            jax.ShapeDtypeStruct((ext, width), LOW),
            jax.ShapeDtypeStruct((2, ext, width // 2), LOW),
            jax.ShapeDtypeStruct((ext, ranks), LOW),
            jax.ShapeDtypeStruct((rows, ranks), LOW),
            jax.ShapeDtypeStruct((rows, ranks), F32),
            jax.ShapeDtypeStruct((rows, width), LOW),
            jax.ShapeDtypeStruct((rows, ranks), LOW),
        ],
        compiler_params=pltpu.CompilerParams(vmem_limit_bytes=VMEM),
        cost_estimate=lasting(3),
        name="prepare",
    )(meta, x, before, gain, down, grad, up)


def decay_kernel(cfg, heads, meta_ref, normed, hidden, w, up, cw, cb, dt_bias, rates, ci, step, slope, taps, logs3, step2, enter2, rest2, weight2, log_t, through, g, gt, b_low, c_low, bt, ct):
    streams, length, slots, groups, per_group, headdim = cfg
    meta = Meta(meta_ref, groups, slots)
    first = meta.first()
    lower = (iota((length, length), 0) >= iota((length, length), 1)).astype(F32)
    per_block = BLOCK // headdim
    state_size = c_low.shape[1]
    bc_cols = 2 * state_size
    both = dot(normed[...], w[...])
    low = (both[:, :bc_cols] + dot(hidden[...], up[...])).astype(LOW)
    ci[...] = low
    for s in range(streams):
        at = slice(s * length, (s + 1) * length)
        ext = slice(s * (HALO + length), (s + 1) * (HALO + length))
        pos = first + iota((length, LANES), 0)
        seg = meta.segment(s, pos)
        lane = iota((length, LANES), 1)
        columns = jnp.zeros((length, LANES), F32)
        for k in range(cw.shape[0] - 1):
            same = meta.segment(s, pos - (cw.shape[0] - 1 - k)) == seg
            columns = jnp.where((lane == k) & same, 1.0, columns)
        taps[at] = columns
        pre = conv_pre(low[ext].astype(F32), tap_masks(columns, cw.shape[0]), cw[...], cb[...])
        bc = pre * sigmoid(pre)
        b_in, c_in = bc[:, :state_size], bc[:, state_size:]
        dt_in = both[ext][HALO:, bc_cols:] + dt_bias[...]
        real = iota((length, LANES), 1) < heads
        st = jnp.where(real, jnp.maximum(dt_in, 0.0) + jnp.log1p(jnp.exp(-jnp.abs(dt_in))), 0.0)
        step[at] = st
        slope[at] = jnp.where(real, sigmoid(dt_in), 0.0)
        prior = meta.scalar_segment(s, first - 1)
        last = meta.scalar_segment(s, first + length - 1)
        seg_u = meta.segment(s, first + iota((length, length), 1))
        seg_t = meta.segment(s, first + iota((length, length), 0))
        logs = dot(lower, -st * rates[...], HIGHEST)
        logs3[at] = packed(logs, heads, 3)
        step2[at] = packed(st, heads, 2)
        enter2[at] = packed(jnp.where(real & (seg == prior), jnp.exp(logs), 0.0), heads, 2)
        remain = jnp.where(real & (seg == last), jnp.exp(logs[length - 1 : length] - logs), 0.0)
        rest2[at] = packed(remain, heads, 2)
        weight2[at] = packed(remain * st, heads, 2)
        kept = jnp.where(prior == last, jnp.exp(logs[length - 1 : length]), 0.0)
        kept = jnp.where(real[:8], jnp.broadcast_to(kept, (8, LANES)), 0.0)
        through[s] = expand(packed(kept, heads, 3), spread_of(0, through.shape[2], headdim, heads, 3))
        turned_logs = jnp.transpose(logs)
        for b in range(log_t.shape[1]):
            log_t[s, b, 0:per_block] = turned_logs[b * per_block : (b + 1) * per_block]
        pairs = jnp.where(seg_u == seg_t, lower, 0.0) * dot_nt(c_in, b_in, HIGHEST)
        g[s] = pairs
        gt[s] = jnp.transpose(pairs)
        b_low[at] = b_in.astype(LOW)
        c_low[at] = c_in.astype(LOW)
        bt[s] = jnp.transpose(b_in).astype(LOW)
        ct[s] = jnp.transpose(c_in).astype(LOW)


def decays(cfg, meta, normed, hidden, w, in_up, conv_weight, conv_bias, dt_bias, rates, heads):
    streams, length, slots, groups, per_group, headdim = cfg
    rows = streams * length
    blocks = heads * headdim // BLOCK
    state_size = (w.shape[1] - LANES) // 2
    row = lambda dtype, cols: jax.ShapeDtypeStruct((rows, cols), dtype)
    cube = lambda dtype, a, b: jax.ShapeDtypeStruct((streams, a, b), dtype)
    outs = [
        jax.ShapeDtypeStruct((hidden.shape[0], 2 * state_size), LOW),
        *[row(F32, LANES)] * 3, row(LOW, 2 * LANES), *[row(LOW, LANES)] * 4,
        jax.ShapeDtypeStruct((streams, blocks, 8, length), F32),
        cube(F32, 8, heads * headdim),
        cube(F32, length, length), cube(F32, length, length),
        row(LOW, state_size), row(LOW, state_size),
        cube(LOW, state_size, length), cube(LOW, state_size, length),
    ]
    zeros = lambda n: (lambda i, m: (0,) * n)
    whole = lambda a: pl.BlockSpec(a.shape, zeros(len(a.shape)))
    last = lambda a: pl.BlockSpec((a.shape[0], BLOCK), lambda i, m: (0, a.shape[1] // BLOCK - 1))
    return in_order(
        functools.partial(decay_kernel, cfg, heads),
        grid_spec=dict(
            grid=(1,),
            in_specs=[
                whole(normed), whole(hidden), whole(w), last(in_up), last(conv_weight), last(conv_bias),
                whole(dt_bias), whole(rates),
            ],
            out_specs=[whole(a) for a in outs],
        ),
        out_shape=outs,
        compiler_params=pltpu.CompilerParams(vmem_limit_bytes=VMEM),
        cost_estimate=lasting(4),
        name="decays",
    )(meta, normed, hidden, w, in_up, conv_weight, conv_bias, dt_bias, rates)


def inside_kernel(cfg, slot, meta_ref, x, step2, logs3, log_t, g, y):
    streams, length, slots, groups, per_group, headdim = cfg
    heads = groups * per_group
    per_block = BLOCK // headdim
    first_head = meta_ref[slot] * per_group + pl.program_id(0) * per_block
    spread = spread_of(first_head, BLOCK, headdim, heads)
    columns = spread_of(first_head, per_block * LANES, LANES, heads, 3)
    half = length // 2
    left = iota((half, LANES), 1) < headdim
    for s in range(streams):
        at = slice(s * length, (s + 1) * length)
        log_col = expand(logs3[at], columns)
        xs = (x[at] * expand(step2[at], spread)).astype(LOW)
        for pair in range(per_block // 2):
            cols = slice(pair * LANES, (pair + 1) * LANES)
            tops, lows = [], []
            for h in (2 * pair, 2 * pair + 1):
                col = log_col[:, h * LANES : (h + 1) * LANES]
                row = log_t[s, 0, h : h + 1]
                tops.append((jnp.exp(jnp.minimum(col[:half] - row[:, :half], 0.0)) * g[s, :half, :half]).astype(LOW))
                lows.append(
                    (jnp.exp(jnp.minimum(wide(col[half:], length) - row, 0.0)) * g[s, half:]).astype(LOW)
                )
            top = dot(jnp.concatenate(tops, axis=0), xs[:half, cols])
            low = dot(jnp.concatenate(lows, axis=0), xs[:, cols])
            start = s * length
            y[start : start + half, cols] = jnp.where(left, top[:half], top[half:])
            y[start + half : start + length, cols] = jnp.where(left, low[:half], low[half:])


def inside(cfg, meta, slot, x, step2, logs3, log_t, g):
    streams, length, slots, groups, per_group, headdim = cfg
    blocks = x.shape[1] // BLOCK
    whole = lambda i, m: (0, 0)
    own = pl.BlockSpec((x.shape[0], BLOCK), lambda i, m: (0, i))
    return in_order(
        functools.partial(inside_kernel, cfg, slot),
        grid_spec=dict(
            grid=(blocks,),
            in_specs=[
                own,
                pl.BlockSpec(step2.shape, whole),
                pl.BlockSpec(logs3.shape, whole),
                pl.BlockSpec((streams, 1, 8, length), lambda i, m: (0, m[slot] * blocks + i, 0, 0)),
                pl.BlockSpec(g.shape, lambda i, m: (0, 0, 0)),
            ],
            out_specs=own,
        ),
        out_shape=jax.ShapeDtypeStruct(x.shape, F32),
        compiler_params=pltpu.CompilerParams(vmem_limit_bytes=VMEM),
        cost_estimate=lasting(5),
        name="inside",
    )(meta, x, step2, logs3, log_t, g)


def gate_kernel(cfg, meta_ref, *refs):
    streams, length, slots, groups, per_group, headdim = cfg
    xs, ys, states = (refs[i * groups : (i + 1) * groups] for i in range(3))
    refs = refs[3 * groups :]
    gate, d_pieces, d_hidden, down, enter2, c_low, ct, skip, gain = refs[:9]
    out_low, d_mixed, d_gate, row_sum, d_state, y_all, v_all, held, d_out, scales = refs[9:]
    width = per_group * headdim
    inner = groups * width
    rows = gate.shape[0]
    per_stream = length // rows
    entering = enter2[...]
    heads = groups * per_group
    squares = jnp.zeros((rows, LANES), F32)
    crossed = jnp.zeros((rows, LANES), F32)
    d_out[...] = jnp.concatenate([d_pieces[p] for p in range(d_pieces.shape[0])], axis=1)

    def fold(values):
        total = values[:, :LANES]
        for j in range(1, values.shape[1] // LANES):
            total = total + values[:, j * LANES : (j + 1) * LANES]
        return total

    for j in range(groups):
        place = meta_ref[j]
        cols = pl.ds(pl.multiple_of(place * width, width), width)
        scale = expand(entering, spread_of(place * per_group, width, headdim, heads))
        scales[:, cols] = scale
        y = ys[j][...] + dot(c_low[...], states[j][0]) * scale
        y_all[:, cols] = y
        gated = gate[:, cols].astype(F32)
        v = (y + skip[:, cols] * xs[j][...]) * (gated * sigmoid(gated))
        v_all[:, cols] = v
        wanted = (d_out[:, cols] + dot(d_hidden[...], down[:, cols])) * gain[:, cols]
        d_out[:, cols] = wanted
        squares = squares + fold(v * v)
        crossed = crossed + fold(v * wanted)
    mean_sq = jnp.sum(squares, axis=1, keepdims=True) / inner
    rs = lax.rsqrt(mean_sq + EPSILON)
    mean_cross = jnp.sum(crossed, axis=1, keepdims=True) / inner
    pull = rs * rs * rs * mean_cross
    sums = jnp.zeros((rows, LANES), F32)
    fresh = pl.program_id(0) % per_stream == 0
    for j in range(groups):
        place = meta_ref[j]
        cols = pl.ds(pl.multiple_of(place * width, width), width)
        gated = gate[:, cols].astype(F32)
        sig = sigmoid(gated)
        v = v_all[:, cols]
        y = y_all[:, cols]
        out_low[:, cols] = (v * rs * gain[:, cols]).astype(LOW)
        d_v = rs * d_out[:, cols] - v * pull
        dm = d_v * (gated * sig)
        d_mixed[:, cols] = dm
        mixed = y + skip[:, cols] * xs[j][...]
        d_gate[:, cols] = (d_v * mixed * (sig * (1.0 + gated * (1.0 - sig)))).astype(LOW)
        sums = sums + sum_heads(
            dm.astype(LOW).astype(F32) * y, gather_of(place * per_group, width, headdim)
        )
        part = dot(ct[0], (dm * scales[:, cols]).astype(LOW))
        before = jnp.where(fresh, 0.0, held[:, cols])
        held[:, cols] = before + part
        d_state[0, :, cols] = (before + part).astype(LOW)
    row_sum[...] = sums


def gated(cfg, meta, xs, ys, states, gate, d_pieces, d_hidden, down, enter_d, c_low, ct, skip, gain):
    streams, length, slots, groups, per_group, headdim = cfg
    rows = 128
    per_stream = length // rows
    width = xs[0].shape[1]
    inner = gate.shape[1]
    state_size = c_low.shape[1]
    total = streams * length
    row = lambda cols: pl.BlockSpec((rows, cols), lambda i, m: (i, 0))
    state = pl.BlockSpec((1, state_size, width), lambda i, m: (i // per_stream, 0, 0))
    flat = pl.BlockSpec((1, inner), lambda i, m: (0, 0))
    return in_order(
        functools.partial(gate_kernel, cfg),
        grid_spec=dict(
            grid=(total // rows,),
            in_specs=[row(width)] * (2 * groups) + [state] * groups
            + [
                row(inner), pl.BlockSpec((d_pieces.shape[0], rows, d_pieces.shape[2]), lambda i, m: (0, i, 0)),
                row(d_hidden.shape[1]), pl.BlockSpec(down.shape, lambda i, m: (0, 0)), row(LANES), row(state_size),
                pl.BlockSpec((1, state_size, rows), lambda i, m: (i // per_stream, 0, i % per_stream)),
                flat, flat,
            ],
            out_specs=[
                row(inner), row(inner), row(inner), row(LANES),
                pl.BlockSpec((1, state_size, inner), lambda i, m: (i // per_stream, 0, 0)),
            ],
            scratch_shapes=[
                pltpu.VMEM((rows, inner), F32), pltpu.VMEM((rows, inner), F32), pltpu.VMEM((state_size, inner), F32),
                pltpu.VMEM((rows, inner), F32), pltpu.VMEM((rows, inner), F32),
            ],
        ),
        out_shape=[
            jax.ShapeDtypeStruct((total, inner), LOW),
            jax.ShapeDtypeStruct((total, inner), F32),
            jax.ShapeDtypeStruct((total, inner), LOW),
            jax.ShapeDtypeStruct((total, LANES), F32),
            jax.ShapeDtypeStruct((streams, state_size, inner), LOW),
        ],
        compiler_params=pltpu.CompilerParams(vmem_limit_bytes=2 * VMEM),
        cost_estimate=lasting(19),
        name="gated",
    )(meta, *placed([*xs, *ys, *states, gate, d_pieces, d_hidden, down, enter_d, c_low, ct, skip, gain], 8 << 20))


def pick(refs, which):
    value = refs[0][...]
    for j in range(1, len(refs)):
        value = jnp.where(which == j, refs[j][...], value)
    return value


def inside_back_kernel(cfg, slot, count, blocks, meta_ref, *refs):
    streams, length, slots, groups, per_group, headdim = cfg
    xs, states = refs[:count], refs[count : 2 * count]
    d_mixed, step2, logs3, enter2, log_t, gt, dxs, dgt, dc = refs[2 * count :]
    heads = groups * per_group
    per_block = BLOCK // headdim
    which = lax.div(pl.program_id(0), blocks)
    first_head = meta_ref[slot + which] * per_group + lax.rem(pl.program_id(0), blocks) * per_block
    spread = spread_of(first_head, BLOCK, headdim, heads)
    columns = spread_of(first_head, per_block * LANES, LANES, heads, 3)
    half = length // 2
    left = iota((half, LANES), 1) < headdim
    x_all, state = pick(xs, which), pick(states, which)

    @pl.when(pl.program_id(0) == 0)
    def _():
        dgt[...] = jnp.zeros_like(dgt)
        dc[...] = jnp.zeros_like(dc)

    for s in range(streams):
        start = s * length
        at = slice(start, start + length)
        log_col = expand(logs3[at], columns)
        x = (x_all[at] * expand(step2[at], spread)).astype(LOW)
        dm = d_mixed[at]
        dm_low = dm.astype(LOW)
        dc[at] += dot_nt((dm * expand(enter2[at], spread)).astype(LOW), state[s])
        sum_top, sum_low = None, None
        for pair in range(per_block // 2):
            cols = slice(pair * LANES, (pair + 1) * LANES)
            decay_top, decay_low, k_top, k_low, x_top, x_low = [], [], [], [], [], []
            for h in (2 * pair, 2 * pair + 1):
                col = log_col[:, h * LANES : (h + 1) * LANES]
                row = log_t[s, 0, h : h + 1]
                top = jnp.exp(jnp.minimum(row - wide(col[:half], length), 0.0))
                low = jnp.exp(jnp.minimum(row[:, half:] - col[half:], 0.0))
                decay_top.append(top)
                decay_low.append(low)
                k_top.append((top * gt[s, :half]).astype(LOW))
                k_low.append((low * gt[s, half:, half:]).astype(LOW))
                mine = left if h % 2 == 0 else jnp.logical_not(left)
                zero = jnp.zeros((half, LANES), LOW)
                x_top.append(jnp.where(mine, x[:half, cols], zero))
                x_low.append(jnp.where(mine, x[half:, cols], zero))
            join = lambda parts: jnp.concatenate(parts, axis=0)
            got_top, got_low = dot(join(k_top), dm_low[:, cols]), dot(join(k_low), dm_low[half:, cols])
            dxs[start : start + half, cols] = jnp.where(left, got_top[:half], got_top[half:])
            dxs[start + half : start + length, cols] = jnp.where(left, got_low[:half], got_low[half:])
            add_top = dot_nt(join(x_top), dm_low[:, cols])
            add_low = dot_nt(join(x_low), dm_low[half:, cols])
            add_top = add_top[:half] * decay_top[0] + add_top[half:] * decay_top[1]
            add_low = add_low[:half] * decay_low[0] + add_low[half:] * decay_low[1]
            sum_top = add_top if sum_top is None else sum_top + add_top
            sum_low = add_low if sum_low is None else sum_low + add_low
        dgt[s, :half] += sum_top
        dgt[s, half:, half:] += sum_low


def inside_back(cfg, meta, slot, xs, d_mixed, step2, logs3, enter2, log_t, gt, states):
    streams, length, slots, groups, per_group, headdim = cfg
    count = len(xs)
    rows, cols = xs[0].shape
    blocks = cols // BLOCK
    state_size = states[0].shape[1]
    whole = lambda i, m: (0, 0)
    cube = lambda i, m: (0, 0, 0)
    at = lambda i, m: m[slot + lax.div(i, blocks)] * blocks + lax.rem(i, blocks)
    local_at = lambda i, j: jnp.clip(i - blocks * j, 0, blocks - 1)
    return in_order(
        functools.partial(inside_back_kernel, cfg, slot, count, blocks),
        grid_spec=dict(
            grid=(count * blocks,),
            in_specs=[pl.BlockSpec((rows, BLOCK), lambda i, m, j=j: (0, local_at(i, j))) for j in range(count)]
            + [
                pl.BlockSpec((streams, state_size, BLOCK), lambda i, m, j=j: (0, 0, local_at(i, j)))
                for j in range(count)
            ]
            + [
                pl.BlockSpec((rows, BLOCK), lambda i, m: (0, at(i, m))),
                pl.BlockSpec(step2.shape, whole),
                pl.BlockSpec(logs3.shape, whole),
                pl.BlockSpec(enter2.shape, whole),
                pl.BlockSpec((streams, 1, 8, length), lambda i, m: (0, at(i, m), 0, 0)),
                pl.BlockSpec(gt.shape, cube),
            ],
            out_specs=[
                pl.BlockSpec((rows, BLOCK), lambda i, m: (0, i)),
                pl.BlockSpec(gt.shape, cube),
                pl.BlockSpec((rows, state_size), whole),
            ],
        ),
        out_shape=[
            jax.ShapeDtypeStruct((rows, count * cols), F32),
            jax.ShapeDtypeStruct(gt.shape, F32),
            jax.ShapeDtypeStruct((rows, state_size), F32),
        ],
        compiler_params=pltpu.CompilerParams(vmem_limit_bytes=VMEM),
        cost_estimate=lasting(12),
        name="inside_back",
    )(meta, *placed([*xs, *states, d_mixed, step2, logs3, enter2, log_t, gt]))


def after_kernel(cfg, blocks, parts, meta_ref, *refs):
    streams, length, slots, groups, per_group, headdim = cfg
    xs, states, cis = (refs[i * groups : (i + 1) * groups] for i in range(3))
    dxss, refs = refs[3 * groups : 3 * groups + parts], refs[3 * groups + parts :]
    d_mixed, d_after, step, step2, rest2, taps, b_low, skip, cw, cb, dci, tail, spill, direct, sums, db = refs
    per_block = BLOCK // headdim
    which = lax.div(pl.program_id(0), blocks)
    first_head = meta_ref[which] * per_group + lax.rem(pl.program_id(0), blocks) * per_block
    spread = spread_of(first_head, BLOCK, headdim, groups * per_group)
    gather = gather_of(first_head, BLOCK, headdim)
    x, state, ci = pick(xs, which), pick(states, which), pick(cis, which)
    dxs = pick(dxss, lax.div(which, groups // parts))

    @pl.when(pl.program_id(0) == 0)
    def _():
        direct[...] = jnp.zeros_like(direct)
        sums[...] = jnp.zeros_like(sums)
        db[...] = jnp.zeros_like(db)

    for s in range(streams):
        at = slice(s * length, (s + 1) * length)
        st = step[at]
        x_s = x[at]
        step_wide = expand(step2[at], spread)
        rest_wide = expand(rest2[at], spread)
        back = rest_wide * dot(b_low[at], d_after[s])
        inner_back = dxs[at]
        x_weighted = x_s * (rest_wide * step_wide)
        db[at] += dot_nt(x_weighted.astype(LOW), d_after[s])
        from_after = dot((x_s * back).astype(LOW), gather)
        direct[at] += dot((x_s * inner_back).astype(LOW), gather) + from_after
        crossed = jnp.sum(d_after[s].astype(F32) * state[s].astype(F32), axis=0, keepdims=True)
        crossed = sum_heads(jnp.broadcast_to(crossed, (8, BLOCK)), gather)
        after_sum = jnp.broadcast_to(jnp.sum(from_after * st, axis=0, keepdims=True), (8, LANES))
        sums[s] += jnp.where(iota((8, LANES), 0) == 0, crossed, after_sum)
        d_x = step_wide * (inner_back + back) + skip[...] * d_mixed[at]
        block = ci[s * (HALO + length) : (s + 1) * (HALO + length)].astype(F32)
        masks = tap_masks(taps[at], cw.shape[0])
        total = conv_back(d_x, block, masks, cw[...], cb[...])
        dci[at] = total[HALO:].astype(LOW)
        tail[s] = total[length:]
        spill[s] = total[HALO - 8 : HALO]


def after(cfg, meta, xs, states, cis, dxss, d_mixed, d_after, step, step2, rest2, taps, b_low, skip, conv_weight, conv_bias):
    streams, length, slots, groups, per_group, headdim = cfg
    rows, cols = xs[0].shape
    blocks = cols // BLOCK
    state_size = states[0].shape[1]
    total_cols = groups * cols
    parts = len(dxss)
    part_blocks = total_cols // parts // BLOCK
    whole = lambda i, m: (0, 0)
    at = lambda i, m: m[lax.div(i, blocks)] * blocks + lax.rem(i, blocks)
    spot = lambda r: pl.BlockSpec((r, BLOCK), lambda i, m: (0, at(i, m)))
    local_at = lambda i, j, n: jnp.clip(i - n * j, 0, n - 1)
    cube = lambda r: pl.BlockSpec((streams, r, BLOCK), lambda i, m: (0, 0, i))
    listed = lambda r, n, many: [pl.BlockSpec((r, BLOCK), lambda i, m, j=j: (0, local_at(i, j, n))) for j in range(many)]
    return in_order(
        functools.partial(after_kernel, cfg, blocks, parts),
        grid_spec=dict(
            grid=(groups * blocks,),
            in_specs=listed(rows, blocks, groups)
            + [
                pl.BlockSpec((streams, state_size, BLOCK), lambda i, m, j=j: (0, 0, local_at(i, j, blocks)))
                for j in range(groups)
            ]
            + listed(cis[0].shape[0], blocks, groups)
            + listed(rows, part_blocks, parts)
            + [
                spot(rows),
                pl.BlockSpec((streams, state_size, BLOCK), lambda i, m: (0, 0, at(i, m))),
                *[pl.BlockSpec(a.shape, whole) for a in (step, step2, rest2, taps, b_low)],
                spot(1), spot(conv_weight.shape[0]), spot(1),
            ],
            out_specs=[
                pl.BlockSpec((rows, BLOCK), lambda i, m: (0, i)), cube(HALO), cube(8),
                pl.BlockSpec((rows, LANES), whole),
                pl.BlockSpec((streams, 8, LANES), lambda i, m: (0, 0, 0)),
                pl.BlockSpec((rows, state_size), whole),
            ],
        ),
        out_shape=[
            jax.ShapeDtypeStruct((rows, total_cols), LOW),
            jax.ShapeDtypeStruct((streams, HALO, total_cols), F32),
            jax.ShapeDtypeStruct((streams, 8, total_cols), F32),
            jax.ShapeDtypeStruct((rows, LANES), F32),
            jax.ShapeDtypeStruct((streams, 8, LANES), F32),
            jax.ShapeDtypeStruct((rows, state_size), F32),
        ],
        compiler_params=pltpu.CompilerParams(vmem_limit_bytes=VMEM),
        cost_estimate=lasting(39),
        name="after",
    )(meta, *placed([*xs, *states, *cis, *dxss, d_mixed, d_after, step, step2, rest2, taps, b_low, skip, conv_weight, conv_bias], 1 << 18))


def finish_kernel(cfg, meta_ref, *refs):
    streams, length, slots, groups, per_group, headdim = cfg
    meta = Meta(meta_ref, groups, slots)
    parts = (len(refs) - 18) // 2
    dgts, dcs, refs = refs[:parts], refs[parts : 2 * parts], refs[2 * parts :]
    db_in, direct_in, sums, row_sum, step, slope, taps, through, rates, b_low, c_low, ci, cw, cb = refs[:14]
    width = through.shape[2]
    pick = (iota((width, LANES), 0) == iota((width, LANES), 1) * headdim).astype(F32)
    kept = [dot(through[s], pick, HIGHEST) for s in range(streams)]
    d_raw, dci, tail, spill = refs[14:]
    upper = (iota((length, length), 0) <= iota((length, length), 1)).astype(F32)
    add = lambda parts, at: functools.reduce(lambda a, b: a + b, [p[at] for p in parts])
    for s in range(streams):
        at = slice(s * length, (s + 1) * length)
        direct = direct_in[at]
        ends = sums[s]
        from_end = kept[s][0:1] * ends[0:1] + ends[1:2]
        d_log = dot(upper, row_sum[at] - step[at] * direct, HIGHEST) + from_end
        d_raw[at] = ((direct - rates[...] * d_log) * slope[at]).astype(LOW)
        seg_u = meta.segment(s, meta.first() + iota((length, length), 0))
        seg_t = meta.segment(s, meta.first() + iota((length, length), 1))
        dgt = jnp.where(seg_u == seg_t, upper, 0.0) * add(dgts, s)
        d_b = db_in[at] + dot(dgt.astype(LOW), c_low[at])
        d_c = add(dcs, at) + dot(jnp.transpose(dgt).astype(LOW), b_low[at])
        block = ci[s * (HALO + length) : (s + 1) * (HALO + length)].astype(F32)
        masks = tap_masks(taps[at], cw.shape[0])
        total = conv_back(jnp.concatenate([d_b, d_c], axis=1), block, masks, cw[...], cb[...])
        dci[at] = total[HALO:].astype(LOW)
        tail[s] = total[length:]
        spill[s] = total[HALO - 8 : HALO]


def finish(cfg, meta, dgts, dcs, db, direct, sums, row_sum, step, slope, taps, through, rates, b_low, c_low, ci, conv_weight, conv_bias, block_at):
    streams, length, slots, groups, per_group, headdim = cfg
    rows = streams * length
    args = [*dgts, *dcs, db, direct, sums, row_sum, step, slope, taps, through, rates, b_low, c_low, ci]
    zeros = lambda n: (lambda i, m: (0,) * n)
    conv_at = lambda i, m: (0, block_at)
    outs = [
        jax.ShapeDtypeStruct((rows, LANES), LOW),
        jax.ShapeDtypeStruct((rows, BLOCK), LOW),
        jax.ShapeDtypeStruct((streams, HALO, BLOCK), F32),
        jax.ShapeDtypeStruct((streams, 8, BLOCK), F32),
    ]
    return in_order(
        functools.partial(finish_kernel, cfg),
        grid_spec=dict(
            grid=(1,),
            in_specs=[pl.BlockSpec(a.shape, zeros(a.ndim)) for a in args]
            + [pl.BlockSpec((conv_weight.shape[0], BLOCK), conv_at), pl.BlockSpec((1, BLOCK), conv_at)],
            out_specs=[pl.BlockSpec(a.shape, zeros(len(a.shape))) for a in outs],
        ),
        out_shape=outs,
        compiler_params=pltpu.CompilerParams(vmem_limit_bytes=VMEM),
        cost_estimate=lasting(4),
        name="finish",
    )(meta, *placed([*args, conv_weight, conv_bias]))


def mend(d, tail, spill):
    streams = tail.shape[0]
    length = d.shape[0] // streams
    parts = []
    for s in range(streams):
        parts.append(d[s * length : (s + 1) * length - HALO])
        added = jnp.concatenate([jnp.zeros((HALO - 8, spill.shape[2]), F32), spill[s]], axis=0)
        parts.append((tail[s] + added).astype(LOW))
    return jnp.concatenate(parts, axis=0)


def turned(a, b):
    return lax.dot_general(a, b, (((0,), (0,)), ((), ())), preferred_element_type=F32)


def back_project_kernel(groups, blocks, core_place, chips, late, meta_ref, *refs):
    if late:
        d_ref, tail, spill, dn_in, dh_in = refs[:5]
        refs = refs[5:]
    else:
        d_ref, refs = refs[0], refs[1:]
    many = 2 * groups if late else 4
    weights, refs = refs[:many], refs[many:]
    hidden, up, dn, dh, g_up = refs[:5]
    held = refs[5] if late else dn
    step = pl.program_id(0)

    @pl.when(step == 0)
    def _():
        held[...] = dn_in[...] if late else jnp.zeros_like(held)
        dh[...] = dh_in[...] if late else jnp.zeros_like(dh)

    d = d_ref[...]
    if late:
        d = mend(d, tail[...], spill[...])
        for j in range(groups):

            @pl.when(lax.div(step, blocks) == j)
            def _():
                held[0] += dot_nt(d, weights[2 * j][...])
                held[1] += dot_nt(d, weights[2 * j + 1][...])
    else:
        near = step < blocks
        held[0] += dot_nt(d, jnp.where(near, weights[0][...], weights[1][0]))
        held[1] += dot_nt(d, jnp.where(near, weights[2][...], weights[3][0]))
    dh[...] += dot_nt(d, up[...])
    g_up[...] = jnp.transpose(turned(hidden[...], d))

    if late:
        core, chip = meta_ref[core_place], meta_ref[core_place + 1]
        size = dn.shape[2]

        @pl.when(step == groups * blocks - 1)
        def _():
            for k, distance in enumerate(ring_order(chips)):
                at = 2 * lax.rem(chip + distance, chips)
                cols = slice(k * size, (k + 1) * size)
                dn[at + core] = held[0, :, cols]
                dn[at + 1 - core] = held[1, :, cols]


def back_project(cfg, meta, ds, weights, hidden, in_up, first_block, late=None):
    streams, length, slots, groups, per_group, headdim = cfg
    rows = hidden.shape[0]
    half, cols = weights[0][0].shape
    blocks = cols // WIDE
    chips = lax.axis_size("fsdp") // 2
    core = core_at(groups, streams, slots)
    at = lambda i, m: m[lax.div(i, blocks)] * blocks + lax.rem(i, blocks)
    local_at = lambda i, j: jnp.clip(i - blocks * j, 0, blocks - 1)
    whole = lambda i, m: (0, 0)
    dn_spec = pl.BlockSpec((2, rows, half), lambda i, m: (0, 0, 0))
    dh_spec = pl.BlockSpec((rows, in_up.shape[0]), whole)
    out_spec = dn_spec
    if late is None:
        in_specs = [pl.BlockSpec((rows, WIDE), lambda i, m: (0, at(i, m)))]
        args = [ds]
    else:
        out_spec = pl.BlockSpec((2 * chips, rows, half // chips), lambda i, m: (0, 0, 0))
        tail, spill, dn, dh = late
        in_specs = [pl.BlockSpec((rows, WIDE), lambda i, m: (0, i))]
        in_specs += [pl.BlockSpec((streams, r, WIDE), lambda i, m: (0, 0, i)) for r in (HALO, 8)]
        in_specs += [dn_spec, dh_spec]
        args = [ds, tail, spill, dn, dh]
    if late is None:
        in_specs += quarter_specs(half, blocks) * 2
        args += [*weights[0], *weights[1]]
    else:
        for j, pair in enumerate(weights):
            for w in pair:
                in_specs.append(pl.BlockSpec((half, WIDE), lambda i, m, j=j: (0, local_at(i, j))))
                args.append(w)
    in_specs += [
        pl.BlockSpec(hidden.shape, whole),
        pl.BlockSpec((in_up.shape[0], WIDE), lambda i, m: (0, first_block + at(i, m))),
    ]
    args += [hidden, in_up]
    return in_order(
        functools.partial(back_project_kernel, groups, blocks, core, chips, late is not None),
        grid_spec=dict(
            grid=(groups * blocks,), in_specs=in_specs,
            out_specs=[out_spec, dh_spec, pl.BlockSpec((WIDE, in_up.shape[0]), lambda i, m: (at(i, m), 0))],
            scratch_shapes=[] if late is None else [pltpu.VMEM((2, rows, half), F32)],
        ),
        out_shape=[
            jax.ShapeDtypeStruct(out_spec.block_shape, F32),
            jax.ShapeDtypeStruct((rows, in_up.shape[0]), F32),
            jax.ShapeDtypeStruct((groups * cols, in_up.shape[0]), F32),
        ],
        compiler_params=pltpu.CompilerParams(vmem_limit_bytes=2 * VMEM),
        cost_estimate=lasting(15),
        name="back_project",
    )(meta, *placed(args))


def close_kernel(meta_ref, dn, dh, d_bc, tail, spill, w_small, d_raw, up, allowed, down, hidden, normed, x_in, gain, grad, out, g_bc, g_down):
    state_cols = d_bc.shape[1]
    width = x_in.shape[1]
    d = mend(d_bc[...], tail[...], spill[...])
    d_hidden = ((dh[...] + dot_nt(d, up[...])) * allowed[...]).astype(LOW)
    x = x_in[...].astype(F32)
    rs = lax.rsqrt(jnp.mean(x * x, axis=-1, keepdims=True) + EPSILON)
    d_normed = jnp.concatenate([dn[p] for p in range(dn.shape[0])], axis=1)
    d_normed = d_normed + dot_nt(d, w_small[:, :state_cols]) + dot_nt(d_raw[...], w_small[:, state_cols:])
    scaled = (d_normed + dot(d_hidden, down[...])) * gain[...]
    cross = jnp.sum(scaled * x, axis=-1, keepdims=True) / width
    out[...] = grad[...].astype(F32) + rs * (scaled - x * (rs * rs * cross))
    add_bc = jnp.transpose(turned(hidden[...], d))
    add_down = jnp.transpose(turned(d_hidden, normed[HALO:]))

    @pl.when(pl.program_id(0) == 0)
    def _():
        g_bc[...] = add_bc
        g_down[...] = add_down

    @pl.when(pl.program_id(0) > 0)
    def _():
        g_bc[...] += add_bc
        g_down[...] += add_down


def close(streams, meta, dn, dh, d_bc, tail, spill, w_small, d_raw, in_up, allowed, down, hidden, normed, x_in, gain, grad):
    rows, width = x_in.shape
    length = rows // streams
    ranks = hidden.shape[1]
    state_cols = d_bc.shape[1]
    row = lambda cols: pl.BlockSpec((length, cols), lambda i, m: (i, 0))
    stack = pl.BlockSpec((dn.shape[0], length, dn.shape[2]), lambda i, m: (0, i, 0))
    whole = lambda a: pl.BlockSpec(a.shape, lambda i, m: (0, 0))
    end = lambda r: pl.BlockSpec((1, r, state_cols), lambda i, m: (i, 0, 0))
    return in_order(
        close_kernel,
        grid_spec=dict(grid=(streams,), in_specs=[
            stack, row(ranks), row(state_cols), end(HALO), end(8), whole(w_small), row(LANES),
            pl.BlockSpec((ranks, state_cols), lambda i, m: (0, in_up.shape[1] // state_cols - 1)),
            row(ranks), whole(down), row(ranks), pl.BlockSpec((length + HALO, width), lambda i, m: (i, 0)), row(width),
            whole(gain), row(width),
        ],
        out_specs=[
            row(width),
            pl.BlockSpec((state_cols, ranks), lambda i, m: (0, 0)),
            pl.BlockSpec((width, ranks), lambda i, m: (0, 0)),
        ]),
        out_shape=[
            jax.ShapeDtypeStruct((rows, width), F32),
            jax.ShapeDtypeStruct((state_cols, ranks), F32),
            jax.ShapeDtypeStruct((width, ranks), F32),
        ],
        compiler_params=pltpu.CompilerParams(vmem_limit_bytes=2 * VMEM),
        cost_estimate=lasting(5),
        name="close",
    )(meta, *placed([dn, dh, d_bc, tail, spill, w_small, d_raw, in_up, allowed, down, hidden, normed, x_in, gain, grad], 8 << 20))


def out_back_kernel(groups, chips, meta_ref, d_branch, w_mine, w_mine_far, w_other, w_other_far, out, ordered):
    cols = w_mine.shape[1]

    @pl.when(pl.program_id(0) == 0)
    def _():
        for j in range(groups):
            ordered[:, j * cols : (j + 1) * cols] = d_branch[:, pl.ds(pl.multiple_of(meta_ref[j] * cols, cols), cols)]

    def product(near, far):
        w = jnp.concatenate([near[...]] + [far[j] for j in range(groups - 1)], axis=1)
        out[0] = dot_nt(ordered[...], w)

    @pl.when(pl.program_id(0) < chips)
    def _():
        product(w_mine, w_mine_far)

    @pl.when(pl.program_id(0) >= chips)
    def _():
        product(w_other, w_other_far)


def out_back(cfg, meta, d_branch, weights):
    streams, length, slots, groups, per_group, headdim = cfg
    rows, width = d_branch.shape
    chips = lax.axis_size("fsdp") // 2
    core = core_at(groups, streams, slots)
    half, cols = weights[0][0].shape
    size = half // chips

    def device(i, m):
        distance = jnp.int32(0)
        for at, value in enumerate(ring_order(chips)):
            distance = jnp.where(lax.rem(i, chips) == at, value, distance)
        return 2 * lax.rem(m[core + 1] + distance, chips) + jnp.where(i < chips, m[core], 1 - m[core])

    block = lambda i, side: jnp.clip(i - side * chips, 0, chips - 1)
    weight = lambda side: [
        pl.BlockSpec((size, cols), lambda i, m: (block(i, side), 0)),
        pl.BlockSpec((groups - 1, size, cols), lambda i, m: (0, block(i, side), 0)),
    ]
    return in_order(
        functools.partial(out_back_kernel, groups, chips),
        grid_spec=dict(
            grid=(2 * chips,),
            in_specs=[pl.BlockSpec((rows, width), lambda i, m: (0, 0)), *weight(0), *weight(1)],
            out_specs=pl.BlockSpec((1, rows, size), lambda i, m: (device(i, m), 0, 0)),
            scratch_shapes=[pltpu.VMEM((rows, width), LOW)],
        ),
        out_shape=jax.ShapeDtypeStruct((2 * chips, rows, size), F32),
        compiler_params=pltpu.CompilerParams(vmem_limit_bytes=VMEM),
        cost_estimate=lasting(8),
        name="out_back",
    )(meta, *placed([d_branch, *weights[0], *weights[1]]))


def out_project_kernel(cfg, chips, meta_ref, out_low, d_branch, x, allowed, down, up, d_hidden, w_mine, w_mine_far, w_other, w_other_far, y, g_down, g_up, pieces, ordered, hidden):
    streams, length, slots, groups, per_group, headdim = cfg
    meta = Meta(meta_ref, groups, slots)
    core = meta_ref[core_at(groups, streams, slots)]
    chip = meta_ref[core_at(groups, streams, slots) + 1]
    size = pieces.shape[2]

    @pl.when(pl.program_id(0) == 0)
    def _():
        for p in range(2 * chips):
            pieces[p] = out_low[:, p * size : (p + 1) * size]
        for k, distance in enumerate(ring_order(chips)):
            at = 2 * lax.rem(chip + distance, chips)
            ordered[0, :, k * size : (k + 1) * size] = pieces[at + core]
            ordered[1, :, k * size : (k + 1) * size] = pieces[at + 1 - core]
        hidden[...] = (dot_nt(out_low[...], down[...]) * allowed[...]).astype(LOW)

    near = pl.program_id(0) == 0
    w_mine = jnp.where(near, w_mine[...], w_mine_far[0])
    w_other = jnp.where(near, w_other[...], w_other_far[0])
    branch = dot(ordered[0], w_mine) + dot(ordered[1], w_other) + dot(hidden[...], up[...])
    for s in range(streams):
        at = slice(s * length, (s + 1) * length)
        seg = meta.segment(s, meta.first() + iota((length, LANES), 0))
        kept = jnp.where(wide(seg, branch.shape[1]) < slots, branch[at], 0.0)
        y[at] = (x[at].astype(F32) + kept).astype(LOW)
    cols = g_down.shape[0]
    start = pl.multiple_of(pl.program_id(0) * cols, cols)
    g_down[...] = jnp.transpose(turned(d_hidden[...], out_low[:, pl.ds(start, cols)]))
    g_up[...] = jnp.transpose(turned(hidden[...], d_branch[...]))


def out_project(cfg, meta, out_low, d_branch, x, allowed, down, up, d_hidden, weights):
    streams, length, slots, groups, per_group, headdim = cfg
    rows, width = x.shape
    inner = out_low.shape[1]
    chips = lax.axis_size("fsdp") // 2
    half, cols = weights[0][0].shape
    ranks = down.shape[0]
    whole = lambda a: pl.BlockSpec(a.shape, lambda i, m: (0, 0))
    turn = pl.BlockSpec((rows, cols), lambda i, m: (0, m[i]))
    far = pl.BlockSpec((1, half, cols), lambda i, m: (jnp.maximum(i - 1, 0), 0, 0))
    return in_order(
        functools.partial(out_project_kernel, cfg, chips),
        grid_spec=dict(
            grid=(groups,),
            in_specs=[
                whole(out_low), turn, turn, whole(allowed), whole(down),
                pl.BlockSpec((ranks, cols), lambda i, m: (0, m[i])), whole(d_hidden),
                whole(weights[0][0]), far, whole(weights[1][0]), far,
            ],
            out_specs=[
                turn,
                pl.BlockSpec((inner // groups, ranks), lambda i, m: (i, 0)),
                pl.BlockSpec((cols, ranks), lambda i, m: (m[i], 0)),
            ],
            scratch_shapes=[
                pltpu.VMEM((2 * chips, rows, half // chips), LOW), pltpu.VMEM((2, rows, half), LOW),
                pltpu.VMEM((rows, ranks), LOW),
            ],
        ),
        out_shape=[
            jax.ShapeDtypeStruct((rows, width), LOW),
            jax.ShapeDtypeStruct((inner, ranks), F32),
            jax.ShapeDtypeStruct((width, ranks), F32),
        ],
        compiler_params=pltpu.CompilerParams(vmem_limit_bytes=2 * VMEM),
        cost_estimate=lasting(10),
        name="out_project",
    )(meta, out_low, d_branch, x, allowed, down, up, d_hidden, *placed([*weights[0], *weights[1]]))


def swap_cores(value):
    return lax.ppermute(value, "fsdp", [(i, i ^ 1) for i in range(lax.axis_size("fsdp"))])


def then(value, earlier):
    return lax.optimization_barrier((value, earlier))[0]


class Scan:
    def __init__(self, own, kept_mine, kept_other, reverse):
        self.count = lax.axis_size("fsdp")
        self.core = core = lax.axis_index("fsdp") % 2
        self.reverse = reverse
        half = own.shape[2] // 2
        take = lambda a, side: lax.dynamic_slice_in_dim(a, side * half, half, 2)
        mine = take(own, core)
        self.other = other = swap_cores(take(own, 1 - core))
        self.early = early = (core == 1) if reverse else (core == 0)
        self.first = jnp.where(early, mine, other).astype(F32)
        second = jnp.where(early, other, mine).astype(F32)
        kept_mine, kept_other = take(kept_mine, core), take(kept_other, core)
        self.kept_first = jnp.where(early, kept_mine, kept_other)
        kept_second = jnp.where(early, kept_other, kept_mine)
        self.added = kept_second * self.first + second
        self.kept_both = self.kept_first * kept_second
        self.hops = self.count // 2 - 1
        self.entering = None

    def hop(self, number, earlier=None):
        send = self.added
        if self.entering is not None:
            send = self.kept_both * self.entering.astype(F32) + send
        send = send.astype(LOW)
        if earlier is not None:
            send = then(send, earlier)
        chip = self.hops - number if self.reverse else number
        route = [(2 * chip + c, 2 * (chip - 1 if self.reverse else chip + 1) + c) for c in (0, 1)]
        got = lax.ppermute(send, "fsdp", route)
        self.entering = got if self.entering is None else self.entering + got
        return got

    def end(self, earlier=None):
        entering = self.entering.astype(F32)
        entering_second = self.kept_first * entering + self.first
        keep = jnp.where(self.early, entering, entering_second).astype(LOW)
        send = jnp.where(self.early, entering_second, entering).astype(LOW)
        if earlier is not None:
            send = then(send, earlier)
        got = swap_cores(send)
        low, high = jnp.concatenate([keep, got], 2), jnp.concatenate([got, keep], 2)
        return jnp.where(self.core == 0, low, high)


def reduce_rows(parts, partial):
    count, replicas = lax.axis_size("fsdp"), lax.axis_size("dp")
    place, replica = lax.axis_index("fsdp"), lax.axis_index("dp")
    chips, chip, core = count // 2, place // 2, place % 2
    sizes = [p.shape[0] // (count * replicas) for p in parts]
    lanes = parts[0].shape[1]
    cut = [p.reshape(chips, 2, replicas, n, lanes) for p, n in zip(parts, sizes)]
    spare = -sum(sizes) % HALO
    if spare:
        cut.append(jnp.zeros((chips, 2, replicas, spare, lanes), F32))
    whole = jnp.concatenate(cut, axis=3)
    pick = lambda a, i, dim: lax.dynamic_index_in_dim(a, i, dim, False)
    total = pick(whole, core, 1) + swap_cores(pick(whole, 1 - core, 1))
    each = total.shape[2]
    partial = partial.reshape(replicas, -1, lanes)
    short = partial.shape[1]
    column = lambda r: jnp.concatenate([pick(total, r, 1).reshape(-1, lanes), pick(partial, r, 0)])
    mine = column(replica)
    for k in range(1, replicas):
        mine = mine + over_dp(column(replica ^ k).astype(LOW), k).astype(F32)
    mine, part_sum = mine[: chips * each].reshape(chips, each, lanes), mine[chips * each :]
    last = pick(mine, chip, 0)
    for k in range(1, chips):
        route = [(i, (i + 2 * k) % count) for i in range(count)]
        last = last + lax.ppermute(pick(mine, (chip + k) % chips, 0).astype(LOW), "fsdp", route).astype(F32)
    last = jnp.concatenate([last, part_sum]).astype(LOW)
    near = jnp.stack([last] + [over_dp(last, k) for k in range(1, replicas)])
    full = jnp.stack([pick(near, replica ^ a, 0) for a in range(replicas)])
    full = full.astype(F32)
    outs, start = [], 0
    for n in sizes:
        outs.append(full[:, start : start + n].reshape(replicas * n, lanes))
        start += n
    return *outs, full[:, each:].reshape(replicas * short, lanes)


def over_dp(value, bit):
    return lax.ppermute(value, "dp", [(i, i ^ bit) for i in range(lax.axis_size("dp"))])


def after_token(value, token):
    return value + token.astype(value.dtype)


class Share:
    def __init__(self, near, mine, other):
        self.near, self.mine, self.other = near, mine, other
        self.one, self.two = over_dp(mine[1:], 1), over_dp(mine[1:], 2)
        part = mine.shape[1] // 2
        self.halves = self.one[:, :part], self.two[:, part:]
        self.last = over_dp(self.halves[0], 2), over_dp(self.halves[1], 1)

    def join(self, j, token=None):
        far, near = (None, self.one, self.two, None)[j], self.near[j]
        if far is None:
            far = jnp.concatenate(self.last, axis=1)
        if token is not None:
            near, far = after_token(near, token), after_token(far, token)
        return flat(jnp.concatenate([near[None], far]))

    def end(self):
        got = jnp.stack([self.join(j) for j in range(1, len(self.near))])
        return (flat(self.mine), got), (flat(self.other), swap_cores(got))


def in_ring(every, token=0):
    count, place = every.shape[0], lax.axis_index("fsdp") + token
    take = lambda k, flip: lax.dynamic_index_in_dim(every, (place + 2 * k) % count ^ flip, 0, False)
    return [jnp.stack([take(k, flip) for k in ring_order(count // 2)]) for flip in (0, 1)]


def flat(chips):
    return chips.reshape(-1, chips.shape[2])


def local(
    block_input, seq_lengths, adapter_ids, norm_gain, w_in, w_dt, conv_weight, conv_bias, dt_bias,
    head_rates, skip_gain, gate_gain, w_out, in_down, in_up, out_down, out_up, out_grad,
):
    streams, length, width = block_input.shape[1:]
    inner = gate_gain.shape[0]
    conv_cols = conv_weight.shape[1]
    heads = dt_bias.shape[0]
    headdim = inner // heads
    state_size = (conv_cols - inner) // 2
    adapters, ranks = in_down.shape[:2]
    in_cols = in_up.shape[2]
    slots = seq_lengths.shape[2]
    rows = streams * length
    groups = lax.axis_size("dp")
    per_group = heads // groups
    group_cols = inner // groups
    cfg = (streams, length, slots, groups, per_group, headdim)
    count = lax.axis_size("fsdp")
    first_pos = lax.axis_index("fsdp") * length
    ends = jnp.cumsum(seq_lengths[0], axis=-1, dtype=jnp.int32)
    place = lax.axis_index("fsdp")
    core, chip, chips = place % 2, place // 2, count // 2
    order = lax.axis_index("dp") ^ jnp.arange(groups, dtype=jnp.int32)
    meta = [order, first_pos[None], ends.reshape(-1), core[None], chip[None], adapter_ids.reshape(-1)]
    meta = jnp.concatenate(meta).astype(jnp.int32)
    ids_place = core_at(groups, streams, slots) + 2
    pad_heads = lambda a: jnp.pad(a, ((0, 0), (0, LANES - heads)))

    small = jnp.concatenate([w_in[:, 2 * inner :], pad_heads(w_dt)], axis=1)
    first = jnp.concatenate(
        [lax.dynamic_slice_in_dim(w_in, inner + lax.axis_index("dp") * group_cols, group_cols, 1), small], axis=1
    )
    every = lax.all_gather(first, "fsdp")
    w_later = then(w_in, first)
    quarters = lambda a: [
        lax.dynamic_slice_in_dim(a, order[j] * group_cols, group_cols, 1) for j in range(groups)
    ]
    own_x, own_gate = quarters(w_later[:, inner : 2 * inner]), quarters(w_later[:, :inner])
    w_small = every[:, :, group_cols:].reshape(width, -1)
    every_gate = lax.all_gather(own_gate[0], "fsdp")
    out_cols = width // groups
    own_out = [lax.dynamic_slice_in_dim(w_out, order[j] * out_cols, out_cols, 1) for j in range(groups)]
    every_out = lax.all_gather(own_out[0], "fsdp")
    Order.waits = [own_gate[0], own_out[0]]
    devices = range(count)
    before = lax.ppermute(block_input[0, :, length - HALO :], "fsdp", [(i - 1, i) for i in devices if i > 0])
    down_in = in_down.reshape(adapters * ranks, width)
    up_in = in_up.reshape(adapters * ranks, in_cols)
    down_out = out_down.reshape(adapters * ranks, inner)
    up_out = out_up.reshape(adapters * ranks, width)
    x_rows, grad_rows = block_input.reshape(rows, width), out_grad.reshape(rows, width)
    normed_ext, nx_ext, hidden_ext, hidden_in, allowed, d_branch, d_hidden_out = prepare(
        cfg, meta, ids_place, ranks, x_rows, before.reshape(streams * HALO, width), norm_gain[None],
        down_in, grad_rows, up_out,
    )

    rates = pad_heads(head_rates[None])
    bias_row = conv_bias[None]
    (ci_bc, step, slope, taps, logs3, step2, enter2, rest2, weight2, log_t, through, g, gt, b_low, c_low, bt, ct) = decays(
        cfg, meta, normed_ext, hidden_ext, w_small, up_in, conv_weight, bias_row, pad_heads(dt_bias[None]), rates, heads
    )
    kept_mine = through[:, :1]
    kept_other = swap_cores(kept_mine)
    of_group = lambda a, j: lax.dynamic_slice_in_dim(a, order[j] * group_cols, group_cols, 2)

    w_x, ci, xs, ys, added = [], [], [], [], []

    def enter_group(j, weights):
        w_x.append(weights)
        ci_j, x_j, own = project(cfg, meta, j, nx_ext, hidden_ext, weights, up_in, conv_weight, bias_row, weight2, taps, bt)
        ci.append(ci_j)
        xs.append(x_j)
        added.append(own)

    def scan_of(js):
        kept = [jnp.concatenate([of_group(a, j) for j in js], axis=2) for a in (kept_mine, kept_other)]
        return Scan(jnp.concatenate([added[j] for j in js], axis=2), *kept, False)

    pairs = lambda j: inside(cfg, meta, j, xs[j], step2, logs3, log_t, g)
    x_share = Share(own_x, *in_ring(every[:, :, :group_cols]))
    enter_group(0, (flat(x_share.mine), flat(x_share.other)))
    ys.append(pairs(0))
    near = [x_share.join(j) for j in (1, 2)]
    near = [(w, swap_cores(w)) for w in near]
    wait_for(*x_share.halves)
    enter_group(1, near[0])
    gate_share = Share(own_gate, *in_ring(every_gate, Order.token))
    enter_group(2, near[1])
    scans = [scan_of((0, 1))]
    got = scans[0].hop(0)
    last = x_share.join(3, Order.token)
    wait_for(last, scans[0].other)
    enter_group(3, (last, swap_cores(last)))
    out_share = Share(own_out, *in_ring(every_out, Order.token))
    scans.append(scan_of((2, 3)))
    wait_for(got, scans[1].other)
    ys.append(pairs(1))
    got = [scans[0].hop(1), scans[1].hop(0)]
    wait_for(*gate_share.halves, *got)
    ys.append(pairs(2))
    got = [scans[0].hop(2), scans[1].hop(1)]
    w_gate = gate_share.end()
    wait_for(*got)
    ys.append(pairs(3))
    got = [scans[1].hop(2)]
    for hop in range(3, chips - 1):
        got = [scans[0].hop(hop), scans[1].hop(hop)]
    wait_for(*out_share.halves)
    gate = gate_project(cfg, meta, nx_ext, hidden_ext, w_gate, up_in)
    w_o = out_share.end()
    wait_for(*got)
    pair_states = [scan.end() for scan in scans]
    states = [pair_states[j // 2][:, :, (j % 2) * group_cols : (j % 2 + 1) * group_cols] for j in range(groups)]
    d_pieces = out_back(cfg, meta, d_branch, w_o)

    skip_row = jnp.repeat(skip_gain, headdim)[None]
    out_low, d_mixed, d_gate, row_sum, d_state = gated(
        cfg, meta, xs, ys, states, gate, d_pieces, d_hidden_out, down_out, enter2, c_low, ct, skip_row, gate_gain[None]
    )
    pieces = 2
    wide_cols = inner // pieces
    part = lambda a, j: a[:, :, j * wide_cols : (j + 1) * wide_cols]
    scans = [Scan(part(d_state, j), part(kept_mine, j), part(kept_other, j), True) for j in range(pieces)]
    arrived = [[scan.hop(0) for scan in scans]]

    wait_for(*[scan.other for scan in scans])

    block_output, g_out_down, g_out_up = out_project(
        cfg, meta, out_low, d_branch, x_rows, allowed, down_out, up_out, d_hidden_out, w_o
    )
    wait_for(*arrived[0])
    early = back_project(cfg, meta, d_gate, w_gate, hidden_in, up_in, 0)
    for hop in range(1, chips - 1):
        arrived.append([scan.hop(hop) for scan in scans])
    half_groups = groups // 2
    inside_parts = []
    for p in (0, 1):
        wait_for(*arrived[p + 1])
        js = slice(p * half_groups, (p + 1) * half_groups)
        inside_parts.append(
            inside_back(cfg, meta, p * half_groups, xs[js], d_mixed, step2, logs3, enter2, log_t, gt, states[js])
        )
    dxs, dgts, dcs = zip(*inside_parts)
    d_after = jnp.concatenate([scan.end() for scan in scans], axis=2)
    by_device = lambda a: a.reshape(count, a.shape[0] // count, a.shape[1])
    out_sums = jnp.concatenate([by_device(g_out_down), by_device(g_out_up)], axis=1)
    out_sums = lax.psum_scatter(then(out_sums, dxs[1]), "fsdp", scatter_dimension=0, tiled=False)
    dci, tail, spill, direct, sums, db = after(
        cfg, meta, xs, states, ci, dxs, d_mixed, d_after, step, step2, rest2, taps, b_low, skip_row, conv_weight, bias_row
    )
    to_earlier = lambda a: lax.ppermute(a, "fsdp", [(i, i - 1) for i in devices if i > 0])
    spill = to_earlier(spill)
    d_raw, dci_bc, tail_bc, spill_bc = finish(
        cfg, meta, dgts, dcs, db, direct, sums, row_sum, step, slope, taps, through, rates, b_low, c_low,
        ci_bc, conv_weight, bias_row, inner // BLOCK,
    )
    spill_bc = to_earlier(spill_bc)
    late = back_project(
        cfg, meta, dci, w_x, hidden_in, up_in, inner // WIDE, (tail, spill, early[0], early[1])
    )
    input_grad, g_bc, g_in_down = close(
        streams, meta, late[0], late[1], dci_bc, tail_bc, spill_bc, w_small, d_raw, up_in, allowed, down_in, hidden_in,
        normed_ext, x_rows, norm_gain[None], grad_rows,
    )
    in_down_sum, in_up_sum, out_sums = reduce_rows(
        [g_in_down, jnp.concatenate([early[2], late[2], g_bc], axis=0)], out_sums
    )
    out_sums = jnp.split(out_sums, [inner // count], axis=0)
    totals = [a.T.reshape(adapters, ranks, -1) for a in (in_down_sum, in_up_sum, *out_sums)]
    return (block_output.reshape(1, streams, length, width), input_grad.reshape(1, streams, length, width), *totals)


def solution(mesh):
    rows = P("dp", None, "fsdp", None)
    cut = P("fsdp", None)
    per_group = P("dp", None, None)
    in_specs = (
        rows, per_group, per_group, P(), cut, cut, P(), P(), P(), P(), P(), P(), cut, P(), P(), P(), P(), rows,
    )
    out_specs = (rows, rows) + (P(None, None, "fsdp"),) * 4
    return jax.shard_map(local, mesh=mesh, in_specs=in_specs, out_specs=out_specs, check_vma=False)
```
